32 devices in a mesh: seq: 8 (over y, x, core), head: 4 (over z).
Axes of the slice: x: 2, y: 2, z: 4, core: 2. Of those that a mesh axis runs over, the one named last changes fastest.
Arguments:
- tokens: bfloat16 [8192, 2048], P('seq', 'head'), may hold values from -6 to 6
- prenorm: bfloat16 [2048], P('head'), may hold values from 0.5 to 1.5
- gating: bfloat16 [2048, 4096], P(None, 'head'), may hold values from -0.125 to 0.125
- values: bfloat16 [2048, 4096], P(None, 'head'), may hold values from -0.125 to 0.125
- control: bfloat16 [2048, 256], replicated, may hold values from -0.125 to 0.125
- timestep: bfloat16 [2048, 64], P(None, 'head'), may hold values from -0.125 to 0.125
- kernel: float32 [4, 4096], P(None, 'head'), may hold values from -3 to 3
- offset: float32 [4096], P('head'), may hold values from -1.8 to 1.8
- filters: float32 [4, 256], replicated, may hold values from -3 to 3
- baseline: float32 [256], replicated, may hold values from -1.8 to 1.8
- timing: float32 [64], P('head'), may hold values from -5 to -4
- damping: float32 [64], P('head')
- direct: float32 [64], P('head'), may hold values from 0.5 to 1.5
- postnorm: float32 [4096], P('head'), may hold values from 0.5 to 1.5
- readout: bfloat16 [2048, 4096], P(None, 'head'), may hold values from -0.09375 to 0.09375
- doc_starts: int32 [8192], P('seq'), may hold values from 0 to 1, as said below
- cotangent: bfloat16 [8192, 2048], P('seq', 'head'), may hold values from -6 to 6
Outputs:
- mixed: bfloat16 [8192, 2048], P('seq', 'head')
- tokens_gradient: float32 [8192, 2048], P('seq', 'head')
- prenorm_gradient: float32 [2048], replicated
- gating_gradient: float32 [2048, 4096], P('seq', 'head')
- values_gradient: float32 [2048, 4096], P('seq', 'head')
- control_gradient: float32 [2048, 256], replicated
- timestep_gradient: float32 [2048, 64], P('seq', 'head')
- kernel_gradient: float32 [4, 4096], replicated
- offset_gradient: float32 [4096], replicated
- filters_gradient: float32 [4, 256], replicated
- baseline_gradient: float32 [256], replicated
- timing_gradient: float32 [64], replicated
- damping_gradient: float32 [64], replicated
- direct_gradient: float32 [64], replicated
- postnorm_gradient: float32 [4096], replicated
- readout_gradient: float32 [2048, 4096], P('seq', 'head')
The draws below stay inside these ranges and needn't reach their ends.
Inputs may be any that keep to these rules, and one draw needn't show every extreme that they name: `doc_starts`: token 0 starts a document.
All inputs are finite; a program needn't handle non-finite values.
Results may differ from the reference program's by a relative error of at most 0.012.
Values may be sent and summed in bfloat16 or wider, within the bound.
No kernel may reach another device: no remote copies, remote signals or barrier semaphores. Data moves between devices by JAX's collectives and lax.ppermute only.
A program may use at most 256 MiB of HBM per device.

```python
import math
from functools import partial
import jax
import jax.numpy as jnp
from jax import lax

D = 2048
HEADS = 64
HDIM = 64
STATE = 128
CONV = 4
SPAN = 256
TOK_DEV = 1024
INNER = 4096
TOKENS = 8192
N_HEAD = 4


def draw_doc_starts(key, part):
    keys = jax.random.split(key, 4)
    opening = jax.random.randint(keys[0], (), 1, TOK_DEV)
    closing = TOKENS - jax.random.randint(keys[1], (), 1, TOK_DEV)
    places = jnp.arange(TOKENS)
    regions = TOKENS // 16 + 1
    spacing = jax.random.randint(keys[2], (regions,), 3, 97)[places // 16]
    coins = jax.random.randint(keys[3], (TOKENS,), 0, 1 << 20)
    outside = (places < opening) | (places >= closing)
    marked = outside & (coins % spacing == 0)
    marked = marked | (places == 0) | (places == opening) | (places == closing)
    return marked.astype(jnp.int32)


def draw_damping(key, part):
    lowest = math.log(0.5 / (TOKENS * 0.011))
    highest_value = math.log(2.3)
    uniform = jax.random.uniform(key, (HEADS,), jnp.float32)
    return (lowest + (highest_value - lowest) * uniform).astype(jnp.float32)


def block_scale(rng, extent, cuts, low, top_value):
    loudness, own = 1.0, jax.random.fold_in(rng, 6)
    for dim, parts in cuts:
        draws = jnp.exp(jax.random.uniform(jax.random.fold_in(own, dim), (parts,), jnp.float32, low / len(cuts), top_value / len(cuts)))
        loudness = loudness * jnp.repeat(draws, extent[dim] // parts).reshape([-1 if axis == dim else 1 for axis in range(len(extent))])
    return loudness


def noise(own_key, extent, scale, bound, shards=(), kind=jnp.bfloat16):
    drawn = scale * jax.random.normal(own_key, extent, jnp.float32)
    if shards:
        drawn = drawn * block_scale(own_key, extent, shards, -0.22, 0.18)
    return jnp.clip(drawn, -bound, bound).astype(kind)


def setup_inputs(seed: int = 0) -> dict:
    seeds = jax.random.split(jax.random.key(seed), 18)
    tokens = noise(seeds[0], (TOKENS, D), 1.0, 6.0, ((0, 8), (1, 4)))
    prenorm = jnp.clip(1.0 + 0.1 * jax.random.normal(seeds[1], (D,), jnp.float32), 0.5, 1.5).astype(jnp.bfloat16)
    gating = noise(seeds[2], (D, INNER), D ** -0.5, 0.125, ((1, 4),))
    values = noise(seeds[3], (D, INNER), D ** -0.5, 0.125, ((1, 4),))
    control = noise(seeds[4], (D, 2 * STATE), D ** -0.5, 0.125)
    timestep = noise(seeds[5], (D, HEADS), D ** -0.5, 0.125, ((1, 4),))
    kernel = noise(seeds[6], (CONV, INNER), CONV ** -0.5, 3.0, ((1, 4),), jnp.float32)
    offset = noise(seeds[7], (INNER,), 0.3, 1.8, ((0, 4),), jnp.float32)
    filters = noise(seeds[8], (CONV, 2 * STATE), CONV ** -0.5, 3.0, (), jnp.float32)
    baseline = noise(seeds[9], (2 * STATE,), 0.3, 1.8, (), jnp.float32)
    timing = jnp.clip(-5.0 + 1.0 * jax.random.uniform(seeds[10], (HEADS,), jnp.float32) ** block_scale(seeds[10], (HEADS,), ((0, 4),), -0.2, 0.2), -5.0, -4.0)
    damping = draw_damping(jax.random.fold_in(seeds[17], 71), 0)
    direct = jnp.clip(0.5 + 1.0 * jax.random.uniform(seeds[12], (HEADS,), jnp.float32) ** block_scale(seeds[12], (HEADS,), ((0, 4),), -0.2, 0.2), 0.5, 1.5)
    postnorm = jnp.clip(1.0 + 0.1 * jax.random.normal(seeds[13], (INNER,), jnp.float32), 0.5, 1.5)
    readout = noise(seeds[14], (D, INNER), INNER ** -0.5, 0.09375, ((1, 4),))
    doc_starts = draw_doc_starts(jax.random.fold_in(seeds[17], 71), 0)
    cotangent = noise(seeds[16], (TOKENS, D), 1.0, 6.0, ((0, 8), (1, 4)))
    return dict(tokens=tokens, prenorm=prenorm, gating=gating, values=values, control=control, timestep=timestep, kernel=kernel, offset=offset, filters=filters, baseline=baseline, timing=timing, damping=damping, direct=direct, postnorm=postnorm, readout=readout, doc_starts=doc_starts, cotangent=cotangent)


epsilon = 1e-05
highest = lax.Precision.HIGHEST

@jax.custom_vjp
def low(v):
    return lax.optimization_barrier(v.astype(jnp.bfloat16)).astype(jnp.float32)

@jax.custom_vjp
def low_back(v):
    return v

def low_keep(v):
    return (low(v), None)

def low_pass(kept, grad):
    return (grad,)

def back_keep(v):
    return (v, None)

def back_low(kept, grad):
    return (low(grad),)
low.defvjp(low_keep, low_pass)
low_back.defvjp(back_keep, back_low)

def causal_conv(extended, weights, biases, length):
    summed = biases
    for offset_index in range(weights.shape[0]):
        summed = summed + weights[offset_index] * lax.slice_in_dim(extended, offset_index, offset_index + length, axis=extended.ndim - 2)
    return summed

def spanned_scan(signal, writers, readers, step_size, log_decay, starts, incoming):
    length, head_count = step_size.shape
    blocks = length // SPAN
    signal_blocks = signal.reshape(blocks, SPAN, head_count, HDIM)
    write_blocks = writers.reshape(blocks, SPAN, -1)
    read_blocks = readers.reshape(blocks, SPAN, -1)
    step_blocks = jnp.swapaxes(step_size.reshape(blocks, SPAN, head_count), 1, 2)
    cumulative = jnp.cumsum(jnp.swapaxes(log_decay.reshape(blocks, SPAN, head_count), 1, 2), axis=2)
    segment = jnp.cumsum(starts.reshape(blocks, SPAN), axis=1)
    places = jnp.arange(SPAN)
    linked = (segment[:, :, None] == segment[:, None, :]) & (places[:, None] >= places[None, :])
    spread = cumulative[:, :, :, None] - cumulative[:, :, None, :]
    decays = jnp.exp(jnp.where(linked[:, None], spread, -1e+30))
    scores = jnp.einsum('ktn,ksn->kts', read_blocks, write_blocks, precision=highest)
    mixing = decays * scores[:, None] * step_blocks[:, :, None, :]
    within = jnp.einsum('khts,kshp->kthp', mixing, signal_blocks, precision=highest)
    ending = segment == segment[:, -1:]
    toward = jnp.exp(jnp.where(ending[:, None, :], cumulative[:, :, -1:] - cumulative, -1e+30)) * step_blocks
    produced = jnp.einsum('khs,kshp,ksn->khpn', toward, signal_blocks, write_blocks, precision=highest)
    passing = jnp.exp(cumulative[:, :, -1]) * (segment[:, -1] == 0)[:, None]
    entering = jnp.exp(cumulative) * (segment == 0)[:, None, :]
    current = incoming
    entries = []
    for position in range(blocks):
        entries.append(current)
        current = passing[position][:, None, None] * current + produced[position]
    carried = jnp.einsum('khq,kqn,khpn->kqhp', entering, read_blocks, jnp.stack(entries), precision=highest)
    return ((within + carried).reshape(length, head_count * HDIM), current)

def layer(doc_starts, tokens, prenorm, gating, values, control, timestep, kernel, offset, filters, baseline, timing, damping, direct, postnorm, readout):
    groups = N_HEAD
    per_group = HEADS // groups
    width = CONV - 1
    blocks = TOKENS // TOK_DEV

    def advance(carry, inputs):
        state, edge_values, edge_shared = carry
        residual, marks = inputs
        length = residual.shape[0]
        scale = lax.rsqrt(lax.optimization_barrier(jnp.mean(residual * residual, axis=1, keepdims=True)) + epsilon)
        normed = low(residual * scale * prenorm)
        gate_in = low_back(jnp.dot(normed, gating, precision=highest))
        projected = low_back(jnp.dot(normed, values, precision=highest))
        shared = jnp.dot(normed, control, precision=highest)
        copies = low_back(jnp.broadcast_to(shared, (groups,) + shared.shape))
        timestep_in = low_back(jnp.dot(normed, timestep, precision=highest))
        signal = jax.nn.silu(causal_conv(jnp.concatenate([edge_values, projected], axis=0), kernel, offset, length))
        control_out = jax.nn.silu(causal_conv(jnp.concatenate([edge_shared, copies], axis=1), filters, baseline, length))
        step_size = jax.nn.softplus(timestep_in + timing)
        log_decay = -step_size * jnp.exp(damping)
        signal_groups = jnp.swapaxes(signal.reshape(length, groups, per_group * HDIM), 0, 1)
        step_groups = jnp.swapaxes(step_size.reshape(length, groups, per_group), 0, 1)
        decay_groups = jnp.swapaxes(log_decay.reshape(length, groups, per_group), 0, 1)
        state_groups = state.reshape(groups, per_group, HDIM, STATE)
        scanned, ending = jax.vmap(spanned_scan, in_axes=(0, 0, 0, 0, 0, None, 0))(signal_groups, control_out[:, :, :STATE], control_out[:, :, STATE:], step_groups, decay_groups, marks, state_groups)
        scanned = jnp.swapaxes(scanned, 0, 1).reshape(length, HEADS * HDIM)
        full = scanned + jnp.repeat(direct, HDIM) * signal
        gated = full * jax.nn.silu(gate_in)
        inverse = lax.rsqrt(lax.optimization_barrier(jnp.mean(gated * gated, axis=1, keepdims=True)) + epsilon)
        normalized = low(gated * inverse * postnorm)
        branch = jnp.dot(normalized, readout.T, precision=highest)
        following = (ending.reshape(HEADS, HDIM, STATE), projected[length - width:], copies[:, length - width:])
        return (following, residual + branch)
    initial = (jnp.zeros((HEADS, HDIM, STATE), jnp.float32), jnp.zeros((width, HEADS * HDIM), jnp.float32), jnp.zeros((groups, width, 2 * STATE), jnp.float32))
    inputs = (tokens.reshape(blocks, TOK_DEV, D), doc_starts.reshape(blocks, TOK_DEV))
    ignored, outputs = lax.scan(jax.checkpoint(advance), initial, inputs)
    return outputs.reshape(TOKENS, D)

def reference(tokens, prenorm, gating, values, control, timestep, kernel, offset, filters, baseline, timing, damping, direct, postnorm, readout, doc_starts, cotangent):
    params = tuple((item.astype(jnp.float32) for item in (tokens, prenorm, gating, values, control, timestep, kernel, offset, filters, baseline, timing, damping, direct, postnorm, readout)))
    mixed, backward = jax.vjp(partial(layer, doc_starts.astype(jnp.int32)), *params)
    grads = backward(cotangent.astype(jnp.float32))
    return (mixed.astype(jnp.bfloat16), grads[0], grads[1], grads[2], grads[3], grads[4], grads[5], grads[6], grads[7], grads[8], grads[9], grads[10], grads[11], grads[12], grads[13], grads[14])
```

```python
import jax
import jax.numpy as jnp
from jax import lax
from jax.sharding import PartitionSpec as P

D = 2048
HEADS = 64
HDIM = 64
STATE = 128
SPAN = 256
INNER = 4096


epsilon = 1e-05


def shifted(value, axis, steps):
    count = lax.axis_size(axis)
    leading, last = (max(0, -steps), min(count, count - steps))
    return lax.ppermute(value, axis, [(source, source + steps) for source in range(leading, last)])


def rotation(count, steps):
    return [(source, (source + steps) % count) for source in range(count)]


def flips(count, bit):
    return [(source, source ^ (1 << bit)) for source in range(count)]


def bits_of(count):
    return count.bit_length() - 1


def gather_blocks(block, axis):
    count = lax.axis_size(axis)
    half = count // 2
    rows = block.shape[0] // 2
    found = [None] * count
    found[0] = block
    left = right = block
    for step in range(1, half):
        left = lax.ppermute(left, axis, rotation(count, 1))
        right = lax.ppermute(right, axis, rotation(count, -1))
        found[count - step] = left
        found[step] = right
    far_low = lax.ppermute(left[:rows], axis, rotation(count, 1))
    far_high = lax.ppermute(right[rows:], axis, rotation(count, -1))
    found[half] = jnp.concatenate([far_low, far_high], axis=0)
    return found


def gather_columns(block, axis):
    count = lax.axis_size(axis)
    me = lax.axis_index(axis)
    width = block.shape[1]
    whole = jnp.zeros((block.shape[0], count * width), block.dtype)
    for step, piece in enumerate(gather_blocks(block, axis)):
        whole = lax.dynamic_update_slice_in_dim(whole, piece, (me + step) % count * width, 1)
    return whole


def scatter_columns(whole, axis):
    count = lax.axis_size(axis)
    me = lax.axis_index(axis)
    half = count // 2
    width = whole.shape[1] // count
    rows = whole.shape[0] // 2

    def part(step):
        return lax.dynamic_slice_in_dim(whole, (me + step) % count * width, width, 1)

    far = part(half)
    ahead = lax.ppermute(far[:rows].astype(jnp.bfloat16), axis, rotation(count, 1))
    behind = lax.ppermute(far[rows:].astype(jnp.bfloat16), axis, rotation(count, -1))
    first = True
    for step in range(half - 1, 0, -1):
        up = part(step).astype(jnp.float32)
        down = part(count - step).astype(jnp.float32)
        if first:
            up = up.at[:rows].add(ahead.astype(jnp.float32))
            down = down.at[rows:].add(behind.astype(jnp.float32))
            first = False
        else:
            up = up + ahead.astype(jnp.float32)
            down = down + behind.astype(jnp.float32)
        ahead = lax.ppermute(up.astype(jnp.bfloat16), axis, rotation(count, 1))
        behind = lax.ppermute(down.astype(jnp.bfloat16), axis, rotation(count, -1))
    return part(0).astype(jnp.float32) + ahead.astype(jnp.float32) + behind.astype(jnp.float32)


def small_sum(value, axis):
    count = lax.axis_size(axis)
    total = value
    for step in range(1, count):
        total = total + lax.ppermute(value, axis, rotation(count, step))
    return total


def doubled_sum(value, axis):
    count = lax.axis_size(axis)
    for bit in range(bits_of(count)):
        value = value + lax.ppermute(value, axis, flips(count, bit))
    return value


def halve(value, axis, bit, position):
    count = lax.axis_size(axis)
    mine = (lax.axis_index(axis) >> bit) & 1
    kept = lax.dynamic_index_in_dim(value, mine, position, False)
    sent = lax.dynamic_index_in_dim(value, 1 - mine, position, False)
    return kept + lax.ppermute(sent, axis, flips(count, bit))


def scatter_rows(value, axis):
    count = lax.axis_size(axis)
    bits = bits_of(count)
    rows, columns = value.shape
    split = value.reshape((2,) * bits + (rows // count, columns))
    split = halve(split, axis, 0, bits - 1)
    parts = []
    for piece in range(2):
        half = split[..., piece * (columns // 2) : (piece + 1) * (columns // 2)]
        left = list(range(bits - 1, 0, -1))
        order = list(range(1, bits)) if piece == 0 else list(range(bits - 1, 0, -1))
        for bit in order:
            half = halve(half, axis, bit, left.index(bit))
            left.remove(bit)
        parts.append(half)
    return jnp.concatenate(parts, axis=1).astype(jnp.float32)


def prefix_state(passing, state, axis, reverse):
    count = lax.axis_size(axis)
    me = lax.axis_index(axis)
    total_pass, total_state = passing, state
    prefix = jnp.zeros_like(state)
    prefix_pass = jnp.ones_like(passing)
    for bit in range(bits_of(count)):
        other_pass = lax.ppermute(total_pass, axis, flips(count, bit))
        other_state = lax.ppermute(total_state, axis, flips(count, bit))
        upper = ((me >> bit) & 1) == 1
        other_first = jnp.logical_not(upper) if reverse else upper
        prefix = jnp.where(other_first, prefix_pass[:, None, None] * other_state + prefix, prefix)
        prefix_pass = jnp.where(other_first, prefix_pass * other_pass, prefix_pass)
        total_state = jnp.where(
            other_first,
            total_pass[:, None, None] * other_state + total_state,
            other_pass[:, None, None] * total_state + other_state,
        )
        total_pass = total_pass * other_pass
    return prefix


def gather_small(value, axis):
    count = lax.axis_size(axis)
    me = lax.axis_index(axis)
    whole = jnp.zeros((count,) + value.shape, value.dtype)
    for step in range(count):
        piece = value if step == 0 else lax.ppermute(value, axis, rotation(count, -step))
        whole = lax.dynamic_update_index_in_dim(whole, piece, (me + step) % count, 0)
    return whole


def sum_everywhere(value):
    count, heads = lax.axis_size("seq"), lax.axis_size("head")
    bits = bits_of(count)
    rows, columns = value.shape
    split = value.reshape((2,) * bits + (rows // count, columns))
    for bit in range(bits):
        split = halve(split, "seq", bit, bits - 1 - bit)
    blocks = split.reshape(heads, rows // count // heads, columns)
    me = lax.axis_index("head")
    total = lax.dynamic_index_in_dim(blocks, me, 0, False)
    for step in range(1, heads):
        sent = lax.dynamic_index_in_dim(blocks, (me + step) % heads, 0, False)
        total = total + lax.ppermute(sent, "head", rotation(heads, step))
    whole = gather_small(total.astype(jnp.bfloat16), "head").reshape(rows // count, columns)
    place = lax.axis_index("seq")
    for bit in range(bits - 1, -1, -1):
        other = lax.ppermute(whole, "seq", flips(count, bit))
        upper = ((place >> bit) & 1) == 1
        low = jnp.where(upper, other, whole)
        high = jnp.where(upper, whole, other)
        whole = jnp.stack([low, high])
    order = list(range(bits - 1, -1, -1)) + [bits, bits + 1]
    return whole.transpose(order).reshape(rows, columns).astype(jnp.float32)


def causal_conv(extended, weights, biases, length):
    summed = biases
    for offset_index in range(weights.shape[0]):
        summed = summed + weights[offset_index] * lax.slice_in_dim(
            extended, offset_index, offset_index + length, axis=extended.ndim - 2
        )
    return summed


def spanned_scan(signal, writers, readers, step_size, log_decay, starts, incoming):
    length, head_count = step_size.shape
    blocks = length // SPAN
    signal_blocks = signal.reshape(blocks, SPAN, head_count, HDIM)
    write_blocks = writers.reshape(blocks, SPAN, -1)
    read_blocks = readers.reshape(blocks, SPAN, -1)
    step_blocks = jnp.swapaxes(step_size.reshape(blocks, SPAN, head_count), 1, 2)
    cumulative = jnp.cumsum(jnp.swapaxes(log_decay.reshape(blocks, SPAN, head_count), 1, 2), axis=2)
    segment = jnp.cumsum(starts.reshape(blocks, SPAN), axis=1)
    places = jnp.arange(SPAN)
    linked = (segment[:, :, None] == segment[:, None, :]) & (places[:, None] >= places[None, :])
    spread = cumulative[:, :, :, None] - cumulative[:, :, None, :]
    decays = jnp.exp(jnp.where(linked[:, None], spread, -1e30))
    scores = jnp.einsum("ktn,ksn->kts", read_blocks, write_blocks, precision=lax.Precision.DEFAULT)
    mixing = decays * scores[:, None] * step_blocks[:, :, None, :]
    within = jnp.einsum("khts,kshp->kthp", mixing, signal_blocks, precision=lax.Precision.DEFAULT)
    ending = segment == segment[:, -1:]
    toward = (
        jnp.exp(jnp.where(ending[:, None, :], cumulative[:, :, -1:] - cumulative, -1e30))
        * step_blocks
    )
    produced = jnp.einsum(
        "khs,kshp,ksn->khpn", toward, signal_blocks, write_blocks, precision=lax.Precision.DEFAULT
    )
    passing = jnp.exp(cumulative[:, :, -1]) * (segment[:, -1] == 0)[:, None]
    entering = jnp.exp(cumulative) * (segment == 0)[:, None, :]
    current = incoming
    entries = []
    for position in range(blocks):
        entries.append(current)
        current = passing[position][:, None, None] * current + produced[position]
    carried = jnp.einsum(
        "khq,kqn,khpn->kqhp", entering, read_blocks, jnp.stack(entries), precision=lax.Precision.HIGHEST
    )
    return ((within + carried).reshape(length, head_count * HDIM), current)


def activate(
    projected,
    shared,
    timestep_in,
    edge_values,
    edge_shared,
    kernel,
    offset,
    filters,
    baseline,
    timing,
    damping,
):
    length = projected.shape[0]
    signal = jax.nn.silu(
        causal_conv(jnp.concatenate([edge_values, projected], axis=0), kernel, offset, length)
    )
    control_out = jax.nn.silu(
        causal_conv(jnp.concatenate([edge_shared, shared], axis=0), filters, baseline, length)
    )
    step_size = jax.nn.softplus(timestep_in + timing)
    log_decay = -step_size * jnp.exp(damping)
    return (signal, control_out[:, :STATE], control_out[:, STATE:], step_size, log_decay)


def shards(
    tokens,
    prenorm,
    gating,
    values,
    control,
    timestep,
    kernel,
    offset,
    filters,
    baseline,
    timing,
    damping,
    direct,
    postnorm,
    readout,
    doc_starts,
    cotangent,
):
    contract_last = (((1,), (1,)), ((), ()))
    contract_first = (((0,), (0,)), ((), ()))
    gain_full = gather_small(prenorm, "head").reshape(-1)
    gathered = gather_columns(tokens, "head")
    residual = gathered.astype(jnp.float32)
    scale = lax.rsqrt(jnp.mean(residual * residual, axis=1, keepdims=True) + epsilon)
    unit_rows = residual * scale
    normed = (unit_rows * gain_full.astype(jnp.float32)).astype(jnp.bfloat16)
    gate_in = jnp.dot(normed, gating, preferred_element_type=jnp.float32)
    projected = jnp.dot(normed, values, preferred_element_type=jnp.float32)
    shared = jnp.dot(normed, control, preferred_element_type=jnp.float32)
    timestep_in = jnp.dot(normed, timestep, preferred_element_type=jnp.float32)
    width = kernel.shape[0] - 1
    length = tokens.shape[0]
    edge_values, edge_shared = shifted(
        (projected[length - width :], shared[length - width :]), "seq", 1
    )
    outputs, activate_back = jax.vjp(
        activate,
        projected,
        shared,
        timestep_in,
        edge_values,
        edge_shared,
        kernel,
        offset,
        filters,
        baseline,
        timing,
        damping,
    )
    signal, writers, readers, step_size, log_decay = outputs
    head_count = step_size.shape[1]
    running = jnp.cumsum(log_decay, axis=0)
    counted = jnp.cumsum(doc_starts)
    passing = jnp.exp(running[-1]) * (counted[-1] == 0)
    toward = (
        jnp.exp(jnp.where((counted == counted[-1])[:, None], running[-1] - running, -1e30))
        * step_size
    )
    produced = jnp.einsum(
        "th,thp,tn->hpn",
        toward,
        signal.reshape(length, head_count, HDIM),
        writers,
        precision=lax.Precision.HIGHEST,
    )
    prefix = prefix_state(passing, produced, "seq", False)

    def scan_local(signal_in, writers_in, readers_in, step_in, decay_in, incoming):
        return spanned_scan(
            signal_in, writers_in, readers_in, step_in, decay_in, doc_starts, incoming
        )

    scan_out, scan_back = jax.vjp(
        scan_local, signal, writers, readers, step_size, log_decay, prefix
    )
    skip = jnp.repeat(direct, HDIM)
    full = scan_out[0] + skip * signal
    gate = jax.nn.silu(gate_in)
    gated = full * gate
    squares = small_sum(jnp.sum(gated * gated, axis=1), "head")
    inverse = lax.rsqrt(squares / INNER + epsilon)[:, None]
    unit_gated = gated * inverse
    normalized = (unit_gated * postnorm).astype(jnp.bfloat16)
    partial_rows = lax.dot_general(
        normalized, readout, contract_last, preferred_element_type=jnp.float32
    ).astype(jnp.bfloat16)
    branch = scatter_columns(partial_rows, "head")
    mixed = (tokens.astype(jnp.float32) + branch).astype(jnp.bfloat16)
    upstream = gather_columns(cotangent, "head")
    norm_cot = jnp.dot(upstream, readout, preferred_element_type=jnp.float32)
    readout_local = lax.dot_general(
        upstream, normalized, contract_first, preferred_element_type=jnp.float32
    )
    postnorm_local = jnp.sum(norm_cot * unit_gated, axis=0)
    scaled_cot = norm_cot * postnorm
    inner_sum = small_sum(jnp.sum(scaled_cot * unit_gated, axis=1), "head")
    gated_cot = inverse * (scaled_cot - unit_gated * (inner_sum / INNER)[:, None])
    full_cot = gated_cot * gate
    sigmoid_gate = jax.nn.sigmoid(gate_in)
    gate_cot = gated_cot * full * sigmoid_gate * (1.0 + gate_in * (1.0 - sigmoid_gate))
    direct_local = jnp.sum((full_cot * signal).reshape(length, head_count, HDIM), axis=(0, 2))
    entering = jnp.exp(running) * (counted == 0)[:, None]
    pending = jnp.einsum(
        "th,thp,tn->hpn",
        entering,
        full_cot.reshape(length, head_count, HDIM),
        readers,
        precision=lax.Precision.HIGHEST,
    )
    suffix = prefix_state(passing, pending, "seq", True)
    signal_cot, writer_cot, reader_cot, step_cot, decay_cot, ignored = scan_back(
        (full_cot, suffix)
    )
    signal_cot = signal_cot + skip * full_cot
    back = activate_back((signal_cot, writer_cot, reader_cot, step_cot, decay_cot))
    values_cot, shared_cot, timestep_cot, edge_values_cot, edge_shared_cot = (
        back[0],
        back[1],
        back[2],
        back[3],
        back[4],
    )
    kernel_local, offset_local, filters_local, baseline_local, timing_local, damping_local = (
        back[5],
        back[6],
        back[7],
        back[8],
        back[9],
        back[10],
    )
    later_values, later_shared = shifted((edge_values_cot, edge_shared_cot), "seq", -1)
    values_cot = values_cot.at[length - width :].add(later_values)
    shared_cot = shared_cot.at[length - width :].add(later_shared)
    gate_low = gate_cot.astype(jnp.bfloat16)
    values_low = values_cot.astype(jnp.bfloat16)
    shared_low = shared_cot.astype(jnp.bfloat16)
    timestep_low = timestep_cot.astype(jnp.bfloat16)
    normed_cot = lax.dot_general(
        gate_low, gating, contract_last, preferred_element_type=jnp.float32
    )
    normed_cot = normed_cot + lax.dot_general(
        values_low, values, contract_last, preferred_element_type=jnp.float32
    )
    normed_cot = normed_cot + lax.dot_general(
        shared_low, control, contract_last, preferred_element_type=jnp.float32
    )
    normed_cot = normed_cot + lax.dot_general(
        timestep_low, timestep, contract_last, preferred_element_type=jnp.float32
    )
    gating_local = lax.dot_general(
        normed, gate_low, contract_first, preferred_element_type=jnp.float32
    )
    values_local = lax.dot_general(
        normed, values_low, contract_first, preferred_element_type=jnp.float32
    )
    control_local = lax.dot_general(
        normed, shared_low, contract_first, preferred_element_type=jnp.float32
    )
    timestep_local = lax.dot_general(
        normed, timestep_low, contract_first, preferred_element_type=jnp.float32
    )
    share = tokens.shape[1]
    heads = lax.axis_size("head")
    begin = lax.axis_index("head") * share
    unit_gain = gain_full.astype(jnp.float32)
    cot_units = normed_cot * unit_rows
    prenorm_local = jnp.sum(cot_units, axis=0)
    row_mean = small_sum(jnp.sum(cot_units * unit_gain, axis=1), "head") / D
    own_total = scatter_columns(normed_cot.astype(jnp.bfloat16), "head")
    own_units = tokens.astype(jnp.float32) * scale
    tokens_gradient = cotangent.astype(jnp.float32) + scale * (
        own_total * prenorm.astype(jnp.float32) - own_units * row_mean[:, None]
    )
    gating_gradient, values_gradient, readout_gradient = (
        scatter_rows(gating_local.astype(jnp.bfloat16), "seq"),
        scatter_rows(values_local.astype(jnp.bfloat16), "seq"),
        scatter_rows(readout_local.astype(jnp.bfloat16), "seq"),
    )
    timestep_gradient = scatter_rows(timestep_local, "seq")
    control_gradient = sum_everywhere(control_local)
    everywhere = (filters_local, baseline_local, prenorm_local)
    split = (kernel_local, offset_local, timing_local, damping_local, direct_local, postnorm_local)
    flat_every = jnp.concatenate([item.reshape(-1) for item in everywhere])
    flat_split = jnp.concatenate([item.reshape(-1) for item in split])
    flat = doubled_sum(jnp.concatenate([flat_every, flat_split]), "seq")
    blocks = gather_small(flat, "head")
    summed = jnp.sum(blocks[:, : flat_every.shape[0]], axis=0)
    totals = []
    place = 0
    for item in everywhere:
        totals.append(summed[place : place + item.size].reshape(item.shape))
        place += item.size
    for item in split:
        piece = blocks[:, place : place + item.size].reshape((heads,) + item.shape)
        totals.append(jnp.moveaxis(piece, 0, -2).reshape(item.shape[:-1] + (-1,)))
        place += item.size
    return (
        mixed,
        tokens_gradient,
        totals[2],
        gating_gradient,
        values_gradient,
        control_gradient,
        timestep_gradient,
        totals[3],
        totals[4],
        totals[0],
        totals[1],
        totals[5],
        totals[6],
        totals[7],
        totals[8],
        readout_gradient,
    )


def solution(mesh):
    return jax.shard_map(
        shards,
        mesh=mesh,
        in_specs=(
            P("seq", "head"),
            P("head"),
            P(None, "head"),
            P(None, "head"),
            P(),
            P(None, "head"),
            P(None, "head"),
            P("head"),
            P(),
            P(),
            P("head"),
            P("head"),
            P("head"),
            P("head"),
            P(None, "head"),
            P("seq"),
            P("seq", "head"),
        ),
        out_specs=(
            P("seq", "head"),
            P("seq", "head"),
            P(),
            P("seq", "head"),
            P("seq", "head"),
            P(),
            P("seq", "head"),
            P(),
            P(),
            P(),
            P(),
            P(),
            P(),
            P(),
            P(),
            P("seq", "head"),
        ),
        check_vma=False,
    )
```

```python
import jax
import jax.numpy as jnp
from jax import lax
from jax.experimental import pallas as pl
from jax.experimental.pallas import tpu as pltpu
from jax.sharding import PartitionSpec as P

HDIM = 64
STATE = 128
SPAN = 128
BLOCK = 256


epsilon = 1e-05


def shifted(value, axis, steps):
    count = lax.axis_size(axis)
    leading, last = (max(0, -steps), min(count, count - steps))
    return lax.ppermute(value, axis, [(source, source + steps) for source in range(leading, last)])


def rotation(count, steps):
    return [(source, (source + steps) % count) for source in range(count)]


def flips(count, bit):
    return [(source, source ^ (1 << bit)) for source in range(count)]


def bits_of(count):
    return count.bit_length() - 1


def gather_blocks(block, axis):
    count = lax.axis_size(axis)
    half = count // 2
    rows = block.shape[0] // 2
    found = [None] * count
    found[0] = block
    left = right = block
    for step in range(1, half):
        left = lax.ppermute(left, axis, rotation(count, 1))
        right = lax.ppermute(right, axis, rotation(count, -1))
        found[count - step] = left
        found[step] = right
    far_low = lax.ppermute(left[:rows], axis, rotation(count, 1))
    far_high = lax.ppermute(right[rows:], axis, rotation(count, -1))
    found[half] = jnp.concatenate([far_low, far_high], axis=0)
    return found


def gather_columns(block, axis):
    count = lax.axis_size(axis)
    me = lax.axis_index(axis)
    width = block.shape[1]
    whole = jnp.zeros((block.shape[0], count * width), block.dtype)
    for step, piece in enumerate(gather_blocks(block, axis)):
        whole = lax.dynamic_update_slice_in_dim(whole, piece, (me + step) % count * width, 1)
    return whole


def scatter_columns(whole, axis):
    count = lax.axis_size(axis)
    me = lax.axis_index(axis)
    half = count // 2
    width = whole.shape[1] // count
    rows = whole.shape[0] // 2

    def part(step):
        return lax.dynamic_slice_in_dim(whole, (me + step) % count * width, width, 1)

    far = part(half)
    ahead = lax.ppermute(far[:rows].astype(jnp.bfloat16), axis, rotation(count, 1))
    behind = lax.ppermute(far[rows:].astype(jnp.bfloat16), axis, rotation(count, -1))
    first = True
    for step in range(half - 1, 0, -1):
        up = part(step).astype(jnp.float32)
        down = part(count - step).astype(jnp.float32)
        if first:
            up = up.at[:rows].add(ahead.astype(jnp.float32))
            down = down.at[rows:].add(behind.astype(jnp.float32))
            first = False
        else:
            up = up + ahead.astype(jnp.float32)
            down = down + behind.astype(jnp.float32)
        ahead = lax.ppermute(up.astype(jnp.bfloat16), axis, rotation(count, 1))
        behind = lax.ppermute(down.astype(jnp.bfloat16), axis, rotation(count, -1))
    return part(0).astype(jnp.float32) + ahead.astype(jnp.float32) + behind.astype(jnp.float32)


def small_sum(value, axis):
    count = lax.axis_size(axis)
    total = value
    for step in range(1, count):
        total = total + lax.ppermute(value, axis, rotation(count, step))
    return total


def doubled_sum(value, axis):
    count = lax.axis_size(axis)
    for bit in range(bits_of(count)):
        value = value + lax.ppermute(value, axis, flips(count, bit))
    return value


def halve(value, axis, bit, position):
    count = lax.axis_size(axis)
    mine = (lax.axis_index(axis) >> bit) & 1
    kept = lax.dynamic_index_in_dim(value, mine, position, False)
    sent = lax.dynamic_index_in_dim(value, 1 - mine, position, False)
    return kept + lax.ppermute(sent, axis, flips(count, bit))


def scatter_rows(value, axis):
    count = lax.axis_size(axis)
    bits = bits_of(count)
    rows, columns = value.shape
    split = value.reshape((2,) * bits + (rows // count, columns))
    split = halve(split, axis, 0, bits - 1)
    parts = []
    for piece in range(2):
        half = split[..., piece * (columns // 2) : (piece + 1) * (columns // 2)]
        left = list(range(bits - 1, 0, -1))
        order = list(range(1, bits)) if piece == 0 else list(range(bits - 1, 0, -1))
        for bit in order:
            half = halve(half, axis, bit, left.index(bit))
            left.remove(bit)
        parts.append(half)
    return jnp.concatenate(parts, axis=1).astype(jnp.float32)


def prefix_state(passing, state, axis, reverse):
    count = lax.axis_size(axis)
    me = lax.axis_index(axis)
    depth = state.shape[0]
    total = jnp.concatenate([state, jnp.broadcast_to(passing, (8, state.shape[1]))], axis=0)
    prefix = jnp.zeros_like(state)
    prefix_pass = jnp.ones_like(passing)
    for bit in range(bits_of(count)):
        other = lax.ppermute(total, axis, flips(count, bit))
        upper = ((me >> bit) & 1) == 1
        other_first = jnp.logical_not(upper) if reverse else upper
        other_state, other_pass = other[:depth], other[depth : depth + 1]
        total_state, total_pass = total[:depth], total[depth : depth + 1]
        prefix = jnp.where(other_first, prefix_pass * other_state + prefix, prefix)
        prefix_pass = jnp.where(other_first, prefix_pass * other_pass, prefix_pass)
        if bit < bits_of(count) - 1:
            joined = jnp.where(other_first, total_pass * other_state + total_state, other_pass * total_state + other_state)
            total = jnp.concatenate([joined, jnp.broadcast_to(total_pass * other_pass, (8, state.shape[1]))], axis=0)
    return prefix


def gather_small(value, axis):
    count = lax.axis_size(axis)
    me = lax.axis_index(axis)
    whole = jnp.zeros((count,) + value.shape, value.dtype)
    for step in range(count):
        piece = value if step == 0 else lax.ppermute(value, axis, rotation(count, -step))
        whole = lax.dynamic_update_index_in_dim(whole, piece, (me + step) % count, 0)
    return whole


def sum_everywhere(value):
    count, heads = lax.axis_size("seq"), lax.axis_size("head")
    bits = bits_of(count)
    rows, columns = value.shape
    split = value.reshape((2,) * bits + (rows // count, columns))
    for bit in range(bits):
        split = halve(split, "seq", bit, bits - 1 - bit)
    blocks = split.reshape(heads, rows // count // heads, columns)
    me = lax.axis_index("head")
    total = lax.dynamic_index_in_dim(blocks, me, 0, False)
    for step in range(1, heads):
        sent = lax.dynamic_index_in_dim(blocks, (me + step) % heads, 0, False)
        total = total + lax.ppermute(sent, "head", rotation(heads, step))
    whole = gather_small(total.astype(jnp.bfloat16), "head").reshape(rows // count, columns)
    place = lax.axis_index("seq")
    for bit in range(bits - 1, -1, -1):
        other = lax.ppermute(whole, "seq", flips(count, bit))
        upper = ((place >> bit) & 1) == 1
        low = jnp.where(upper, other, whole)
        high = jnp.where(upper, whole, other)
        whole = jnp.stack([low, high])
    order = list(range(bits - 1, -1, -1)) + [bits, bits + 1]
    return whole.transpose(order).reshape(rows, columns).astype(jnp.float32)


def dot(a, b, dims=(((1,), (0,)), ((), ()))):
    return lax.dot_general(a, b, dims, preferred_element_type=jnp.float32)


LAST = (((1,), (1,)), ((), ()))
FIRST = (((0,), (0,)), ((), ()))


def halves(value):
    high = value.astype(jnp.bfloat16)
    return high, (value - high.astype(jnp.float32)).astype(jnp.bfloat16)


def spread_heads(value, expand):
    high, rest = halves(value)
    return dot(high, expand) + dot(rest, expand)


def sum_heads(value, expand):
    high, rest = halves(value)
    return dot(high, expand, LAST) + dot(rest, expand, LAST)


def two_part(state):
    return jnp.concatenate(halves(state), axis=0)


def twice(value):
    value = value.astype(jnp.bfloat16)
    return jnp.concatenate([value, value], axis=1)


def triangle(size, upper):
    row = lax.broadcasted_iota(jnp.int32, (size, size), 0)
    column = lax.broadcasted_iota(jnp.int32, (size, size), 1)
    keep = column >= row if upper else row >= column
    return jnp.where(keep, 1.0, 0.0).astype(jnp.float32)


def exact_dot(a, b):
    return lax.dot_general(
        a, b, (((1,), (0,)), ((), ())), precision=lax.Precision.HIGHEST, preferred_element_type=jnp.float32
    )


def pair_blocks(value):
    lane = lax.broadcasted_iota(jnp.int32, value.shape, 1)
    zero = jnp.zeros_like(value)
    return jnp.concatenate(
        [jnp.where(lane < HDIM, value, zero), jnp.where(lane >= HDIM, value, zero)], axis=0
    )


def conv_rows(extended, taps, bias, rows):
    count = taps.shape[0]
    total = bias
    for tap in range(count):
        begin = 8 - (count - 1) + tap
        total = total + taps[tap : tap + 1] * extended[begin : begin + rows, :]
    return total


def head_terms(dt, timing, damping, seg_column, seg_row):
    value = dt + timing
    step = jnp.maximum(value, 0.0) + jnp.log1p(jnp.exp(-jnp.abs(value)))
    rate = jnp.exp(damping)
    log_decay = -step * rate
    rows = dt.shape[0]
    running = exact_dot(triangle(rows, False), log_decay)
    last = running[rows - 1 : rows]
    seg_last = seg_row[:, rows - 1 : rows]
    entering = jnp.where(seg_column == 0.0, jnp.exp(running), 0.0)
    toward = jnp.where(seg_column == seg_last, jnp.exp(last - running), 0.0)
    return value, step, rate, log_decay, running, entering, toward


def forward_kernel(
    proj, shared, dt, seg_col, seg_row, edge_v, edge_s, taps, offset, filters, baseline, timing, damping, skip, expand,
    full, readers_out, run_out, entry_out, states_out, final_out,
    ext_v, ext_s, state, carried,
):
    rows = dt.shape[0]
    heads = dt.shape[1]

    @pl.when(pl.program_id(0) == 0)
    def start():
        ext_v[0:8, :] = edge_v[...]
        ext_s[0:8, :] = edge_s[...]
        state[...] = jnp.zeros_like(state)
        carried[...] = jnp.ones_like(carried)

    ext_v[8 : 8 + rows, :] = proj[...]
    ext_s[8 : 8 + rows, :] = shared[...]
    pre = conv_rows(ext_v, taps[...], offset[...], rows)
    signal = pre * jax.nn.sigmoid(pre)
    pre_c = conv_rows(ext_s, filters[...], baseline[...], rows)
    control = pre_c * jax.nn.sigmoid(pre_c)
    ext_v[0:8, :] = ext_v[rows : rows + 8, :]
    ext_s[0:8, :] = ext_s[rows : rows + 8, :]
    writers = control[:, :STATE].astype(jnp.bfloat16)
    readers = control[:, STATE:].astype(jnp.bfloat16)
    readers_out[...] = readers
    seg_c, seg_r = seg_col[...], seg_row[0]
    value, step, rate, log_decay, running, entering, toward = head_terms(dt[...], timing[...], damping[...], seg_c, seg_r)
    across = running.T
    row = lax.broadcasted_iota(jnp.int32, (rows, rows), 0)
    column = lax.broadcasted_iota(jnp.int32, (rows, rows), 1)
    bias = jnp.where((seg_c == seg_r) & (row >= column), 0.0, -1e30)
    scores = dot(readers, writers, LAST)
    bias = jnp.concatenate([bias, bias], axis=1)
    scores = jnp.concatenate([scores, scores], axis=1)
    spread = spread_heads(jnp.concatenate([step, entering, toward, entering * carried[...]], axis=0), expand[...])
    step_e, enter_e, toward_e = spread[:rows], spread[rows : 2 * rows], spread[2 * rows : 3 * rows]
    run_out[...] = entering * carried[...]
    weighted = signal * step_e
    low = weighted.astype(jnp.bfloat16)
    old = state[...]
    states_out[0] = old
    carry = dot(twice(readers), two_part(old)) * enter_e + skip[...] * signal
    for pair in range(heads // 2):
        a, b = 2 * pair, 2 * pair + 1
        lanes = slice(pair * 2 * HDIM, (pair + 1) * 2 * HDIM)
        ahead = jnp.concatenate(
            [running[:, a : a + 1] - across[a : a + 1], running[:, b : b + 1] - across[b : b + 1]], axis=1
        )
        mixing = (jnp.exp(ahead + bias) * scores).astype(jnp.bfloat16)
        full[:, lanes] = dot(mixing, pair_blocks(low[:, lanes])) + carry[:, lanes]
    passing = enter_e[rows - 1 : rows]
    new = passing * old + dot(writers, (weighted * toward_e).astype(jnp.bfloat16), FIRST)
    state[...] = new
    final_out[...] = new
    entry_out[0] = carried[...]
    carried[...] = carried[...] * entering[rows - 1 : rows]


def vmem(limit=56):
    return pltpu.CompilerParams(vmem_limit_bytes=limit * 1024 * 1024, dimension_semantics=("arbitrary",))


def whole_spec(array):
    return pl.BlockSpec(array.shape, lambda *index: (0,) * array.ndim)


def forward_scan(proj, shared, dt, seg_col, seg_row, edge_v, edge_s, taps, offset, filters, baseline, timing, damping, skip, expand):
    length, inner = proj.shape
    heads = dt.shape[1]
    blocks = length // SPAN
    rows2 = lambda width: pl.BlockSpec((SPAN, width), lambda c: (c, 0))
    fixed = (edge_v, edge_s, taps, offset, filters, baseline, timing, damping, skip, expand)
    return pl.pallas_call(
        forward_kernel,
        grid=(blocks,),
        in_specs=[rows2(inner), rows2(2 * STATE), rows2(heads), rows2(1), pl.BlockSpec((1, 1, SPAN), lambda c: (c, 0, 0))]
        + [whole_spec(a) for a in fixed],
        out_specs=[
            rows2(inner), rows2(STATE), rows2(heads),
            pl.BlockSpec((1, 1, heads), lambda c: (c, 0, 0)),
            pl.BlockSpec((1, STATE, inner), lambda c: (c, 0, 0)),
            pl.BlockSpec((STATE, inner), lambda c: (0, 0)),
        ],
        out_shape=[
            jax.ShapeDtypeStruct((length, inner), jnp.float32),
            jax.ShapeDtypeStruct((length, STATE), jnp.bfloat16),
            jax.ShapeDtypeStruct((length, heads), jnp.float32),
            jax.ShapeDtypeStruct((blocks, 1, heads), jnp.float32),
            jax.ShapeDtypeStruct((blocks, STATE, inner), jnp.float32),
            jax.ShapeDtypeStruct((STATE, inner), jnp.float32),
        ],
        scratch_shapes=[
            pltpu.VMEM((SPAN + 8, inner), jnp.float32),
            pltpu.VMEM((SPAN + 8, 2 * STATE), jnp.float32),
            pltpu.VMEM((STATE, inner), jnp.float32),
            pltpu.VMEM((1, heads), jnp.float32),
        ],
        compiler_params=vmem(),
    )(proj, shared, dt, seg_col, seg_row, *fixed)


def join_kernel(local, readers, run, gate_in, incoming, expand, full, squares):
    run_e = spread_heads(run[...], expand[...])
    value = local[...] + run_e * dot(twice(readers[...]), two_part(incoming[...]))
    full[...] = value
    gate = gate_in[...]
    gated = value * gate * jax.nn.sigmoid(gate)
    squares[...] = jnp.sum(gated * gated, axis=1, keepdims=True)


def join_incoming(local, readers, run, gate_in, incoming, expand):
    length, inner = local.shape
    heads = run.shape[1]
    rows2 = lambda width: pl.BlockSpec((BLOCK, width), lambda c: (c, 0))
    return pl.pallas_call(
        join_kernel,
        grid=(length // BLOCK,),
        in_specs=[rows2(inner), rows2(STATE), rows2(heads), rows2(inner), whole_spec(incoming), whole_spec(expand)],
        out_specs=[rows2(inner), rows2(1)],
        out_shape=[jax.ShapeDtypeStruct((length, inner), jnp.float32), jax.ShapeDtypeStruct((length, 1), jnp.float32)],
        compiler_params=vmem(),
    )(local, readers, run, gate_in, incoming, expand)


def norm_cot_kernel(upstream, readout, full, gate_in, inverse, postnorm, norm_cot, inner_sum, gain_sum):
    @pl.when(pl.program_id(0) == 0)
    def start():
        gain_sum[...] = jnp.zeros_like(gain_sum)

    cot = dot(upstream[...], readout[...])
    norm_cot[...] = cot
    gate = gate_in[...]
    product = cot * (full[...] * gate * jax.nn.sigmoid(gate) * inverse[...])
    gain_sum[...] += jnp.sum(product.reshape(-1, 8, product.shape[1]), axis=0)
    inner_sum[...] = jnp.sum(product * postnorm[...], axis=1, keepdims=True)


def norm_cotangent(upstream, readout, full, gate_in, inverse, postnorm):
    length, inner = full.shape
    rows2 = lambda width: pl.BlockSpec((BLOCK, width), lambda c: (c, 0))
    return pl.pallas_call(
        norm_cot_kernel,
        grid=(length // BLOCK,),
        in_specs=[rows2(upstream.shape[1]), whole_spec(readout), rows2(inner), rows2(inner), rows2(1), whole_spec(postnorm)],
        out_specs=[rows2(inner), rows2(1), pl.BlockSpec((8, inner), lambda c: (0, 0))],
        out_shape=[
            jax.ShapeDtypeStruct((length, inner), jnp.float32),
            jax.ShapeDtypeStruct((length, 1), jnp.float32),
            jax.ShapeDtypeStruct((8, inner), jnp.float32),
        ],
        compiler_params=vmem(),
    )(upstream, readout, full, gate_in, inverse, postnorm)


def gate_kernel(norm_cot, full_in, gate_in, inverse, mean, postnorm, run, readers, expand, full_cot, gate_low, pending):
    @pl.when(pl.program_id(0) == 0)
    def start():
        pending[...] = jnp.zeros_like(pending)

    gate, full = gate_in[...], full_in[...]
    sigmoid = jax.nn.sigmoid(gate)
    active = gate * sigmoid
    scaled = inverse[...]
    unit = full * active * scaled
    gated_cot = scaled * (norm_cot[...] * postnorm[...] - unit * mean[...])
    cot = gated_cot * active
    full_cot[...] = cot
    gate_low[...] = (gated_cot * full * sigmoid * (1.0 + gate * (1.0 - sigmoid))).astype(jnp.bfloat16)
    run_e = spread_heads(run[...], expand[...])
    high, rest = halves(cot * run_e)
    pending[...] += dot(readers[...], high, FIRST)


def gate_cotangent(norm_cot, full, gate_in, inverse, mean, postnorm, run, readers, expand):
    length, inner = full.shape
    heads = run.shape[1]
    rows2 = lambda width: pl.BlockSpec((BLOCK, width), lambda c: (c, 0))
    return pl.pallas_call(
        gate_kernel,
        grid=(length // BLOCK,),
        in_specs=[rows2(inner), rows2(inner), rows2(inner), rows2(1), rows2(1), whole_spec(postnorm), rows2(heads), rows2(STATE), whole_spec(expand)],
        out_specs=[rows2(inner), rows2(inner), pl.BlockSpec((STATE, inner), lambda c: (0, 0))],
        out_shape=[
            jax.ShapeDtypeStruct((length, inner), jnp.float32),
            jax.ShapeDtypeStruct((length, inner), jnp.bfloat16),
            jax.ShapeDtypeStruct((STATE, inner), jnp.float32),
        ],
        compiler_params=vmem(),
    )(norm_cot, full, gate_in, inverse, mean, postnorm, run, readers, expand)


def silu_slope(pre, sigmoid):
    return sigmoid * (1.0 + pre * (1.0 - sigmoid))


def fold(value):
    return jnp.sum(value.reshape(-1, 8, value.shape[1]), axis=0)


def taps_back(pre_cot, taps, following, rows):
    count = taps.shape[0]
    total = taps[count - 1 : count] * pre_cot
    for tap in range(count - 1):
        later = count - 1 - tap
        total = total + taps[tap : tap + 1] * following[later : later + rows, :]
    return total


def backward_kernel(
    proj, shared, before_v, before_s, dt, seg_col, seg_row, full_cot, states, entry,
    edge_v, edge_s, taps, offset, filters, baseline, timing, damping, skip, expand, incoming, leaving, after_v, after_s,
    values_low, shared_low, dt_low, tap_sum, offset_sum, filter_sum, base_sum, timing_sum, damping_sum, direct_sum,
    tail_v, tail_s, head_v, head_s,
    ext_v, ext_s, later_v, later_s, lam,
):
    rows, heads = dt.shape
    step_index = pl.program_id(0)
    blocks = pl.num_programs(0)

    @pl.when(step_index == 0)
    def start():
        lam[...] = leaving[...]
        later_v[rows : rows + 8, :] = after_v[...]
        later_s[rows : rows + 8, :] = after_s[...]
        for item in (tap_sum, offset_sum, filter_sum, base_sum, timing_sum, damping_sum, direct_sum):
            item[...] = jnp.zeros_like(item)

    @pl.when(step_index == blocks - 1)
    def first_block():
        ext_v[0:8, :] = edge_v[...]
        ext_s[0:8, :] = edge_s[...]

    @pl.when(step_index < blocks - 1)
    def other_block():
        ext_v[0:8, :] = before_v[...]
        ext_s[0:8, :] = before_s[...]

    ext_v[8 : 8 + rows, :] = proj[...]
    ext_s[8 : 8 + rows, :] = shared[...]
    pre = conv_rows(ext_v, taps[...], offset[...], rows)
    sigmoid = jax.nn.sigmoid(pre)
    signal = pre * sigmoid
    pre_c = conv_rows(ext_s, filters[...], baseline[...], rows)
    sigmoid_c = jax.nn.sigmoid(pre_c)
    control = pre_c * sigmoid_c
    writers = control[:, :STATE].astype(jnp.bfloat16)
    readers = control[:, STATE:].astype(jnp.bfloat16)
    seg_c, seg_r = seg_col[...], seg_row[0]
    value, step, rate, log_decay, running, entering, toward = head_terms(dt[...], timing[...], damping[...], seg_c, seg_r)
    across = running.T
    row = lax.broadcasted_iota(jnp.int32, (rows, rows), 0)
    column = lax.broadcasted_iota(jnp.int32, (rows, rows), 1)
    bias = jnp.where((seg_c == seg_r) & (column >= row), 0.0, -1e30)
    scores = dot(writers, readers, LAST)
    bias = jnp.concatenate([bias, bias], axis=1)
    scores = jnp.concatenate([scores, scores], axis=1)
    one_hot = expand[...]
    spread = spread_heads(jnp.concatenate([step, entering, toward], axis=0), one_hot)
    step_e, enter_e, toward_e = spread[:rows], spread[rows : 2 * rows], spread[2 * rows : 3 * rows]
    cot = full_cot[...]
    cot_low = cot.astype(jnp.bfloat16)
    weighted = signal * step_e
    low = weighted.astype(jnp.bfloat16)
    after = lam[...]
    after_parts = two_part(after)
    from_state = dot(twice(writers), after_parts) * toward_e
    entry_e = spread_heads(jnp.broadcast_to(entry[0], (8, heads)), one_hot)
    old = states[0] + entry_e[0:1] * incoming[...]
    old_parts = two_part(old)
    cot_entering = cot * enter_e
    cot_entering_low = cot_entering.astype(jnp.bfloat16)
    score_cot = jnp.zeros((rows, rows), jnp.float32)
    row_sums = jnp.zeros((rows, heads), jnp.float32)
    column_sums = []
    ones = jnp.ones((8, rows), jnp.bfloat16)
    place = lax.broadcasted_iota(jnp.int32, (2 * rows, heads), 0) // rows
    head_place = lax.broadcasted_iota(jnp.int32, (2 * rows, heads), 1)
    direct_part = []
    step_part = []
    for pair in range(heads // 2):
        a, b = 2 * pair, 2 * pair + 1
        lanes = slice(pair * 2 * HDIM, (pair + 1) * 2 * HDIM)
        ahead = jnp.concatenate(
            [across[a : a + 1] - running[:, a : a + 1], across[b : b + 1] - running[:, b : b + 1]], axis=1
        )
        decays = jnp.exp(ahead + bias)
        mixing = decays * scores
        blocked = pair_blocks(cot_low[:, lanes])
        weighted_cot = dot(mixing.astype(jnp.bfloat16), blocked) + from_state[:, lanes]
        step_part.append(weighted_cot * signal[:, lanes])
        later_v[0:rows, lanes] = weighted_cot * step_e[:, lanes] + skip[:, lanes] * cot[:, lanes]
        inner = dot(low[:, lanes], blocked, LAST)
        linked = inner * decays
        score_cot = score_cot + linked[:, :rows] + linked[:, rows:]
        energy = (inner * mixing).astype(jnp.bfloat16)
        chosen = jnp.where(head_place == place + a, 1.0, 0.0).astype(jnp.bfloat16)
        row_sums = row_sums + dot(energy, chosen)
        column_sums.append(dot(ones, energy))
    step_cot = sum_heads(jnp.concatenate(step_part, axis=1), one_hot)
    sums_across = jnp.concatenate(
        [piece for pair in column_sums for piece in (pair[0:1, :rows], pair[0:1, rows:])], axis=0
    )
    state_term = weighted * from_state
    enter_term = cot_entering * dot(twice(readers), old_parts)
    passing = enter_e[rows - 1 : rows]
    last_term = fold(state_term) + fold(after * old * passing)
    running_cot = sums_across.T - row_sums + sum_heads(enter_term - state_term, one_hot)
    last_cot = jnp.sum(sum_heads(last_term, one_hot), axis=0, keepdims=True)
    decay_cot = exact_dot(triangle(rows, True), running_cot) + last_cot
    step_cot = step_cot - decay_cot * rate
    dt_cot = step_cot * jax.nn.sigmoid(value)
    dt_low[...] = dt_cot.astype(jnp.bfloat16)
    timing_sum[...] += fold(dt_cot)
    damping_sum[...] += fold(decay_cot * log_decay)
    direct_sum[...] += fold(cot * signal)
    score_low = score_cot.astype(jnp.bfloat16)
    reader_cot = dot(score_low, writers, FIRST) + dot(
        jnp.concatenate([cot_entering_low, cot_entering_low], axis=1), jnp.concatenate(halves(old), axis=1), LAST
    )
    push = (weighted * toward_e).astype(jnp.bfloat16)
    writer_cot = dot(score_low, readers) + dot(
        jnp.concatenate([push, push], axis=1), jnp.concatenate(halves(after), axis=1), LAST
    )
    lam[...] = passing * after + dot(readers, cot_entering_low, FIRST)

    pre_cot = later_v[0:rows, :] * silu_slope(pre, sigmoid)
    later_v[0:rows, :] = pre_cot
    pre_cot_c = jnp.concatenate([writer_cot, reader_cot], axis=1) * silu_slope(pre_c, sigmoid_c)
    later_s[0:rows, :] = pre_cot_c
    values_cot = taps_back(pre_cot, taps[...], later_v, rows)
    shared_cot = taps_back(pre_cot_c, filters[...], later_s, rows)
    values_low[...] = values_cot.astype(jnp.bfloat16)
    shared_low[...] = shared_cot.astype(jnp.bfloat16)
    count = taps.shape[0]
    for tap in range(count):
        begin = 8 - (count - 1) + tap
        tap_sum[tap] += fold(pre_cot * ext_v[begin : begin + rows, :])
        filter_sum[tap] += fold(pre_cot_c * ext_s[begin : begin + rows, :])
    offset_sum[...] += fold(pre_cot)
    base_sum[...] += fold(pre_cot_c)
    later_v[rows : rows + 8, :] = later_v[0:8, :]
    later_s[rows : rows + 8, :] = later_s[0:8, :]

    @pl.when(step_index == 0)
    def tail():
        tail_v[...] = values_cot[rows - 8 :, :]
        tail_s[...] = shared_cot[rows - 8 :, :]

    @pl.when(step_index == blocks - 1)
    def head():
        head_v[...] = pre_cot[0:8, :]
        head_s[...] = pre_cot_c[0:8, :]


def backward_scan(
    proj, shared, dt, seg_col, seg_row, full_cot, states, entry,
    edge_v, edge_s, taps, offset, filters, baseline, timing, damping, skip, expand, incoming, leaving, after_v, after_s,
):
    length, inner = proj.shape
    heads = dt.shape[1]
    blocks = length // SPAN
    count = taps.shape[0]
    back = lambda c: blocks - 1 - c
    rows2 = lambda width: pl.BlockSpec((SPAN, width), lambda c: (back(c), 0))
    before = lambda width: pl.BlockSpec((8, width), lambda c: (jnp.maximum(back(c) * (SPAN // 8) - 1, 0), 0))
    lead = lambda *shape: pl.BlockSpec((1,) + shape, lambda c: (back(c), 0, 0))
    fixed = (edge_v, edge_s, taps, offset, filters, baseline, timing, damping, skip, expand, incoming, leaving, after_v, after_s)
    f32 = lambda *shape: jax.ShapeDtypeStruct(shape, jnp.float32)
    sums = [f32(count, 8, inner), f32(8, inner), f32(count, 8, 2 * STATE), f32(8, 2 * STATE), f32(8, heads), f32(8, heads), f32(8, inner), f32(8, inner), f32(8, 2 * STATE), f32(8, inner), f32(8, 2 * STATE)]
    low = lambda width: jax.ShapeDtypeStruct((length, width), jnp.bfloat16)
    return pl.pallas_call(
        backward_kernel,
        grid=(blocks,),
        in_specs=[rows2(inner), rows2(2 * STATE), before(inner), before(2 * STATE), rows2(heads), rows2(1), lead(1, SPAN), rows2(inner), lead(STATE, inner), lead(1, heads)]
        + [whole_spec(a) for a in fixed],
        out_specs=[rows2(inner), rows2(2 * STATE), rows2(heads)] + [whole_spec(a) for a in sums],
        out_shape=[low(inner), low(2 * STATE), low(heads)] + sums,
        scratch_shapes=[
            pltpu.VMEM((SPAN + 8, inner), jnp.float32),
            pltpu.VMEM((SPAN + 8, 2 * STATE), jnp.float32),
            pltpu.VMEM((SPAN + 8, inner), jnp.float32),
            pltpu.VMEM((SPAN + 8, 2 * STATE), jnp.float32),
            pltpu.VMEM((STATE, inner), jnp.float32),
        ],
        compiler_params=vmem(),
    )(proj, shared, proj, shared, dt, seg_col, seg_row, full_cot, states, entry, *fixed)


def normed_cot_kernel(gate_low, values_low, shared_low, dt_low, gating, values, control, timestep, tokens, scale, gain, low, row_sum, gain_sum):
    @pl.when(pl.program_id(0) == 0)
    def start():
        gain_sum[...] = jnp.zeros_like(gain_sum)

    total = dot(gate_low[...], gating[...], LAST) + dot(values_low[...], values[...], LAST)
    total = total + dot(shared_low[...], control[...], LAST) + dot(dt_low[...], timestep[...], LAST)
    low[...] = total.astype(jnp.bfloat16)
    product = total * (tokens[...].astype(jnp.float32) * scale[...])
    gain_sum[...] += fold(product)
    row_sum[...] = jnp.sum(product * gain[...], axis=1, keepdims=True)


def normed_cotangent(gate_low, values_low, shared_low, dt_low, gating, values, control, timestep, tokens, scale, gain):
    length = gate_low.shape[0]
    width = gating.shape[0]
    rows2 = lambda size: pl.BlockSpec((BLOCK, size), lambda c: (c, 0))
    parts = (gate_low, values_low, shared_low, dt_low)
    weights = (gating, values, control, timestep)
    return pl.pallas_call(
        normed_cot_kernel,
        grid=(length // BLOCK,),
        in_specs=[rows2(a.shape[1]) for a in parts] + [whole_spec(a) for a in weights] + [rows2(width), rows2(1), whole_spec(gain)],
        out_specs=[rows2(width), rows2(1), pl.BlockSpec((8, width), lambda c: (0, 0))],
        out_shape=[
            jax.ShapeDtypeStruct((length, width), jnp.bfloat16),
            jax.ShapeDtypeStruct((length, 1), jnp.float32),
            jax.ShapeDtypeStruct((8, width), jnp.float32),
        ],
        compiler_params=vmem(),
    )(*parts, *weights, tokens, scale, gain)


def shards(
    tokens,
    prenorm,
    gating,
    values,
    control,
    timestep,
    kernel,
    offset,
    filters,
    baseline,
    timing,
    damping,
    direct,
    postnorm,
    readout,
    doc_starts,
    cotangent,
):
    length, share = tokens.shape
    inner = kernel.shape[1]
    heads = timing.shape[0]
    ranks = lax.axis_size("head")
    features = share * ranks
    channels = inner * ranks
    blocks = length // SPAN
    f32, bf16 = jnp.float32, jnp.bfloat16

    starts = doc_starts.reshape(blocks, SPAN).astype(bf16)
    place = jnp.arange(SPAN)
    counted = jnp.dot(starts, (place[:, None] <= place[None, :]).astype(bf16), preferred_element_type=f32)
    seg_row, seg_col = counted.reshape(blocks, 1, SPAN), counted.reshape(length, 1)
    expand = (jnp.arange(heads)[:, None] == jnp.arange(inner)[None, :] // HDIM).astype(bf16)
    skip = jnp.repeat(direct, HDIM)[None]
    offset_row, baseline_row, postnorm_row = offset[None], baseline[None], postnorm[None]
    timing_row, damping_row = timing[None], damping[None]

    gain = gather_small(prenorm, "head").reshape(1, features).astype(f32)
    gathered = gather_columns(tokens, "head")
    wide = gathered.astype(f32)
    scale = lax.rsqrt(jnp.mean(wide * wide, axis=1, keepdims=True) + epsilon)
    normed = (wide * scale * gain).astype(bf16)
    gate_in = jnp.dot(normed, gating, preferred_element_type=f32)
    projected = jnp.dot(normed, values, preferred_element_type=f32)
    shared = jnp.dot(normed, control, preferred_element_type=f32)
    timestep_in = jnp.dot(normed, timestep, preferred_element_type=f32)

    edge = shifted(jnp.concatenate([projected[length - 8 :], shared[length - 8 :]], axis=1), "seq", 1)
    edge_v, edge_s = edge[:, :inner], edge[:, inner:]
    local, readers, run, entry, states, final = forward_scan(
        projected, shared, timestep_in, seg_col, seg_row, edge_v, edge_s, kernel, offset_row, filters, baseline_row,
        timing_row, damping_row, skip, expand,
    )
    passing = jnp.repeat(run[length - 1 :], HDIM, axis=1)
    incoming = prefix_state(passing, final, "seq", False)
    full, squares = join_incoming(local, readers, run, gate_in, incoming, expand)
    squares = small_sum(squares.reshape(length), "head")
    inverse = lax.rsqrt(squares / channels + epsilon)[:, None]
    normalized = (full * jax.nn.silu(gate_in) * inverse * postnorm_row).astype(bf16)
    partial_rows = lax.dot_general(normalized, readout, LAST, preferred_element_type=f32).astype(bf16)
    branch = scatter_columns(partial_rows, "head")
    mixed = (tokens.astype(f32) + branch).astype(bf16)

    upstream = gather_columns(cotangent, "head")
    norm_cot, inner_sum, postnorm_sum = norm_cotangent(upstream, readout, full, gate_in, inverse, postnorm_row)
    mean = small_sum(inner_sum.reshape(length), "head")[:, None] / channels
    full_cot, gate_low, pending = gate_cotangent(
        norm_cot, full, gate_in, inverse, mean, postnorm_row, run, readers, expand
    )
    leaving = prefix_state(passing, pending, "seq", True)
    readout_local = lax.dot_general(upstream, normalized, FIRST, preferred_element_type=f32)
    gating_local = lax.dot_general(normed, gate_low, FIRST, preferred_element_type=f32)
    zeros_v, zeros_s = jnp.zeros((8, inner), f32), jnp.zeros((8, 2 * STATE), f32)
    (
        values_low, shared_low, timestep_low, tap_sum, offset_sum, filter_sum, base_sum, timing_sum, damping_sum, direct_sum,
        tail_v, tail_s, head_v, head_s,
    ) = backward_scan(
        projected, shared, timestep_in, seg_col, seg_row, full_cot, states, entry,
        edge_v, edge_s, kernel, offset_row, filters, baseline_row, timing_row, damping_row, skip, expand,
        incoming, leaving, zeros_v, zeros_s,
    )
    ahead = shifted(jnp.concatenate([head_v, head_s], axis=1), "seq", -1)
    ahead = jnp.concatenate([jnp.zeros_like(ahead), ahead], axis=0)
    taps = kernel.shape[0]
    for tap in range(taps):
        begin = taps - 1 - tap
        tail_v = tail_v + kernel[tap] * ahead[begin : begin + 8, :inner]
        tail_s = tail_s + filters[tap] * ahead[begin : begin + 8, inner:]
    values_low = values_low.at[length - 8 :].set(tail_v.astype(bf16))
    shared_low = shared_low.at[length - 8 :].set(tail_s.astype(bf16))

    normed_low, row_sum, prenorm_sum = normed_cotangent(
        gate_low, values_low, shared_low, timestep_low, gating, values, control, timestep, gathered, scale, gain
    )
    row_mean = small_sum(row_sum.reshape(length), "head")[:, None] / features
    own_total = scatter_columns(normed_low, "head")
    own_units = tokens.astype(f32) * scale
    tokens_gradient = cotangent.astype(f32) + scale * (own_total * prenorm.astype(f32) - own_units * row_mean)
    values_local = lax.dot_general(normed, values_low, FIRST, preferred_element_type=f32)
    control_local = lax.dot_general(normed, shared_low, FIRST, preferred_element_type=f32)
    timestep_local = lax.dot_general(normed, timestep_low, FIRST, preferred_element_type=f32)

    gating_gradient, values_gradient, readout_gradient = (
        scatter_rows(gating_local.astype(bf16), "seq"),
        scatter_rows(values_local.astype(bf16), "seq"),
        scatter_rows(readout_local.astype(bf16), "seq"),
    )
    timestep_gradient = scatter_rows(timestep_local, "seq")
    control_gradient = sum_everywhere(control_local)
    everywhere = (filter_sum.sum(1), base_sum.sum(0), prenorm_sum.sum(0))
    split = (
        tap_sum.sum(1), offset_sum.sum(0), timing_sum.sum(0), damping_sum.sum(0),
        direct_sum.sum(0).reshape(heads, HDIM).sum(1), postnorm_sum.sum(0),
    )
    flat_every = jnp.concatenate([item.reshape(-1) for item in everywhere])
    flat_split = jnp.concatenate([item.reshape(-1) for item in split])
    flat = doubled_sum(jnp.concatenate([flat_every, flat_split]), "seq")
    pieces = gather_small(flat, "head")
    summed = jnp.sum(pieces[:, : flat_every.shape[0]], axis=0)
    totals = []
    begin = 0
    for item in everywhere:
        totals.append(summed[begin : begin + item.size].reshape(item.shape))
        begin += item.size
    for item in split:
        piece = pieces[:, begin : begin + item.size].reshape((ranks,) + item.shape)
        totals.append(jnp.moveaxis(piece, 0, -2).reshape(item.shape[:-1] + (-1,)))
        begin += item.size
    return (
        mixed,
        tokens_gradient,
        totals[2],
        gating_gradient,
        values_gradient,
        control_gradient,
        timestep_gradient,
        totals[3],
        totals[4],
        totals[0],
        totals[1],
        totals[5],
        totals[6],
        totals[7],
        totals[8],
        readout_gradient,
    )


def solution(mesh):
    return jax.shard_map(
        shards,
        mesh=mesh,
        in_specs=(
            P("seq", "head"),
            P("head"),
            P(None, "head"),
            P(None, "head"),
            P(),
            P(None, "head"),
            P(None, "head"),
            P("head"),
            P(),
            P(),
            P("head"),
            P("head"),
            P("head"),
            P("head"),
            P(None, "head"),
            P("seq"),
            P("seq", "head"),
        ),
        out_specs=(
            P("seq", "head"),
            P("seq", "head"),
            P(),
            P("seq", "head"),
            P("seq", "head"),
            P(),
            P("seq", "head"),
            P(),
            P(),
            P(),
            P(),
            P(),
            P(),
            P(),
            P(),
            P("seq", "head"),
        ),
        check_vma=False,
    )
```

```python
import functools

import jax
import jax.numpy as jnp
from jax import lax
from jax.experimental import pallas as pl
from jax.experimental.pallas import tpu as pltpu
from jax.sharding import PartitionSpec as P

HDIM = 64
STATE = 128
SPAN = 128
BLOCK = 256


epsilon = 1e-05


def rotation(count, steps):
    return [(source, (source + steps) % count) for source in range(count)]


def flips(count, bit):
    return [(source, source ^ (1 << bit)) for source in range(count)]


def bits_of(count):
    return count.bit_length() - 1


class Chain:
    def __init__(self, gen):
        self.gen = gen
        self.result = None
        self.sends = None
        self.step(None)

    def step(self, moved):
        try:
            self.sends = self.gen.send(moved)
        except StopIteration as stop:
            self.sends, self.result = None, stop.value


def phase(chains, work=None, *inputs):
    chains = [chain for chain in chains if chain.sends is not None]
    values = [[send[0] for send in chain.sends] for chain in chains]
    values, inputs = lax.optimization_barrier((values, inputs))
    moved = [
        [lax.ppermute(value, send[1], send[2]) for value, send in zip(group, chain.sends)]
        for group, chain in zip(values, chains)
    ]
    outs = work(*inputs) if work is not None else ()
    moved, outs = lax.optimization_barrier((moved, outs))
    for chain, group in zip(chains, moved):
        chain.step(group)
    return outs


def finish(*chains):
    while any(chain.sends is not None for chain in chains):
        phase(chains)
    return [chain.result for chain in chains]


def gather_chain(block, axis):
    count = lax.axis_size(axis)
    half = count // 2
    rows = block.shape[0] // 2
    found = [None] * count
    found[0] = block
    left = right = block
    for step in range(1, half):
        left, right = yield [(left, axis, rotation(count, 1)), (right, axis, rotation(count, -1))]
        found[count - step] = left
        found[step] = right
    low, high = yield [(left[:rows], axis, rotation(count, 1)), (right[rows:], axis, rotation(count, -1))]
    found[half] = jnp.concatenate([low, high], axis=0)
    return found


def place_columns(found, axis):
    count = len(found)
    me = lax.axis_index(axis)
    width = found[0].shape[1]
    whole = jnp.zeros((found[0].shape[0], count * width), found[0].dtype)
    for step, piece in enumerate(found):
        whole = lax.dynamic_update_slice_in_dim(whole, piece, (me + step) % count * width, 1)
    return whole


def scatter_chain(whole, axis, pieces=1):
    count = lax.axis_size(axis)
    me = lax.axis_index(axis)
    half = count // 2
    width = whole.shape[1] // count
    rows = whole.shape[0] // 2

    def part(step):
        return lax.dynamic_slice_in_dim(whole, (me + step) % count * width, width, 1)

    far = part(half)
    ahead, behind = yield [(far[:rows], axis, rotation(count, 1)), (far[rows:], axis, rotation(count, -1))]
    for step in range(half - 1, 0, -1):
        up = part(step).astype(jnp.float32)
        down = part(count - step).astype(jnp.float32)
        if step == half - 1:
            up = up.at[:rows].add(ahead.astype(jnp.float32))
            down = down.at[rows:].add(behind.astype(jnp.float32))
        else:
            up = up + ahead.astype(jnp.float32)
            down = down + behind.astype(jnp.float32)
        arrived = []
        cuts = [2 * rows * cut // (16 * pieces) * 16 for cut in range(pieces + 1)]
        for begin, end in zip(cuts, cuts[1:]):
            arrived.append(
                (yield [
                    (up[begin:end].astype(jnp.bfloat16), axis, rotation(count, 1)),
                    (down[begin:end].astype(jnp.bfloat16), axis, rotation(count, -1)),
                ])
            )
        ahead, behind = [jnp.concatenate(side, axis=0) if pieces > 1 else side[0] for side in zip(*arrived)]
    return part(0).astype(jnp.float32) + ahead.astype(jnp.float32) + behind.astype(jnp.float32)


def sum_chain(value, axis):
    count = lax.axis_size(axis)
    moved = yield [(value, axis, rotation(count, step)) for step in range(1, count)]
    for other in moved:
        value = value + other
    return value


def split_half(value, axis, bit, position):
    mine = (lax.axis_index(axis) >> bit) & 1
    kept = lax.dynamic_index_in_dim(value, mine, position, False)
    sent = lax.dynamic_index_in_dim(value, 1 - mine, position, False)
    return kept, (sent, axis, flips(lax.axis_size(axis), bit))


def rows_chain(value, axis):
    count = lax.axis_size(axis)
    bits = bits_of(count)
    rows, columns = value.shape
    split = value.reshape((2,) * bits + (rows // count, columns))
    kept, send = split_half(split, axis, 0, bits - 1)
    (moved,) = yield [send]
    split = kept + moved
    parts = [split[..., : columns // 2], split[..., columns // 2 :]]
    orders = [list(range(1, bits)), list(range(bits - 1, 0, -1))]
    left = [list(range(bits - 1, 0, -1)) for _ in parts]
    for turn in range(bits - 1):
        keeps, sends = [], []
        for piece in range(2):
            bit = orders[piece][turn]
            kept, send = split_half(parts[piece], axis, bit, left[piece].index(bit))
            left[piece].remove(bit)
            keeps.append(kept)
            sends.append(send)
        moved = yield sends
        parts = [kept + other for kept, other in zip(keeps, moved)]
    return jnp.concatenate(parts, axis=1).astype(jnp.float32)


def state_chain(total, reverse):
    count = lax.axis_size("seq")
    me = lax.axis_index("seq")
    chips = count // 2
    chip, core = me // 2, me % 2
    (neighbour,) = yield [(total, "seq", flips(count, 0))]
    half = chip_state(total, neighbour, core, reverse)
    parts = yield [
        (half, "seq", [(source, source ^ (2 * step)) for source in range(count)]) for step in range(1, chips)
    ]
    entering = entering_state(chip, chips, reverse, parts)
    (other,) = yield [(entering, "seq", flips(count, 0))]
    return core_state(entering, other, neighbour, core, reverse)


def all_chain(value, axis):
    count = lax.axis_size(axis)
    me = lax.axis_index(axis)
    moved = yield [(value, axis, rotation(count, -step)) for step in range(1, count)]
    whole = jnp.zeros((count,) + value.shape, value.dtype)
    for step, piece in enumerate([value] + list(moved)):
        whole = lax.dynamic_update_index_in_dim(whole, piece, (me + step) % count, 0)
    return whole


def parts_of(value):
    high = lax.reduce_precision(value, 8, 7)
    return high.astype(jnp.bfloat16), (value - high).astype(jnp.bfloat16)


def shared_chain(value, flat, holder):
    count = lax.axis_size("seq")
    me = lax.axis_index("seq")
    rows, columns = value.shape
    chips = count // 2
    block = rows // count
    chip, core = me // 2, me % 2
    kept, send = split_half(value.reshape(chips, 2, block, columns), "seq", 0, 1)
    moved, flat_moved = yield [send, (flat, "seq", flips(count, 0))]
    own = kept + moved
    flat = flat + flat_moved
    flat_parts = parts_of(flat)
    depth = flat.shape[0]

    def chip_pairs(step):
        return [(source, source ^ (2 * step)) for source in range(count)]

    steps = range(1, chips)
    outgoing = [
        jnp.concatenate([lax.dynamic_index_in_dim(own, chip ^ step, 0, False).astype(jnp.bfloat16), *flat_parts], axis=0)
        for step in steps
    ]
    moved = yield [(part, "seq", chip_pairs(step)) for part, step in zip(outgoing, steps)]
    own = lax.dynamic_index_in_dim(own, chip, 0, False)
    held = jnp.zeros((chips, 2 * depth, columns), jnp.bfloat16)
    held = lax.dynamic_update_index_in_dim(held, jnp.concatenate(flat_parts, axis=0), chip, 0)
    for step, other in zip(steps, moved):
        own = own + other[:block].astype(jnp.float32)
        held = lax.dynamic_update_index_in_dim(held, other[block:], chip ^ step, 0)
    held = held.astype(jnp.float32)
    flat = jnp.sum(held[:, :depth] + held[:, depth:], axis=0)
    pieces = yield from all_chain(jnp.concatenate([own.astype(jnp.bfloat16), *parts_of(flat)], axis=0), "head")
    mine = jnp.sum(pieces[:, :block].astype(jnp.float32), axis=0).astype(jnp.bfloat16)
    copies = pieces[:, block:].astype(jnp.float32)
    copies = copies[:, :depth] + copies[:, depth:]
    holder.append(copies)
    moved = yield [(mine, "seq", chip_pairs(step)) for step in steps]
    found = jnp.zeros((chips,) + mine.shape, mine.dtype)
    for step, piece in zip(range(chips), [mine] + list(moved)):
        found = lax.dynamic_update_index_in_dim(found, piece, chip ^ step, 0)
    (moved,) = yield [(found, "seq", flips(count, 0))]
    low = jnp.where(core == 0, found, moved)
    high = jnp.where(core == 0, moved, found)
    return jnp.stack([low, high], axis=1).astype(jnp.float32).reshape(rows, columns)


def shift_chain(value, axis, steps):
    count = lax.axis_size(axis)
    leading, last = (max(0, -steps), min(count, count - steps))
    (moved,) = yield [(value, axis, [(source, source + steps) for source in range(leading, last)])]
    return moved


def dot(a, b, dims=(((1,), (0,)), ((), ()))):
    return lax.dot_general(a, b, dims, preferred_element_type=jnp.float32)


LAST = (((1,), (1,)), ((), ()))
FIRST = (((0,), (0,)), ((), ()))


def halves(value):
    high = value.astype(jnp.bfloat16)
    return high, (value - high.astype(jnp.float32)).astype(jnp.bfloat16)


def spread_heads(value, expand):
    high, rest = halves(value)
    return dot(high, expand) + dot(rest, expand)


def sum_heads(value, expand):
    high, rest = halves(value)
    return dot(high, expand, LAST) + dot(rest, expand, LAST)


def two_part(state):
    return jnp.concatenate(halves(state), axis=0)


def twice(value):
    value = value.astype(jnp.bfloat16)
    return jnp.concatenate([value, value], axis=1)


def triangle(size, upper):
    row = lax.broadcasted_iota(jnp.int32, (size, size), 0)
    column = lax.broadcasted_iota(jnp.int32, (size, size), 1)
    keep = column >= row if upper else row >= column
    return jnp.where(keep, 1.0, 0.0).astype(jnp.float32)


def exact_dot(a, b):
    return lax.dot_general(
        a, b, (((1,), (0,)), ((), ())), precision=lax.Precision.HIGHEST, preferred_element_type=jnp.float32
    )


def pair_blocks(value):
    lane = lax.broadcasted_iota(jnp.int32, value.shape, 1)
    zero = jnp.zeros_like(value)
    return jnp.concatenate(
        [jnp.where(lane < HDIM, value, zero), jnp.where(lane >= HDIM, value, zero)], axis=0
    )


def conv_rows(extended, taps, bias, rows):
    count = taps.shape[0]
    total = bias
    for tap in range(count):
        begin = 8 - (count - 1) + tap
        total = total + taps[tap : tap + 1] * extended[begin : begin + rows, :]
    return total


def head_terms(dt, timing, damping, seg_column, seg_row):
    value = dt + timing
    step = jnp.maximum(value, 0.0) + jnp.log1p(jnp.exp(-jnp.abs(value)))
    rate = jnp.exp(damping)
    log_decay = -step * rate
    rows = dt.shape[0]
    running = exact_dot(triangle(rows, False), log_decay)
    last = running[rows - 1 : rows]
    seg_last = seg_row[:, rows - 1 : rows]
    entering = jnp.where(seg_column == 0.0, jnp.exp(running), 0.0)
    toward = jnp.where(seg_column == seg_last, jnp.exp(last - running), 0.0)
    return value, step, rate, log_decay, running, entering, toward


def forward_kernel(
    proj, shared, dt, seg_col, seg_row, edge_v, edge_s, taps, offset, filters, baseline, timing, damping, skip, expand,
    full, readers_out, run_out, entry_out, states_out, final_out,
    ext_v, ext_s, state, carried,
):
    rows = dt.shape[0]
    heads = dt.shape[1]

    @pl.when(pl.program_id(0) == 0)
    def start():
        ext_v[0:8, :] = edge_v[...]
        ext_s[0:8, :] = edge_s[...]
        state[...] = jnp.zeros_like(state)
        carried[...] = jnp.ones_like(carried)

    ext_v[8 : 8 + rows, :] = proj[...]
    ext_s[8 : 8 + rows, :] = shared[...]
    pre = conv_rows(ext_v, taps[...], offset[...], rows)
    signal = pre * jax.nn.sigmoid(pre)
    pre_c = conv_rows(ext_s, filters[...], baseline[...], rows)
    control = pre_c * jax.nn.sigmoid(pre_c)
    ext_v[0:8, :] = ext_v[rows : rows + 8, :]
    ext_s[0:8, :] = ext_s[rows : rows + 8, :]
    writers = control[:, :STATE].astype(jnp.bfloat16)
    readers = control[:, STATE:].astype(jnp.bfloat16)
    readers_out[...] = readers
    seg_c, seg_r = seg_col[...], seg_row[0]
    value, step, rate, log_decay, running, entering, toward = head_terms(dt[...], timing[...], damping[...], seg_c, seg_r)
    across = running.T
    row = lax.broadcasted_iota(jnp.int32, (rows, rows), 0)
    column = lax.broadcasted_iota(jnp.int32, (rows, rows), 1)
    bias = jnp.where((seg_c == seg_r) & (row >= column), 0.0, -1e30)
    scores = dot(readers, writers, LAST)
    bias = jnp.concatenate([bias, bias], axis=1)
    scores = jnp.concatenate([scores, scores], axis=1)
    spread = spread_heads(jnp.concatenate([step, entering, toward, entering * carried[...]], axis=0), expand[...])
    step_e, enter_e, toward_e = spread[:rows], spread[rows : 2 * rows], spread[2 * rows : 3 * rows]
    run_out[...] = entering * carried[...]
    weighted = signal * step_e
    low = weighted.astype(jnp.bfloat16)
    old = state[...]
    states_out[0] = old
    carry = dot(twice(readers), two_part(old)) * enter_e + skip[...] * signal
    for pair in range(heads // 2):
        a, b = 2 * pair, 2 * pair + 1
        lanes = slice(pair * 2 * HDIM, (pair + 1) * 2 * HDIM)
        ahead = jnp.concatenate(
            [running[:, a : a + 1] - across[a : a + 1], running[:, b : b + 1] - across[b : b + 1]], axis=1
        )
        mixing = (jnp.exp(ahead + bias) * scores).astype(jnp.bfloat16)
        full[:, lanes] = dot(mixing, pair_blocks(low[:, lanes])) + carry[:, lanes]
    passing = enter_e[rows - 1 : rows]
    new = passing * old + dot(writers, (weighted * toward_e).astype(jnp.bfloat16), FIRST)
    state[...] = new
    entry_out[0] = carried[...]
    through = carried[...] * entering[rows - 1 : rows]
    carried[...] = through

    @pl.when(pl.program_id(0) == pl.num_programs(0) - 1)
    def last():
        final_out[0:STATE, :] = new
        final_out[STATE : STATE + 8, :] = spread_heads(jnp.broadcast_to(through, (8, heads)), expand[...])


def vmem(limit=56):
    return pltpu.CompilerParams(vmem_limit_bytes=limit * 1024 * 1024, dimension_semantics=("arbitrary",))


def whole_spec(array):
    return pl.BlockSpec(array.shape, lambda *index: (0,) * array.ndim)


def forward_scan(proj, shared, dt, seg_col, seg_row, edge_v, edge_s, taps, offset, filters, baseline, timing, damping, skip, expand):
    length, inner = proj.shape
    heads = dt.shape[1]
    blocks = length // SPAN
    rows2 = lambda width: pl.BlockSpec((SPAN, width), lambda c: (c, 0))
    fixed = (edge_v, edge_s, taps, offset, filters, baseline, timing, damping, skip, expand)
    return pl.pallas_call(
        forward_kernel,
        grid=(blocks,),
        in_specs=[rows2(inner), rows2(2 * STATE), rows2(heads), rows2(1), pl.BlockSpec((1, 1, SPAN), lambda c: (c, 0, 0))]
        + [whole_spec(a) for a in fixed],
        out_specs=[
            rows2(inner), rows2(STATE), rows2(heads),
            pl.BlockSpec((1, 1, heads), lambda c: (c, 0, 0)),
            pl.BlockSpec((1, STATE, inner), lambda c: (c, 0, 0)),
            pl.BlockSpec((STATE + 8, inner), lambda c: (0, 0)),
        ],
        out_shape=[
            jax.ShapeDtypeStruct((length, inner), jnp.float32),
            jax.ShapeDtypeStruct((length, STATE), jnp.bfloat16),
            jax.ShapeDtypeStruct((length, heads), jnp.float32),
            jax.ShapeDtypeStruct((blocks, 1, heads), jnp.float32),
            jax.ShapeDtypeStruct((blocks, STATE, inner), jnp.float32),
            jax.ShapeDtypeStruct((STATE + 8, inner), jnp.float32),
        ],
        scratch_shapes=[
            pltpu.VMEM((SPAN + 8, inner), jnp.float32),
            pltpu.VMEM((SPAN + 8, 2 * STATE), jnp.float32),
            pltpu.VMEM((STATE, inner), jnp.float32),
            pltpu.VMEM((1, heads), jnp.float32),
        ],
        compiler_params=vmem(),
    )(proj, shared, dt, seg_col, seg_row, *fixed)


def join_kernel(local, readers, run, gate_in, incoming, expand, full, squares):
    run_e = spread_heads(run[...], expand[...])
    value = local[...] + run_e * dot(twice(readers[...]), two_part(incoming[...]))
    full[...] = value
    gate = gate_in[...]
    gated = value * gate * jax.nn.sigmoid(gate)
    squares[...] = jnp.sum(gated * gated, axis=1, keepdims=True)


def join_incoming(local, readers, run, gate_in, incoming, expand):
    length, inner = local.shape
    heads = run.shape[1]
    rows2 = lambda width: pl.BlockSpec((BLOCK, width), lambda c: (c, 0))
    return pl.pallas_call(
        join_kernel,
        grid=(length // BLOCK,),
        in_specs=[rows2(inner), rows2(STATE), rows2(heads), rows2(inner), whole_spec(incoming), whole_spec(expand)],
        out_specs=[rows2(inner), rows2(1)],
        out_shape=[jax.ShapeDtypeStruct((length, inner), jnp.float32), jax.ShapeDtypeStruct((length, 1), jnp.float32)],
        compiler_params=vmem(),
    )(local, readers, run, gate_in, incoming, expand)


def norm_cot_kernel(upstream, readout, full, gate_in, inverse, postnorm, norm_cot, normalized, inner_sum, gain_sum):
    @pl.when(pl.program_id(0) == 0)
    def start():
        gain_sum[...] = jnp.zeros_like(gain_sum)

    cot = dot(upstream[...], readout[...])
    norm_cot[...] = cot
    gate = gate_in[...]
    unit = full[...] * gate * jax.nn.sigmoid(gate) * inverse[...]
    normalized[...] = (unit * postnorm[...]).astype(jnp.bfloat16)
    product = cot * unit
    gain_sum[...] += jnp.sum(product.reshape(-1, 8, product.shape[1]), axis=0)
    inner_sum[...] = jnp.sum(product * postnorm[...], axis=1, keepdims=True)


def norm_cotangent(upstream, readout, full, gate_in, inverse, postnorm):
    length, inner = full.shape
    rows2 = lambda width: pl.BlockSpec((BLOCK, width), lambda c: (c, 0))
    return pl.pallas_call(
        norm_cot_kernel,
        grid=(length // BLOCK,),
        in_specs=[rows2(upstream.shape[1]), whole_spec(readout), rows2(inner), rows2(inner), rows2(1), whole_spec(postnorm)],
        out_specs=[rows2(inner), rows2(inner), rows2(1), pl.BlockSpec((8, inner), lambda c: (0, 0))],
        out_shape=[
            jax.ShapeDtypeStruct((length, inner), jnp.float32),
            jax.ShapeDtypeStruct((length, inner), jnp.bfloat16),
            jax.ShapeDtypeStruct((length, 1), jnp.float32),
            jax.ShapeDtypeStruct((8, inner), jnp.float32),
        ],
        compiler_params=vmem(),
    )(upstream, readout, full, gate_in, inverse, postnorm)


def gate_kernel(norm_cot, full_in, gate_in, inverse, mean, postnorm, run, readers, expand, final, full_cot, gate_low, pending):
    @pl.when(pl.program_id(0) == 0)
    def start():
        pending[0:STATE, :] = jnp.zeros((STATE, pending.shape[1]), jnp.float32)
        pending[STATE : STATE + 8, :] = final[STATE : STATE + 8, :]

    gate, full = gate_in[...], full_in[...]
    sigmoid = jax.nn.sigmoid(gate)
    active = gate * sigmoid
    scaled = inverse[...]
    unit = full * active * scaled
    gated_cot = scaled * (norm_cot[...] * postnorm[...] - unit * mean[...])
    cot = gated_cot * active
    full_cot[...] = cot
    gate_low[...] = (gated_cot * full * sigmoid * (1.0 + gate * (1.0 - sigmoid))).astype(jnp.bfloat16)
    run_e = spread_heads(run[...], expand[...])
    pending[0:STATE, :] += dot(readers[...], (cot * run_e).astype(jnp.bfloat16), FIRST)


def gate_cotangent(norm_cot, full, gate_in, inverse, mean, postnorm, run, readers, expand, final):
    length, inner = full.shape
    heads = run.shape[1]
    rows2 = lambda width: pl.BlockSpec((BLOCK, width), lambda c: (c, 0))
    return pl.pallas_call(
        gate_kernel,
        grid=(length // BLOCK,),
        in_specs=[rows2(inner), rows2(inner), rows2(inner), rows2(1), rows2(1), whole_spec(postnorm), rows2(heads), rows2(STATE), whole_spec(expand), whole_spec(final)],
        out_specs=[rows2(inner), rows2(inner), pl.BlockSpec((STATE + 8, inner), lambda c: (0, 0))],
        out_shape=[
            jax.ShapeDtypeStruct((length, inner), jnp.float32),
            jax.ShapeDtypeStruct((length, inner), jnp.bfloat16),
            jax.ShapeDtypeStruct((STATE + 8, inner), jnp.float32),
        ],
        compiler_params=vmem(),
    )(norm_cot, full, gate_in, inverse, mean, postnorm, run, readers, expand, final)


def silu_slope(pre, sigmoid):
    return sigmoid * (1.0 + pre * (1.0 - sigmoid))


def fold(value):
    return jnp.sum(value.reshape(-1, 8, value.shape[1]), axis=0)


def taps_back(pre_cot, taps, following, rows):
    count = taps.shape[0]
    total = taps[count - 1 : count] * pre_cot
    for tap in range(count - 1):
        later = count - 1 - tap
        total = total + taps[tap : tap + 1] * following[later : later + rows, :]
    return total


def backward_kernel(
    opening,
    proj, shared, before_v, before_s, dt, seg_col, seg_row, full_cot, states, entry,
    edge_v, edge_s, taps, offset, filters, baseline, timing, damping, skip, expand, incoming, leaving, after_v, after_s, sums_in,
    values_low, shared_low, dt_low, sums_out, head_v, head_s, lam_out,
    ext_v, ext_s, later_v, later_s, lam, tap_sum, offset_sum, filter_sum, base_sum, timing_sum, damping_sum, direct_sum,
):
    rows, heads = dt.shape
    step_index = pl.program_id(0)
    blocks = pl.num_programs(0)

    @pl.when(step_index == 0)
    def start():
        lam[...] = leaving[...]
        later_v[rows : rows + 8, :] = after_v[...]
        later_s[rows : rows + 8, :] = after_s[...]
        for item in (tap_sum, offset_sum, filter_sum, base_sum, timing_sum, damping_sum, direct_sum):
            item[...] = jnp.zeros_like(item)

    ext_v[0:8, :] = before_v[...]
    ext_s[0:8, :] = before_s[...]
    if opening:

        @pl.when(step_index == blocks - 1)
        def first_block():
            ext_v[0:8, :] = edge_v[...]
            ext_s[0:8, :] = edge_s[...]

    ext_v[8 : 8 + rows, :] = proj[...]
    ext_s[8 : 8 + rows, :] = shared[...]
    pre = conv_rows(ext_v, taps[...], offset[...], rows)
    sigmoid = jax.nn.sigmoid(pre)
    signal = pre * sigmoid
    pre_c = conv_rows(ext_s, filters[...], baseline[...], rows)
    sigmoid_c = jax.nn.sigmoid(pre_c)
    control = pre_c * sigmoid_c
    writers = control[:, :STATE].astype(jnp.bfloat16)
    readers = control[:, STATE:].astype(jnp.bfloat16)
    seg_c, seg_r = seg_col[...], seg_row[0]
    value, step, rate, log_decay, running, entering, toward = head_terms(dt[...], timing[...], damping[...], seg_c, seg_r)
    across = running.T
    row = lax.broadcasted_iota(jnp.int32, (rows, rows), 0)
    column = lax.broadcasted_iota(jnp.int32, (rows, rows), 1)
    bias = jnp.where((seg_c == seg_r) & (column >= row), 0.0, -1e30)
    scores = dot(writers, readers, LAST)
    bias = jnp.concatenate([bias, bias], axis=1)
    scores = jnp.concatenate([scores, scores], axis=1)
    one_hot = expand[...]
    spread = spread_heads(jnp.concatenate([step, entering, toward], axis=0), one_hot)
    step_e, enter_e, toward_e = spread[:rows], spread[rows : 2 * rows], spread[2 * rows : 3 * rows]
    cot = full_cot[...]
    cot_low = cot.astype(jnp.bfloat16)
    weighted = signal * step_e
    low = weighted.astype(jnp.bfloat16)
    after = lam[...]
    after_parts = two_part(after)
    from_state = dot(twice(writers), after_parts) * toward_e
    entry_e = spread_heads(jnp.broadcast_to(entry[0], (8, heads)), one_hot)
    old = states[0] + entry_e[0:1] * incoming[...]
    old_parts = two_part(old)
    cot_entering = cot * enter_e
    cot_entering_low = cot_entering.astype(jnp.bfloat16)
    score_cot = jnp.zeros((rows, rows), jnp.float32)
    row_sums = jnp.zeros((rows, heads), jnp.float32)
    column_sums = []
    ones = jnp.ones((8, rows), jnp.bfloat16)
    place = lax.broadcasted_iota(jnp.int32, (2 * rows, heads), 0) // rows
    head_place = lax.broadcasted_iota(jnp.int32, (2 * rows, heads), 1)
    direct_part = []
    step_part = []
    for pair in range(heads // 2):
        a, b = 2 * pair, 2 * pair + 1
        lanes = slice(pair * 2 * HDIM, (pair + 1) * 2 * HDIM)
        ahead = jnp.concatenate(
            [across[a : a + 1] - running[:, a : a + 1], across[b : b + 1] - running[:, b : b + 1]], axis=1
        )
        decays = jnp.exp(ahead + bias)
        mixing = decays * scores
        blocked = pair_blocks(cot_low[:, lanes])
        weighted_cot = dot(mixing.astype(jnp.bfloat16), blocked) + from_state[:, lanes]
        step_part.append(weighted_cot * signal[:, lanes])
        later_v[0:rows, lanes] = weighted_cot * step_e[:, lanes] + skip[:, lanes] * cot[:, lanes]
        inner = dot(low[:, lanes], blocked, LAST)
        linked = inner * decays
        score_cot = score_cot + linked[:, :rows] + linked[:, rows:]
        energy = (inner * mixing).astype(jnp.bfloat16)
        chosen = jnp.where(head_place == place + a, 1.0, 0.0).astype(jnp.bfloat16)
        row_sums = row_sums + dot(energy, chosen)
        column_sums.append(dot(ones, energy))
    step_cot = sum_heads(jnp.concatenate(step_part, axis=1), one_hot)
    sums_across = jnp.concatenate(
        [piece for pair in column_sums for piece in (pair[0:1, :rows], pair[0:1, rows:])], axis=0
    )
    state_term = weighted * from_state
    enter_term = cot_entering * dot(twice(readers), old_parts)
    passing = enter_e[rows - 1 : rows]
    last_term = fold(state_term) + fold(after * old * passing)
    running_cot = sums_across.T - row_sums + sum_heads(enter_term - state_term, one_hot)
    last_cot = jnp.sum(sum_heads(last_term, one_hot), axis=0, keepdims=True)
    decay_cot = exact_dot(triangle(rows, True), running_cot) + last_cot
    step_cot = step_cot - decay_cot * rate
    dt_cot = step_cot * jax.nn.sigmoid(value)
    dt_low[...] = dt_cot.astype(jnp.bfloat16)
    timing_sum[...] += fold(dt_cot)
    damping_sum[...] += fold(decay_cot * log_decay)
    direct_sum[...] += fold(cot * signal)
    score_low = score_cot.astype(jnp.bfloat16)
    reader_cot = dot(score_low, writers, FIRST) + dot(
        jnp.concatenate([cot_entering_low, cot_entering_low], axis=1), jnp.concatenate(halves(old), axis=1), LAST
    )
    push = (weighted * toward_e).astype(jnp.bfloat16)
    writer_cot = dot(score_low, readers) + dot(
        jnp.concatenate([push, push], axis=1), jnp.concatenate(halves(after), axis=1), LAST
    )
    lam[...] = passing * after + dot(readers, cot_entering_low, FIRST)

    pre_cot = later_v[0:rows, :] * silu_slope(pre, sigmoid)
    later_v[0:rows, :] = pre_cot
    pre_cot_c = jnp.concatenate([writer_cot, reader_cot], axis=1) * silu_slope(pre_c, sigmoid_c)
    later_s[0:rows, :] = pre_cot_c
    values_cot = taps_back(pre_cot, taps[...], later_v, rows)
    shared_cot = taps_back(pre_cot_c, filters[...], later_s, rows)
    values_low[...] = values_cot.astype(jnp.bfloat16)
    shared_low[...] = shared_cot.astype(jnp.bfloat16)
    count = taps.shape[0]
    for tap in range(count):
        begin = 8 - (count - 1) + tap
        tap_sum[tap] += fold(pre_cot * ext_v[begin : begin + rows, :])
        filter_sum[tap] += fold(pre_cot_c * ext_s[begin : begin + rows, :])
    offset_sum[...] += fold(pre_cot)
    base_sum[...] += fold(pre_cot_c)
    later_v[rows : rows + 8, :] = later_v[0:8, :]
    later_s[rows : rows + 8, :] = later_s[0:8, :]

    @pl.when(step_index == blocks - 1)
    def head():
        head_v[...] = pre_cot[0:8, :]
        head_s[...] = pre_cot_c[0:8, :]
        lam_out[...] = lam[...]
        sums_out[...] = sums_in[...]
        total = lambda value: jnp.sum(value, axis=0, keepdims=True)
        for tap in range(count):
            sums_out[tap : tap + 1, :] += total(tap_sum[tap])
            sums_out[count + 2 + tap : count + 3 + tap, : 2 * STATE] += total(filter_sum[tap])
        sums_out[count : count + 1, :] += total(offset_sum[...])
        sums_out[count + 1 : count + 2, :] += total(direct_sum[...])
        sums_out[2 * count + 2 : 2 * count + 3, : 2 * STATE] += total(base_sum[...])
        sums_out[2 * count + 3 : 2 * count + 4, :heads] += total(timing_sum[...])
        sums_out[2 * count + 4 : 2 * count + 5, :heads] += total(damping_sum[...])


def backward_scan(
    proj, shared, dt, seg_col, seg_row, full_cot, states, entry,
    edge_v, edge_s, taps, offset, filters, baseline, timing, damping, skip, expand, incoming, leaving, after_v, after_s, sums, base, blocks,
):
    inner = proj.shape[1]
    length = blocks * SPAN
    heads = dt.shape[1]
    count = taps.shape[0]
    back = lambda c: base + blocks - 1 - c
    own = lambda width: pl.BlockSpec((SPAN, width), lambda c: (blocks - 1 - c, 0))
    rows2 = lambda width: pl.BlockSpec((SPAN, width), lambda c: (back(c), 0))
    before = lambda width: pl.BlockSpec((8, width), lambda c: (jnp.maximum(back(c) * (SPAN // 8) - 1, 0), 0))
    lead = lambda *shape: pl.BlockSpec((1,) + shape, lambda c: (back(c), 0, 0))
    fixed = (edge_v, edge_s, taps, offset, filters, baseline, timing, damping, skip, expand, incoming, leaving, after_v, after_s, sums)
    f32 = lambda *shape: jax.ShapeDtypeStruct(shape, jnp.float32)
    carried = [f32(*sums.shape), f32(8, inner), f32(8, 2 * STATE), f32(STATE, inner)]
    low = lambda width: jax.ShapeDtypeStruct((length, width), jnp.bfloat16)
    return pl.pallas_call(
        functools.partial(backward_kernel, base == 0),
        grid=(blocks,),
        in_specs=[rows2(inner), rows2(2 * STATE), before(inner), before(2 * STATE), rows2(heads), rows2(1), lead(1, SPAN), rows2(inner), lead(STATE, inner), lead(1, heads)]
        + [whole_spec(a) for a in fixed],
        out_specs=[own(inner), own(2 * STATE), own(heads)] + [whole_spec(a) for a in carried],
        out_shape=[low(inner), low(2 * STATE), low(heads)] + carried,
        scratch_shapes=[
            pltpu.VMEM((SPAN + 8, inner), jnp.float32),
            pltpu.VMEM((SPAN + 8, 2 * STATE), jnp.float32),
            pltpu.VMEM((SPAN + 8, inner), jnp.float32),
            pltpu.VMEM((SPAN + 8, 2 * STATE), jnp.float32),
            pltpu.VMEM((STATE, inner), jnp.float32),
            pltpu.VMEM((count, 8, inner), jnp.float32),
            pltpu.VMEM((8, inner), jnp.float32),
            pltpu.VMEM((count, 8, 2 * STATE), jnp.float32),
            pltpu.VMEM((8, 2 * STATE), jnp.float32),
            pltpu.VMEM((8, heads), jnp.float32),
            pltpu.VMEM((8, heads), jnp.float32),
            pltpu.VMEM((8, inner), jnp.float32),
        ],
        compiler_params=vmem(),
    )(proj, shared, proj, shared, dt, seg_col, seg_row, full_cot, states, entry, *fixed)


def normed_cot_kernel(gate_low, values_low, shared_low, dt_low, gating, values, control, timestep, tokens, scale, gain, low, row_sum, gain_sum):
    total = dot(gate_low[...], gating[...]) + dot(values_low[...], values[...])
    total = total + dot(shared_low[...], control[...]) + dot(dt_low[...], timestep[...])
    low[...] = total.astype(jnp.bfloat16)
    product = total * (tokens[...].astype(jnp.float32) * scale[...])
    gain_sum[...] = fold(product)

    @pl.when(pl.program_id(0) == 0)
    def start():
        row_sum[...] = jnp.zeros_like(row_sum)

    row_sum[...] += jnp.sum(product * gain[...], axis=1, keepdims=True)


def normed_cotangent(gate_low, values_low, shared_low, dt_low, gating, values, control, timestep, tokens, scale, gain, base):
    length = values_low.shape[0]
    width = gating.shape[1]
    tile = 512
    here = base // length
    fixed = lambda array: pl.BlockSpec((length, array.shape[1]), lambda c: (0, 0))
    late = lambda size: pl.BlockSpec((length, size), lambda c: (here, 0))
    columns = lambda rows: pl.BlockSpec((rows, tile), lambda c: (0, c))
    parts = (gate_low, values_low, shared_low, dt_low)
    weights = (gating, values, control, timestep)
    return pl.pallas_call(
        normed_cot_kernel,
        grid=(width // tile,),
        in_specs=[late(gate_low.shape[1])] + [fixed(a) for a in parts[1:]] + [columns(a.shape[0]) for a in weights]
        + [pl.BlockSpec((length, tile), lambda c: (here, c)), late(1), columns(1)],
        out_specs=[columns(length), pl.BlockSpec((length, 1), lambda c: (0, 0)), columns(8)],
        out_shape=[
            jax.ShapeDtypeStruct((length, width), jnp.bfloat16),
            jax.ShapeDtypeStruct((length, 1), jnp.float32),
            jax.ShapeDtypeStruct((8, width), jnp.float32),
        ],
        compiler_params=vmem(),
    )(*parts, *weights, tokens, scale, gain)


def small_call(kernel, shape, scratch, place, *arrays):
    return pl.pallas_call(
        kernel,
        in_specs=[pl.BlockSpec(memory_space=pltpu.SMEM)] + [pl.BlockSpec(memory_space=pltpu.VMEM)] * len(arrays),
        out_specs=pl.BlockSpec(memory_space=pltpu.VMEM),
        out_shape=jax.ShapeDtypeStruct(shape, jnp.float32),
        scratch_shapes=scratch,
        compiler_params=pltpu.CompilerParams(vmem_limit_bytes=32 * 1024 * 1024),
    )(place.reshape(1), *arrays)


def chip_state(mine, other, core, reverse):
    half = mine.shape[1] // 2

    def kernel(core, mine, other, out):
        index = core[0]
        first = (index == 1) if reverse else (index == 0)
        lanes = pl.ds(pl.multiple_of(index * half, 128), half)
        a, b = mine[:, lanes], other[:, lanes]
        early, late = jnp.where(first, a, b), jnp.where(first, b, a)
        out[0:STATE, :] = late[STATE : STATE + 1] * early[0:STATE] + late[0:STATE]
        out[STATE : STATE + 8, :] = late[STATE : STATE + 8] * early[STATE : STATE + 8]

    return small_call(kernel, (STATE + 8, half), [], core, mine, other)


def entering_state(chip, chips, reverse, parts):
    shape = parts[0].shape

    def kernel(chip, *refs):
        ins, out, held = refs[: len(parts)], refs[len(parts)], refs[len(parts) + 1]
        for step, ref in enumerate(ins):
            held[step + 1] = ref[...]
        here = chip[0]
        out[...] = jnp.zeros_like(out)

        def add(turn, carry):
            source = chips - 1 - turn if reverse else turn
            step = source ^ here
            out[...] = held[step, STATE : STATE + 1, :] * out[...] + held[step, 0:STATE, :]
            return carry

        lax.fori_loop(0, chips - 1 - here if reverse else here, add, 0)

    return small_call(kernel, (STATE, shape[1]), [pltpu.VMEM((chips,) + shape, jnp.float32)], chip, *parts)


def core_state(mine, other, neighbour, core, reverse):
    half = mine.shape[1]

    def kernel(core, mine, other, neighbour, out):
        low = core[0] == 0
        after = low if reverse else jnp.logical_not(low)
        for side, value in enumerate((jnp.where(low, mine[...], other[...]), jnp.where(low, other[...], mine[...]))):
            lanes = slice(side * half, (side + 1) * half)
            passed = neighbour[STATE : STATE + 1, lanes] * value + neighbour[0:STATE, lanes]
            out[:, lanes] = jnp.where(after, passed, value)

    return small_call(kernel, (STATE, 2 * half), [], core, mine, other, neighbour)


def shards(
    tokens,
    prenorm,
    gating,
    values,
    control,
    timestep,
    kernel,
    offset,
    filters,
    baseline,
    timing,
    damping,
    direct,
    postnorm,
    readout,
    doc_starts,
    cotangent,
):
    length, share = tokens.shape
    inner = kernel.shape[1]
    heads = timing.shape[0]
    ranks = lax.axis_size("head")
    features = share * ranks
    channels = inner * ranks
    blocks = length // SPAN
    half = length // 2
    f32, bf16 = jnp.float32, jnp.bfloat16

    starts = doc_starts.reshape(blocks, SPAN).astype(bf16)
    place = jnp.arange(SPAN)
    counted = jnp.dot(starts, (place[:, None] <= place[None, :]).astype(bf16), preferred_element_type=f32)
    seg_row, seg_col = counted.reshape(blocks, 1, SPAN), counted.reshape(length, 1)
    expand = (jnp.arange(heads)[:, None] == jnp.arange(inner)[None, :] // HDIM).astype(bf16)
    skip = jnp.repeat(direct, HDIM)[None]
    offset_row, baseline_row, postnorm_row = offset[None], baseline[None], postnorm[None]
    timing_row, damping_row = timing[None], damping[None]

    gains = Chain(all_chain(prenorm, "head"))
    tokens_in = Chain(gather_chain(tokens, "head"))
    weights_back = phase([tokens_in, gains], lambda *a: tuple(w.T for w in a), gating, values, control, timestep, readout)
    readout_t = weights_back[4]
    finish(tokens_in, gains)
    cot_ready, found, gain_blocks = lax.optimization_barrier((cotangent, tokens_in.result, gains.result))
    upstream = lax.all_gather(cot_ready, "head", axis=1, tiled=True)
    gain = gain_blocks.reshape(1, features).astype(f32)

    def project(*found):
        gathered = place_columns(found, "head")
        wide = gathered.astype(f32)
        scale = lax.rsqrt(jnp.mean(wide * wide, axis=1, keepdims=True) + epsilon)
        normed = (wide * scale * gain).astype(bf16)
        projected = jnp.dot(normed, values, preferred_element_type=f32)
        shared = jnp.dot(normed, control, preferred_element_type=f32)
        timestep_in = jnp.dot(normed, timestep, preferred_element_type=f32)
        return gathered, scale, normed, projected, shared, timestep_in

    gathered, scale, normed, projected, shared, timestep_in = phase([], project, *found)
    edges = Chain(shift_chain(
        jnp.concatenate([projected[length - 8 :], shared[length - 8 :], gathered[length - 8 :].astype(f32)], axis=1), "seq", 1
    ))
    gate_in = phase([edges], lambda n: jnp.dot(n, gating, preferred_element_type=f32), normed)
    edge_v, edge_s = edges.result[:, :inner], edges.result[:, inner : inner + 2 * STATE]
    before = edges.result[:, inner + 2 * STATE :]
    before = jnp.pad(before, ((0, 8), (0, 0)))
    before_scale = lax.rsqrt(jnp.mean(before * before, axis=1, keepdims=True) + epsilon)
    normed_more = jnp.concatenate([normed, (before * before_scale * gain).astype(bf16)], axis=0)
    params = (kernel, offset_row, filters, baseline_row, timing_row, damping_row, skip, expand)
    local, readers, run, entry, states, final = phase(
        [], lambda *a: forward_scan(*a, *params), projected, shared, timestep_in, seg_col, seg_row, edge_v, edge_s
    )
    prefix = Chain(state_chain(final, False))
    finish(prefix)
    incoming = prefix.result
    full, squares = join_incoming(local, readers, run, gate_in, incoming, expand)
    squared = Chain(sum_chain(squares.reshape(length), "head"))
    finish(squared)
    inverse = lax.rsqrt(squared.result / channels + epsilon)[:, None]
    norm_cot, normalized, inner_sum, postnorm_sum = norm_cotangent(
        upstream, readout, full, gate_in, inverse, postnorm_row
    )
    means = Chain(sum_chain(inner_sum.reshape(length), "head"))
    partial_rows = phase(
        [means], lambda n: jnp.dot(n, readout_t, preferred_element_type=f32).astype(bf16), normalized
    )
    branch = lax.psum_scatter(partial_rows, "head", scatter_dimension=1, tiled=True)
    mean = means.result[:, None] / channels
    full_cot, gate_low, pending = gate_cotangent(
        norm_cot, full, gate_in, inverse, mean, postnorm_row, run, readers, expand, final
    )
    suffix = Chain(state_chain(pending, True))
    phase([suffix])
    readout_local, gating_local = phase(
        [suffix],
        lambda u, n, m, g: (
            lax.dot_general(u, n, FIRST, preferred_element_type=f32).astype(bf16),
            lax.dot_general(m, g, FIRST, preferred_element_type=f32).astype(bf16),
        ),
        upstream, normalized, normed, gate_low,
    )
    readout_sum = lax.psum_scatter(readout_local, "seq", scatter_dimension=0, tiled=True)
    gating_sum = lax.psum_scatter(gating_local, "seq", scatter_dimension=0, tiled=True)
    finish(suffix)
    leaving = suffix.result

    def backward(base, size, leaving, after_v, after_s, sums):
        return backward_scan(
            projected, shared, timestep_in, seg_col, seg_row, full_cot, states, entry,
            edge_v, edge_s, *params, incoming, leaving, after_v, after_s, sums, base, size,
        )

    def normed_back(base, *lows):
        return normed_cotangent(gate_low, *lows, *weights_back[:4], gathered, scale, gain, base)

    zeros_v, zeros_s = jnp.zeros((8, inner), f32), jnp.zeros((8, 2 * STATE), f32)
    taps = kernel.shape[0]
    sums = jnp.zeros((2 * taps + 5, inner), f32)
    late = backward(blocks // 2, blocks // 2, leaving, zeros_v, zeros_s, sums)
    normed_late = normed_back(half, *late[:3])
    total_late = Chain(scatter_chain(normed_late[0], "head"))
    middle = phase(
        [total_late], lambda *a: backward(blocks // 4, blocks // 4, *a), late[6], late[4], late[5], late[3]
    )
    branch, middle = lax.optimization_barrier((branch, middle))
    normed_middle, early = phase(
        [total_late],
        lambda lam, head_v, head_s, sums, *lows: (
            normed_back(half // 2, *lows), backward(0, blocks // 4, lam, head_v, head_s, sums)
        ),
        middle[6], middle[4], middle[5], middle[3], *middle[:3],
    )

    def share_before(head, taps_of):
        following = jnp.concatenate([jnp.zeros_like(head), head], axis=0)
        return sum(taps_of[tap][None] * following[taps - 1 - tap : taps + 7 - tap] for tap in range(taps))

    more_v, more_s = share_before(early[4], kernel), share_before(early[5], filters)

    more_v, more_s = [jnp.pad(more.astype(bf16), ((0, 8), (0, 0))) for more in (more_v, more_s)]
    more_dt = jnp.zeros((16, heads), bf16)
    shared_low = jnp.concatenate([early[1], middle[1], late[1], more_s], axis=0)
    control_local = lax.dot_general(normed_more, shared_low, FIRST, preferred_element_type=f32)
    first = length // 4
    normed_early = normed_cotangent(
        jnp.concatenate([gate_low[:first], jnp.zeros((16, inner), bf16)], axis=0),
        jnp.concatenate([early[0], more_v], axis=0),
        jnp.concatenate([early[1], more_s], axis=0),
        jnp.concatenate([early[2], more_dt], axis=0),
        *weights_back[:4],
        jnp.concatenate([gathered[:first], before.astype(bf16)], axis=0),
        jnp.concatenate([scale[:first], before_scale], axis=0), gain, 0,
    )
    finish(total_late)
    total_early = Chain(
        scatter_chain(jnp.concatenate([normed_early[0], normed_middle[0]], axis=0), "head", 2)
    )
    prenorm_sum = (normed_early[2] + normed_middle[2] + normed_late[2]).sum(0).reshape(-1, inner)
    flat = jnp.concatenate([early[3], postnorm_sum.sum(0)[None], prenorm_sum], axis=0)
    flat_rows = flat.shape[0]
    flat = jnp.pad(flat, ((0, -flat_rows % 32), (0, 0))).reshape(-1, 2 * STATE)
    holder = []
    shared_sum = Chain(shared_chain(control_local, flat, holder))
    row_sum = jnp.concatenate(
        [normed_early[1][:first], normed_middle[1], normed_late[1], normed_early[1][first : first + 8]], axis=0
    ).reshape(length + 8)
    rows_of = Chain(sum_chain(row_sum, "head"))

    def weights_of(*lows):
        lows = [jnp.concatenate(group, axis=0) for group in (lows[:4], lows[4:])]
        low = jnp.concatenate([lows[0], jnp.pad(lows[1], ((0, 0), (0, 128 - heads)))], axis=1)
        return lax.dot_general(normed_more, low, FIRST, preferred_element_type=f32).astype(bf16)

    values_local = phase(
        [shared_sum, total_early],
        weights_of, early[0], middle[0], late[0], more_v, early[2], middle[2], late[2], more_dt,
    )
    values_sum = lax.psum_scatter(values_local, "seq", scatter_dimension=0, tiled=True)
    mixed = phase(
        [shared_sum, total_early], lambda t, s: (t.astype(f32) + s.astype(f32)).astype(bf16), tokens, branch
    )
    phase([shared_sum, rows_of])
    readout_sum, gating_sum = phase([shared_sum, total_early], lambda *a: a, readout_sum, gating_sum)
    finish(total_early, rows_of, total_late)
    (copies,) = holder
    scattered = total_early.result
    extra = jnp.concatenate([scattered[first : first + 8], jnp.broadcast_to(rows_of.result[length:, None], (8, share))], axis=0)
    from_next = Chain(shift_chain(extra, "seq", -1))

    def closing(row_sum, early_total, late_total, copies):
        own_total = jnp.concatenate([early_total[:first], early_total[first + 16 :], late_total], axis=0)
        own_units = tokens.astype(f32) * scale
        tokens_gradient = cotangent.astype(f32) + scale * (
            own_total * prenorm.astype(f32) - own_units * (row_sum[:length, None] / features)
        )
        by_head = copies.reshape(ranks, -1, inner)[:, :flat_rows].transpose(1, 0, 2)
        rows = by_head.reshape(flat_rows, channels)
        alike = by_head[:, 0]
        for rank in range(1, ranks):
            alike = alike + by_head[:, rank]
        return (
            tokens_gradient,
            rows[:taps],
            rows[taps],
            alike[taps + 2 : 2 * taps + 2, : 2 * STATE],
            alike[2 * taps + 2, : 2 * STATE],
            by_head[2 * taps + 3, :, :heads].reshape(-1),
            by_head[2 * taps + 4, :, :heads].reshape(-1),
            rows[taps + 1].reshape(ranks * heads, HDIM).sum(1),
            rows[2 * taps + 5],
            alike[2 * taps + 6 :].reshape(-1),
        )

    (
        tokens_gradient, kernel_gradient, offset_gradient, filters_gradient, baseline_gradient, timing_gradient,
        damping_gradient, direct_gradient, postnorm_gradient, prenorm_gradient,
    ) = phase([shared_sum, from_next], closing, rows_of.result, scattered, total_late.result, copies)
    finish(shared_sum, from_next)
    more_rows, more_sums = from_next.result[:8], from_next.result[8:, :1] / features
    last = scale[length - 8 :] * (
        more_rows * prenorm.astype(f32) - tokens[length - 8 :].astype(f32) * scale[length - 8 :] * more_sums
    )
    tokens_gradient = tokens_gradient.at[length - 8 :].add(last)
    return (
        mixed,
        tokens_gradient,
        prenorm_gradient,
        gating_sum.astype(f32),
        values_sum[:, :inner].astype(f32),
        shared_sum.result,
        values_sum[:, inner : inner + heads].astype(f32),
        kernel_gradient,
        offset_gradient,
        filters_gradient,
        baseline_gradient,
        timing_gradient,
        damping_gradient,
        direct_gradient,
        postnorm_gradient,
        readout_sum.astype(f32),
    )


def solution(mesh):
    return jax.shard_map(
        shards,
        mesh=mesh,
        in_specs=(
            P("seq", "head"),
            P("head"),
            P(None, "head"),
            P(None, "head"),
            P(),
            P(None, "head"),
            P(None, "head"),
            P("head"),
            P(),
            P(),
            P("head"),
            P("head"),
            P("head"),
            P("head"),
            P(None, "head"),
            P("seq"),
            P("seq", "head"),
        ),
        out_specs=(
            P("seq", "head"),
            P("seq", "head"),
            P(),
            P("seq", "head"),
            P("seq", "head"),
            P(),
            P("seq", "head"),
            P(),
            P(),
            P(),
            P(),
            P(),
            P(),
            P(),
            P(),
            P("seq", "head"),
        ),
        check_vma=False,
    )
```

```python
import functools

import jax
import jax.numpy as jnp
from jax import lax
from jax.experimental import pallas as pl
from jax.experimental.pallas import tpu as pltpu
from jax.sharding import PartitionSpec as P

HDIM = 64
STATE = 128
SPAN = 128
BLOCK = 256


epsilon = 1e-05


def rotation(count, steps):
    return [(source, (source + steps) % count) for source in range(count)]


def flips(count, bit):
    return [(source, source ^ (1 << bit)) for source in range(count)]


def bits_of(count):
    return count.bit_length() - 1


class Chain:
    def __init__(self, gen):
        self.gen = gen
        self.result = None
        self.sends = None
        self.step(None)

    def step(self, moved):
        try:
            self.sends = self.gen.send(moved)
        except StopIteration as stop:
            self.sends, self.result = None, stop.value


def phase(chains, work=None, *inputs):
    chains = [chain for chain in chains if chain.sends is not None]
    values = [[send[0] for send in chain.sends] for chain in chains]
    values, inputs = lax.optimization_barrier((values, inputs))
    moved = [
        [lax.ppermute(value, send[1], send[2]) for value, send in zip(group, chain.sends)]
        for group, chain in zip(values, chains)
    ]
    outs = work(*inputs) if work is not None else ()
    moved, outs = lax.optimization_barrier((moved, outs))
    for chain, group in zip(chains, moved):
        chain.step(group)
    return outs


def finish(*chains):
    while any(chain.sends is not None for chain in chains):
        phase(chains)
    return [chain.result for chain in chains]


def gather_chain(block, axis):
    count = lax.axis_size(axis)
    half = count // 2
    rows = block.shape[0] // 2
    found = [None] * count
    found[0] = block
    left = right = block
    for step in range(1, half):
        left, right = yield [(left, axis, rotation(count, 1)), (right, axis, rotation(count, -1))]
        found[count - step] = left
        found[step] = right
    low, high = yield [(left[:rows], axis, rotation(count, 1)), (right[rows:], axis, rotation(count, -1))]
    found[half] = jnp.concatenate([low, high], axis=0)
    return found


def place_columns(found, axis):
    count = len(found)
    me = lax.axis_index(axis)
    width = found[0].shape[1]
    whole = jnp.zeros((found[0].shape[0], count * width), found[0].dtype)
    for step, piece in enumerate(found):
        whole = lax.dynamic_update_slice_in_dim(whole, piece, (me + step) % count * width, 1)
    return whole


def scatter_chain(wholes, axis, pieces=1):
    count = lax.axis_size(axis)
    me = lax.axis_index(axis)
    half = count // 2
    rows = sum(whole.shape[1] for whole in wholes) // 2

    def part(step):
        found = [lax.dynamic_index_in_dim(whole, (me + step) % count, 0, False) for whole in wholes]
        return found[0] if len(found) == 1 else jnp.concatenate(found, axis=0)

    far = part(half)
    ahead, behind = yield [(far[:rows], axis, rotation(count, 1)), (far[rows:], axis, rotation(count, -1))]
    for step in range(half - 1, 0, -1):
        up = part(step).astype(jnp.float32)
        down = part(count - step).astype(jnp.float32)
        if step == half - 1:
            up = up.at[:rows].add(ahead.astype(jnp.float32))
            down = down.at[rows:].add(behind.astype(jnp.float32))
        else:
            up = up + ahead.astype(jnp.float32)
            down = down + behind.astype(jnp.float32)
        arrived = []
        cuts = [2 * rows * cut // (16 * pieces) * 16 for cut in range(pieces + 1)]
        for begin, end in zip(cuts, cuts[1:]):
            arrived.append(
                (yield [
                    (up[begin:end].astype(jnp.bfloat16), axis, rotation(count, 1)),
                    (down[begin:end].astype(jnp.bfloat16), axis, rotation(count, -1)),
                ])
            )
        ahead, behind = [jnp.concatenate(side, axis=0) if pieces > 1 else side[0] for side in zip(*arrived)]
    return part(0).astype(jnp.float32) + ahead.astype(jnp.float32) + behind.astype(jnp.float32)


def sum_chain(value, axis):
    count = lax.axis_size(axis)
    moved = yield [(value, axis, rotation(count, step)) for step in range(1, count)]
    for other in moved:
        value = value + other
    return value


def split_half(value, axis, bit, position):
    mine = (lax.axis_index(axis) >> bit) & 1
    kept = lax.dynamic_index_in_dim(value, mine, position, False)
    sent = lax.dynamic_index_in_dim(value, 1 - mine, position, False)
    return kept, (sent, axis, flips(lax.axis_size(axis), bit))


def rows_chain(value, axis):
    count = lax.axis_size(axis)
    bits = bits_of(count)
    rows, columns = value.shape
    split = value.reshape((2,) * bits + (rows // count, columns))
    kept, send = split_half(split, axis, 0, bits - 1)
    (moved,) = yield [send]
    split = kept + moved
    parts = [split[..., : columns // 2], split[..., columns // 2 :]]
    orders = [list(range(1, bits)), list(range(bits - 1, 0, -1))]
    left = [list(range(bits - 1, 0, -1)) for _ in parts]
    for turn in range(bits - 1):
        keeps, sends = [], []
        for piece in range(2):
            bit = orders[piece][turn]
            kept, send = split_half(parts[piece], axis, bit, left[piece].index(bit))
            left[piece].remove(bit)
            keeps.append(kept)
            sends.append(send)
        moved = yield sends
        parts = [kept + other for kept, other in zip(keeps, moved)]
    return jnp.concatenate(parts, axis=1).astype(jnp.float32)


def state_chain(total, reverse):
    count = lax.axis_size("seq")
    me = lax.axis_index("seq")
    chips = count // 2
    chip, core = me // 2, me % 2
    (neighbour,) = yield [(total, "seq", flips(count, 0))]
    half = chip_state(total, neighbour, core, reverse)
    parts = yield [
        (half, "seq", [(source, source ^ (2 * step)) for source in range(count)]) for step in range(1, chips)
    ]
    entering = entering_state(chip, chips, reverse, parts)
    (other,) = yield [(entering, "seq", flips(count, 0))]
    return core_state(entering, other, neighbour, core, reverse)


def all_chain(value, axis):
    count = lax.axis_size(axis)
    me = lax.axis_index(axis)
    moved = yield [(value, axis, rotation(count, -step)) for step in range(1, count)]
    whole = jnp.zeros((count,) + value.shape, value.dtype)
    for step, piece in enumerate([value] + list(moved)):
        whole = lax.dynamic_update_index_in_dim(whole, piece, (me + step) % count, 0)
    return whole


def parts_of(value):
    high = lax.reduce_precision(value, 8, 7)
    return high.astype(jnp.bfloat16), (value - high).astype(jnp.bfloat16)


def shared_chain(value, flat, row_sum, holder):
    count = lax.axis_size("seq")
    me = lax.axis_index("seq")
    rows, columns = value.shape
    chips = count // 2
    block = rows // count
    chip, core = me // 2, me % 2
    kept, send = split_half(value.reshape(chips, 2, block, columns), "seq", 0, 1)
    moved, flat_moved = yield [send, (flat, "seq", flips(count, 0))]
    own = kept + moved
    flat = flat + flat_moved
    flat_parts = parts_of(flat)
    depth = flat.shape[0]

    def chip_pairs(step):
        return [(source, source ^ (2 * step)) for source in range(count)]

    steps = range(1, chips)
    outgoing = [
        jnp.concatenate([lax.dynamic_index_in_dim(own, chip ^ step, 0, False).astype(jnp.bfloat16), *flat_parts], axis=0)
        for step in steps
    ]
    moved = yield [(part, "seq", chip_pairs(step)) for part, step in zip(outgoing, steps)]
    own = lax.dynamic_index_in_dim(own, chip, 0, False)
    held = jnp.zeros((chips, 2 * depth, columns), jnp.bfloat16)
    held = lax.dynamic_update_index_in_dim(held, jnp.concatenate(flat_parts, axis=0), chip, 0)
    for step, other in zip(steps, moved):
        own = own + other[:block].astype(jnp.float32)
        held = lax.dynamic_update_index_in_dim(held, other[block:], chip ^ step, 0)
    held = held.astype(jnp.float32)
    flat = jnp.sum(held[:, :depth] + held[:, depth:], axis=0)
    length = row_sum.shape[0]
    few = -(-length // (16 * columns)) * 16
    row_sum = jnp.pad(row_sum, (0, few * columns - length)).reshape(few, columns)
    pieces = yield from all_chain(
        jnp.concatenate([own.astype(jnp.bfloat16), *parts_of(flat), *parts_of(row_sum)], axis=0), "head"
    )
    mine = jnp.sum(pieces[:, :block].astype(jnp.float32), axis=0).astype(jnp.bfloat16)
    rest = pieces[:, block:].astype(jnp.float32)
    holder.append(rest[:, :depth] + rest[:, depth : 2 * depth])
    rest = jnp.sum(rest[:, 2 * depth :], axis=0)
    holder.append((rest[:few] + rest[few:]).reshape(-1)[:length])
    moved = yield [(mine, "seq", chip_pairs(step)) for step in steps]
    found = jnp.zeros((chips,) + mine.shape, mine.dtype)
    for step, piece in zip(range(chips), [mine] + list(moved)):
        found = lax.dynamic_update_index_in_dim(found, piece, chip ^ step, 0)
    (moved,) = yield [(found, "seq", flips(count, 0))]
    low = jnp.where(core == 0, found, moved)
    high = jnp.where(core == 0, moved, found)
    return jnp.stack([low, high], axis=1).astype(jnp.float32).reshape(rows, columns)


def shift_chain(value, axis, steps):
    count = lax.axis_size(axis)
    leading, last = (max(0, -steps), min(count, count - steps))
    (moved,) = yield [(value, axis, [(source, source + steps) for source in range(leading, last)])]
    return moved


def dot(a, b, dims=(((1,), (0,)), ((), ()))):
    return lax.dot_general(a, b, dims, preferred_element_type=jnp.float32)


LAST = (((1,), (1,)), ((), ()))
FIRST = (((0,), (0,)), ((), ()))


def halves(value):
    high = value.astype(jnp.bfloat16)
    return high, (value - high.astype(jnp.float32)).astype(jnp.bfloat16)


def spread_heads(value, expand):
    high, rest = halves(value)
    return dot(high, expand) + dot(rest, expand)


def sum_heads(value, expand):
    high, rest = halves(value)
    return dot(high, expand, LAST) + dot(rest, expand, LAST)


def two_part(state):
    return jnp.concatenate(halves(state), axis=0)


def twice(value):
    value = value.astype(jnp.bfloat16)
    return jnp.concatenate([value, value], axis=1)


def triangle(size, upper):
    row = lax.broadcasted_iota(jnp.int32, (size, size), 0)
    column = lax.broadcasted_iota(jnp.int32, (size, size), 1)
    keep = column >= row if upper else row >= column
    return jnp.where(keep, 1.0, 0.0).astype(jnp.float32)


def exact_dot(a, b):
    return lax.dot_general(
        a, b, (((1,), (0,)), ((), ())), precision=lax.Precision.HIGHEST, preferred_element_type=jnp.float32
    )


def pair_blocks(value):
    lane = lax.broadcasted_iota(jnp.int32, value.shape, 1)
    zero = jnp.zeros_like(value)
    return jnp.concatenate(
        [jnp.where(lane < HDIM, value, zero), jnp.where(lane >= HDIM, value, zero)], axis=0
    )


def conv_rows(extended, taps, bias, rows):
    count = taps.shape[0]
    total = bias
    for tap in range(count):
        begin = 8 - (count - 1) + tap
        total = total + taps[tap : tap + 1] * extended[begin : begin + rows, :]
    return total


def head_terms(dt, timing, damping, seg_column, seg_row):
    value = dt + timing
    step = jnp.maximum(value, 0.0) + jnp.log1p(jnp.exp(-jnp.abs(value)))
    rate = jnp.exp(damping)
    log_decay = -step * rate
    rows = dt.shape[0]
    running = exact_dot(triangle(rows, False), log_decay)
    last = running[rows - 1 : rows]
    seg_last = seg_row[:, rows - 1 : rows]
    entering = jnp.where(seg_column == 0.0, jnp.exp(running), 0.0)
    toward = jnp.where(seg_column == seg_last, jnp.exp(last - running), 0.0)
    return value, step, rate, log_decay, running, entering, toward


def forward_kernel(
    proj, shared, dt, seg_col, seg_row, edge_v, edge_s, taps, offset, filters, baseline, timing, damping, skip, expand,
    full, readers_out, run_out, entry_out, states_out, final_out,
    ext_v, ext_s, state, carried,
):
    rows = dt.shape[0]
    heads = dt.shape[1]

    @pl.when(pl.program_id(0) == 0)
    def start():
        ext_v[0:8, :] = edge_v[...]
        ext_s[0:8, :] = edge_s[...]
        state[...] = jnp.zeros_like(state)
        carried[...] = jnp.ones_like(carried)

    ext_v[8 : 8 + rows, :] = proj[...]
    ext_s[8 : 8 + rows, :] = shared[...]
    pre = conv_rows(ext_v, taps[...], offset[...], rows)
    signal = pre * jax.nn.sigmoid(pre)
    pre_c = conv_rows(ext_s, filters[...], baseline[...], rows)
    control = pre_c * jax.nn.sigmoid(pre_c)
    ext_v[0:8, :] = ext_v[rows : rows + 8, :]
    ext_s[0:8, :] = ext_s[rows : rows + 8, :]
    writers = control[:, :STATE].astype(jnp.bfloat16)
    readers = control[:, STATE:].astype(jnp.bfloat16)
    readers_out[...] = readers
    seg_c, seg_r = seg_col[...], seg_row[0]
    value, step, rate, log_decay, running, entering, toward = head_terms(dt[...], timing[...], damping[...], seg_c, seg_r)
    across = running.T
    row = lax.broadcasted_iota(jnp.int32, (rows, rows), 0)
    column = lax.broadcasted_iota(jnp.int32, (rows, rows), 1)
    bias = jnp.where((seg_c == seg_r) & (row >= column), 0.0, -1e30)
    scores = dot(readers, writers, LAST)
    bias = jnp.concatenate([bias, bias], axis=1)
    scores = jnp.concatenate([scores, scores], axis=1)
    spread = spread_heads(jnp.concatenate([step, entering, toward, entering * carried[...]], axis=0), expand[...])
    step_e, enter_e, toward_e = spread[:rows], spread[rows : 2 * rows], spread[2 * rows : 3 * rows]
    run_out[...] = entering * carried[...]
    weighted = signal * step_e
    low = weighted.astype(jnp.bfloat16)
    old = state[...]
    states_out[0] = old
    carry = dot(twice(readers), two_part(old)) * enter_e + skip[...] * signal
    for pair in range(heads // 2):
        a, b = 2 * pair, 2 * pair + 1
        lanes = slice(pair * 2 * HDIM, (pair + 1) * 2 * HDIM)
        ahead = jnp.concatenate(
            [running[:, a : a + 1] - across[a : a + 1], running[:, b : b + 1] - across[b : b + 1]], axis=1
        )
        mixing = (jnp.exp(ahead + bias) * scores).astype(jnp.bfloat16)
        full[:, lanes] = dot(mixing, pair_blocks(low[:, lanes])) + carry[:, lanes]
    passing = enter_e[rows - 1 : rows]
    new = passing * old + dot(writers, (weighted * toward_e).astype(jnp.bfloat16), FIRST)
    state[...] = new
    entry_out[0] = carried[...]
    through = carried[...] * entering[rows - 1 : rows]
    carried[...] = through

    @pl.when(pl.program_id(0) == pl.num_programs(0) - 1)
    def last():
        final_out[0:STATE, :] = new
        final_out[STATE : STATE + 8, :] = spread_heads(jnp.broadcast_to(through, (8, heads)), expand[...])


def vmem(limit=56):
    return pltpu.CompilerParams(vmem_limit_bytes=limit * 1024 * 1024, dimension_semantics=("arbitrary",))


def whole_spec(array):
    return pl.BlockSpec(array.shape, lambda *index: (0,) * array.ndim)


def forward_scan(proj, shared, dt, seg_col, seg_row, edge_v, edge_s, taps, offset, filters, baseline, timing, damping, skip, expand):
    length, inner = proj.shape
    heads = dt.shape[1]
    blocks = length // SPAN
    rows2 = lambda width: pl.BlockSpec((SPAN, width), lambda c: (c, 0))
    fixed = (edge_v, edge_s, taps, offset, filters, baseline, timing, damping, skip, expand)
    return pl.pallas_call(
        forward_kernel,
        grid=(blocks,),
        in_specs=[rows2(inner), rows2(2 * STATE), rows2(heads), rows2(1), pl.BlockSpec((1, 1, SPAN), lambda c: (c, 0, 0))]
        + [whole_spec(a) for a in fixed],
        out_specs=[
            rows2(inner), rows2(STATE), rows2(heads),
            pl.BlockSpec((1, 1, heads), lambda c: (c, 0, 0)),
            pl.BlockSpec((1, STATE, inner), lambda c: (c, 0, 0)),
            pl.BlockSpec((STATE + 8, inner), lambda c: (0, 0)),
        ],
        out_shape=[
            jax.ShapeDtypeStruct((length, inner), jnp.float32),
            jax.ShapeDtypeStruct((length, STATE), jnp.bfloat16),
            jax.ShapeDtypeStruct((length, heads), jnp.float32),
            jax.ShapeDtypeStruct((blocks, 1, heads), jnp.float32),
            jax.ShapeDtypeStruct((blocks, STATE, inner), jnp.float32),
            jax.ShapeDtypeStruct((STATE + 8, inner), jnp.float32),
        ],
        scratch_shapes=[
            pltpu.VMEM((SPAN + 8, inner), jnp.float32),
            pltpu.VMEM((SPAN + 8, 2 * STATE), jnp.float32),
            pltpu.VMEM((STATE, inner), jnp.float32),
            pltpu.VMEM((1, heads), jnp.float32),
        ],
        compiler_params=vmem(),
    )(proj, shared, dt, seg_col, seg_row, *fixed)


def join_kernel(local, readers, run, gate_in, incoming, expand, full, squares):
    run_e = spread_heads(run[...], expand[...])
    value = local[...] + run_e * dot(twice(readers[...]), two_part(incoming[...]))
    full[...] = value
    gate = gate_in[...]
    gated = value * gate * jax.nn.sigmoid(gate)
    squares[...] = jnp.sum(gated * gated, axis=1, keepdims=True)


def join_incoming(local, readers, run, gate_in, incoming, expand):
    length, inner = local.shape
    heads = run.shape[1]
    rows2 = lambda width: pl.BlockSpec((BLOCK, width), lambda c: (c, 0))
    return pl.pallas_call(
        join_kernel,
        grid=(length // BLOCK,),
        in_specs=[rows2(inner), rows2(STATE), rows2(heads), rows2(inner), whole_spec(incoming), whole_spec(expand)],
        out_specs=[rows2(inner), rows2(1)],
        out_shape=[jax.ShapeDtypeStruct((length, inner), jnp.float32), jax.ShapeDtypeStruct((length, 1), jnp.float32)],
        compiler_params=vmem(),
    )(local, readers, run, gate_in, incoming, expand)


def norm_cot_kernel(upstream, readout, full, gate_in, inverse, postnorm, norm_cot, normalized, inner_sum, gain_sum):
    @pl.when(pl.program_id(0) == 0)
    def start():
        gain_sum[...] = jnp.zeros_like(gain_sum)

    cot = dot(upstream[...], readout[...])
    norm_cot[...] = cot
    gate = gate_in[...]
    unit = full[...] * gate * jax.nn.sigmoid(gate) * inverse[...]
    normalized[...] = (unit * postnorm[...]).astype(jnp.bfloat16)
    product = cot * unit
    gain_sum[...] += jnp.sum(product.reshape(-1, 8, product.shape[1]), axis=0)
    inner_sum[...] = jnp.sum(product * postnorm[...], axis=1, keepdims=True)


def norm_cotangent(upstream, readout, full, gate_in, inverse, postnorm):
    length, inner = full.shape
    rows2 = lambda width: pl.BlockSpec((BLOCK, width), lambda c: (c, 0))
    return pl.pallas_call(
        norm_cot_kernel,
        grid=(length // BLOCK,),
        in_specs=[rows2(upstream.shape[1]), whole_spec(readout), rows2(inner), rows2(inner), rows2(1), whole_spec(postnorm)],
        out_specs=[rows2(inner), rows2(inner), rows2(1), pl.BlockSpec((8, inner), lambda c: (0, 0))],
        out_shape=[
            jax.ShapeDtypeStruct((length, inner), jnp.float32),
            jax.ShapeDtypeStruct((length, inner), jnp.bfloat16),
            jax.ShapeDtypeStruct((length, 1), jnp.float32),
            jax.ShapeDtypeStruct((8, inner), jnp.float32),
        ],
        compiler_params=vmem(),
    )(upstream, readout, full, gate_in, inverse, postnorm)


def gate_kernel(norm_cot, full_in, gate_in, inverse, mean, postnorm, run, readers, expand, final, full_cot, gate_low, pending):
    @pl.when(pl.program_id(0) == 0)
    def start():
        pending[0:STATE, :] = jnp.zeros((STATE, pending.shape[1]), jnp.float32)
        pending[STATE : STATE + 8, :] = final[STATE : STATE + 8, :]

    gate, full = gate_in[...], full_in[...]
    sigmoid = jax.nn.sigmoid(gate)
    active = gate * sigmoid
    scaled = inverse[...]
    unit = full * active * scaled
    gated_cot = scaled * (norm_cot[...] * postnorm[...] - unit * mean[...])
    cot = gated_cot * active
    full_cot[...] = cot
    gate_low[...] = (gated_cot * full * sigmoid * (1.0 + gate * (1.0 - sigmoid))).astype(jnp.bfloat16)
    run_e = spread_heads(run[...], expand[...])
    pending[0:STATE, :] += dot(readers[...], (cot * run_e).astype(jnp.bfloat16), FIRST)


def gate_cotangent(norm_cot, full, gate_in, inverse, mean, postnorm, run, readers, expand, final):
    length, inner = full.shape
    heads = run.shape[1]
    rows2 = lambda width: pl.BlockSpec((BLOCK, width), lambda c: (c, 0))
    return pl.pallas_call(
        gate_kernel,
        grid=(length // BLOCK,),
        in_specs=[rows2(inner), rows2(inner), rows2(inner), rows2(1), rows2(1), whole_spec(postnorm), rows2(heads), rows2(STATE), whole_spec(expand), whole_spec(final)],
        out_specs=[rows2(inner), rows2(inner), pl.BlockSpec((STATE + 8, inner), lambda c: (0, 0))],
        out_shape=[
            jax.ShapeDtypeStruct((length, inner), jnp.float32),
            jax.ShapeDtypeStruct((length, inner), jnp.bfloat16),
            jax.ShapeDtypeStruct((STATE + 8, inner), jnp.float32),
        ],
        compiler_params=vmem(),
    )(norm_cot, full, gate_in, inverse, mean, postnorm, run, readers, expand, final)


def silu_slope(pre, sigmoid):
    return sigmoid * (1.0 + pre * (1.0 - sigmoid))


def fold(value):
    return jnp.sum(value.reshape(-1, 8, value.shape[1]), axis=0)


def taps_back(pre_cot, taps, following, rows):
    count = taps.shape[0]
    total = taps[count - 1 : count] * pre_cot
    for tap in range(count - 1):
        later = count - 1 - tap
        total = total + taps[tap : tap + 1] * following[later : later + rows, :]
    return total


def backward_kernel(
    opening,
    proj, shared, before_v, before_s, dt, seg_col, seg_row, full_cot, states, entry,
    edge_v, edge_s, taps, offset, filters, baseline, timing, damping, skip, expand, incoming, leaving, after_v, after_s, sums_in,
    values_low, shared_low, dt_low, sums_out, head_v, head_s, lam_out,
    ext_v, ext_s, later_v, later_s, lam, tap_sum, offset_sum, filter_sum, base_sum, timing_sum, damping_sum, direct_sum,
):
    rows, heads = dt.shape
    step_index = pl.program_id(0)
    blocks = pl.num_programs(0)

    @pl.when(step_index == 0)
    def start():
        lam[...] = leaving[...]
        later_v[rows : rows + 8, :] = after_v[...]
        later_s[rows : rows + 8, :] = after_s[...]
        for item in (tap_sum, offset_sum, filter_sum, base_sum, timing_sum, damping_sum, direct_sum):
            item[...] = jnp.zeros_like(item)

    ext_v[0:8, :] = before_v[...]
    ext_s[0:8, :] = before_s[...]
    if opening:

        @pl.when(step_index == blocks - 1)
        def first_block():
            ext_v[0:8, :] = edge_v[...]
            ext_s[0:8, :] = edge_s[...]

    ext_v[8 : 8 + rows, :] = proj[...]
    ext_s[8 : 8 + rows, :] = shared[...]
    pre = conv_rows(ext_v, taps[...], offset[...], rows)
    sigmoid = jax.nn.sigmoid(pre)
    signal = pre * sigmoid
    pre_c = conv_rows(ext_s, filters[...], baseline[...], rows)
    sigmoid_c = jax.nn.sigmoid(pre_c)
    control = pre_c * sigmoid_c
    writers = control[:, :STATE].astype(jnp.bfloat16)
    readers = control[:, STATE:].astype(jnp.bfloat16)
    seg_c, seg_r = seg_col[...], seg_row[0]
    value, step, rate, log_decay, running, entering, toward = head_terms(dt[...], timing[...], damping[...], seg_c, seg_r)
    across = running.T
    row = lax.broadcasted_iota(jnp.int32, (rows, rows), 0)
    column = lax.broadcasted_iota(jnp.int32, (rows, rows), 1)
    bias = jnp.where((seg_c == seg_r) & (column >= row), 0.0, -1e30)
    scores = dot(writers, readers, LAST)
    bias = jnp.concatenate([bias, bias], axis=1)
    scores = jnp.concatenate([scores, scores], axis=1)
    one_hot = expand[...]
    spread = spread_heads(jnp.concatenate([step, entering, toward], axis=0), one_hot)
    step_e, enter_e, toward_e = spread[:rows], spread[rows : 2 * rows], spread[2 * rows : 3 * rows]
    cot = full_cot[...]
    cot_low = cot.astype(jnp.bfloat16)
    weighted = signal * step_e
    low = weighted.astype(jnp.bfloat16)
    after = lam[...]
    after_parts = two_part(after)
    from_state = dot(twice(writers), after_parts) * toward_e
    entry_e = spread_heads(jnp.broadcast_to(entry[0], (8, heads)), one_hot)
    old = states[0] + entry_e[0:1] * incoming[...]
    old_parts = two_part(old)
    cot_entering = cot * enter_e
    cot_entering_low = cot_entering.astype(jnp.bfloat16)
    score_cot = jnp.zeros((rows, rows), jnp.float32)
    row_sums = jnp.zeros((rows, heads), jnp.float32)
    column_sums = []
    head_place = lax.broadcasted_iota(jnp.int32, (rows, heads), 1)
    direct_part = []
    step_part = []
    for pair in range(heads // 2):
        a, b = 2 * pair, 2 * pair + 1
        lanes = slice(pair * 2 * HDIM, (pair + 1) * 2 * HDIM)
        ahead = jnp.concatenate(
            [across[a : a + 1] - running[:, a : a + 1], across[b : b + 1] - running[:, b : b + 1]], axis=1
        )
        decays = jnp.exp(ahead + bias)
        mixing = decays * scores
        blocked = pair_blocks(cot_low[:, lanes])
        weighted_cot = dot(mixing.astype(jnp.bfloat16), blocked) + from_state[:, lanes]
        step_part.append(weighted_cot * signal[:, lanes])
        later_v[0:rows, lanes] = weighted_cot * step_e[:, lanes] + skip[:, lanes] * cot[:, lanes]
        inner = dot(low[:, lanes], blocked, LAST)
        linked = inner * decays
        score_cot = score_cot + linked[:, :rows] + linked[:, rows:]
        energy = inner * mixing
        for head, side in ((a, energy[:, :rows]), (b, energy[:, rows:])):
            row_sums = jnp.where(head_place == head, jnp.sum(side, axis=1, keepdims=True), row_sums)
            column_sums.append(jnp.sum(side, axis=0, keepdims=True))
    sums_across = jnp.concatenate(column_sums, axis=0)
    state_term = weighted * from_state
    enter_term = cot_entering * dot(twice(readers), old_parts)
    passing = enter_e[rows - 1 : rows]
    last_term = fold(state_term) + fold(after * old * passing)
    by_head = sum_heads(
        jnp.concatenate([jnp.concatenate(step_part, axis=1), enter_term - state_term, last_term], axis=0), one_hot
    )
    step_cot = by_head[:rows]
    running_cot = sums_across.T - row_sums + by_head[rows : 2 * rows]
    last_cot = jnp.sum(by_head[2 * rows :], axis=0, keepdims=True)
    decay_cot = exact_dot(triangle(rows, True), running_cot) + last_cot
    step_cot = step_cot - decay_cot * rate
    dt_cot = step_cot * jax.nn.sigmoid(value)
    dt_low[...] = dt_cot.astype(jnp.bfloat16)
    timing_sum[...] += fold(dt_cot)
    damping_sum[...] += fold(decay_cot * log_decay)
    direct_sum[...] += fold(cot * signal)
    score_low = score_cot.astype(jnp.bfloat16)
    reader_cot = dot(score_low, writers, FIRST) + dot(
        jnp.concatenate([cot_entering_low, cot_entering_low], axis=1), jnp.concatenate(halves(old), axis=1), LAST
    )
    push = (weighted * toward_e).astype(jnp.bfloat16)
    writer_cot = dot(score_low, readers) + dot(
        jnp.concatenate([push, push], axis=1), jnp.concatenate(halves(after), axis=1), LAST
    )
    lam[...] = passing * after + dot(readers, cot_entering_low, FIRST)

    pre_cot = later_v[0:rows, :] * silu_slope(pre, sigmoid)
    later_v[0:rows, :] = pre_cot
    pre_cot_c = jnp.concatenate([writer_cot, reader_cot], axis=1) * silu_slope(pre_c, sigmoid_c)
    later_s[0:rows, :] = pre_cot_c
    values_cot = taps_back(pre_cot, taps[...], later_v, rows)
    shared_cot = taps_back(pre_cot_c, filters[...], later_s, rows)
    values_low[...] = values_cot.astype(jnp.bfloat16)
    shared_low[...] = shared_cot.astype(jnp.bfloat16)
    count = taps.shape[0]
    for tap in range(count):
        begin = 8 - (count - 1) + tap
        tap_sum[tap] += fold(pre_cot * ext_v[begin : begin + rows, :])
        filter_sum[tap] += fold(pre_cot_c * ext_s[begin : begin + rows, :])
    offset_sum[...] += fold(pre_cot)
    base_sum[...] += fold(pre_cot_c)
    later_v[rows : rows + 8, :] = later_v[0:8, :]
    later_s[rows : rows + 8, :] = later_s[0:8, :]

    @pl.when(step_index == blocks - 1)
    def head():
        head_v[...] = pre_cot[0:8, :]
        head_s[...] = pre_cot_c[0:8, :]
        lam_out[...] = lam[...]
        sums_out[...] = sums_in[...]
        total = lambda value: jnp.sum(value, axis=0, keepdims=True)
        for tap in range(count):
            sums_out[tap : tap + 1, :] += total(tap_sum[tap])
            sums_out[count + 2 + tap : count + 3 + tap, : 2 * STATE] += total(filter_sum[tap])
        sums_out[count : count + 1, :] += total(offset_sum[...])
        sums_out[count + 1 : count + 2, :] += total(direct_sum[...])
        sums_out[2 * count + 2 : 2 * count + 3, : 2 * STATE] += total(base_sum[...])
        sums_out[2 * count + 3 : 2 * count + 4, :heads] += total(timing_sum[...])
        sums_out[2 * count + 4 : 2 * count + 5, :heads] += total(damping_sum[...])


def backward_scan(
    proj, shared, dt, seg_col, seg_row, full_cot, states, entry,
    edge_v, edge_s, taps, offset, filters, baseline, timing, damping, skip, expand, incoming, leaving, after_v, after_s, sums, base, blocks,
):
    inner = proj.shape[1]
    length = blocks * SPAN
    heads = dt.shape[1]
    count = taps.shape[0]
    back = lambda c: base + blocks - 1 - c
    own = lambda width: pl.BlockSpec((SPAN, width), lambda c: (blocks - 1 - c, 0))
    rows2 = lambda width: pl.BlockSpec((SPAN, width), lambda c: (back(c), 0))
    before = lambda width: pl.BlockSpec((8, width), lambda c: (jnp.maximum(back(c) * (SPAN // 8) - 1, 0), 0))
    lead = lambda *shape: pl.BlockSpec((1,) + shape, lambda c: (back(c), 0, 0))
    fixed = (edge_v, edge_s, taps, offset, filters, baseline, timing, damping, skip, expand, incoming, leaving, after_v, after_s, sums)
    f32 = lambda *shape: jax.ShapeDtypeStruct(shape, jnp.float32)
    carried = [f32(*sums.shape), f32(8, inner), f32(8, 2 * STATE), f32(STATE, inner)]
    low = lambda width: jax.ShapeDtypeStruct((length, width), jnp.bfloat16)
    return pl.pallas_call(
        functools.partial(backward_kernel, base == 0),
        grid=(blocks,),
        in_specs=[rows2(inner), rows2(2 * STATE), before(inner), before(2 * STATE), rows2(heads), rows2(1), lead(1, SPAN), rows2(inner), lead(STATE, inner), lead(1, heads)]
        + [whole_spec(a) for a in fixed],
        out_specs=[own(inner), own(2 * STATE), own(heads)] + [whole_spec(a) for a in carried],
        out_shape=[low(inner), low(2 * STATE), low(heads)] + carried,
        scratch_shapes=[
            pltpu.VMEM((SPAN + 8, inner), jnp.float32),
            pltpu.VMEM((SPAN + 8, 2 * STATE), jnp.float32),
            pltpu.VMEM((SPAN + 8, inner), jnp.float32),
            pltpu.VMEM((SPAN + 8, 2 * STATE), jnp.float32),
            pltpu.VMEM((STATE, inner), jnp.float32),
            pltpu.VMEM((count, 8, inner), jnp.float32),
            pltpu.VMEM((8, inner), jnp.float32),
            pltpu.VMEM((count, 8, 2 * STATE), jnp.float32),
            pltpu.VMEM((8, 2 * STATE), jnp.float32),
            pltpu.VMEM((8, heads), jnp.float32),
            pltpu.VMEM((8, heads), jnp.float32),
            pltpu.VMEM((8, inner), jnp.float32),
        ],
        compiler_params=vmem(),
    )(proj, shared, proj, shared, dt, seg_col, seg_row, full_cot, states, entry, *fixed)


def normed_cot_kernel(gate_low, values_low, shared_low, dt_low, gating, values, control, timestep, tokens, scale, gain, low, row_sum, gain_sum):
    total = dot(gate_low[...], gating[...]) + dot(values_low[...], values[...])
    total = total + dot(shared_low[...], control[...]) + dot(dt_low[...], timestep[...])
    low[0] = total.astype(jnp.bfloat16)
    product = total * (tokens[...].astype(jnp.float32) * scale[...])
    gain_sum[...] = fold(product)

    @pl.when(pl.program_id(0) == 0)
    def start():
        row_sum[...] = jnp.zeros_like(row_sum)

    row_sum[...] += jnp.sum(product * gain[...], axis=1, keepdims=True)


def normed_cotangent(gate_low, values_low, shared_low, dt_low, gating, values, control, timestep, tokens, scale, gain, base, ranks):
    length = values_low.shape[0]
    width = gating.shape[1]
    tile = width // ranks
    here = base // length
    fixed = lambda array: pl.BlockSpec((length, array.shape[1]), lambda c: (0, 0))
    late = lambda size: pl.BlockSpec((length, size), lambda c: (here, 0))
    columns = lambda rows: pl.BlockSpec((rows, tile), lambda c: (0, c))
    parts = (gate_low, values_low, shared_low, dt_low)
    weights = (gating, values, control, timestep)
    return pl.pallas_call(
        normed_cot_kernel,
        grid=(width // tile,),
        in_specs=[late(gate_low.shape[1])] + [fixed(a) for a in parts[1:]] + [columns(a.shape[0]) for a in weights]
        + [pl.BlockSpec((length, tile), lambda c: (here, c)), late(1), columns(1)],
        out_specs=[pl.BlockSpec((1, length, tile), lambda c: (c, 0, 0)), pl.BlockSpec((length, 1), lambda c: (0, 0)), columns(8)],
        out_shape=[
            jax.ShapeDtypeStruct((ranks, length, tile), jnp.bfloat16),
            jax.ShapeDtypeStruct((length, 1), jnp.float32),
            jax.ShapeDtypeStruct((8, width), jnp.float32),
        ],
        compiler_params=vmem(),
    )(*parts, *weights, tokens, scale, gain)


def small_call(kernel, shape, scratch, place, *arrays):
    return pl.pallas_call(
        kernel,
        in_specs=[pl.BlockSpec(memory_space=pltpu.SMEM)] + [pl.BlockSpec(memory_space=pltpu.VMEM)] * len(arrays),
        out_specs=pl.BlockSpec(memory_space=pltpu.VMEM),
        out_shape=jax.ShapeDtypeStruct(shape, jnp.float32),
        scratch_shapes=scratch,
        compiler_params=pltpu.CompilerParams(vmem_limit_bytes=32 * 1024 * 1024),
    )(place.reshape(1), *arrays)


def chip_state(mine, other, core, reverse):
    half = mine.shape[1] // 2

    def kernel(core, mine, other, out):
        index = core[0]
        first = (index == 1) if reverse else (index == 0)
        lanes = pl.ds(pl.multiple_of(index * half, 128), half)
        a, b = mine[:, lanes], other[:, lanes]
        early, late = jnp.where(first, a, b), jnp.where(first, b, a)
        out[0:STATE, :] = late[STATE : STATE + 1] * early[0:STATE] + late[0:STATE]
        out[STATE : STATE + 8, :] = late[STATE : STATE + 8] * early[STATE : STATE + 8]

    return small_call(kernel, (STATE + 8, half), [], core, mine, other)


def entering_state(chip, chips, reverse, parts):
    shape = parts[0].shape

    def kernel(chip, *refs):
        ins, out, held = refs[: len(parts)], refs[len(parts)], refs[len(parts) + 1]
        for step, ref in enumerate(ins):
            held[step + 1] = ref[...]
        here = chip[0]
        out[...] = jnp.zeros_like(out)

        def add(turn, carry):
            source = chips - 1 - turn if reverse else turn
            step = source ^ here
            out[...] = held[step, STATE : STATE + 1, :] * out[...] + held[step, 0:STATE, :]
            return carry

        lax.fori_loop(0, chips - 1 - here if reverse else here, add, 0)

    return small_call(kernel, (STATE, shape[1]), [pltpu.VMEM((chips,) + shape, jnp.float32)], chip, *parts)


def core_state(mine, other, neighbour, core, reverse):
    half = mine.shape[1]

    def kernel(core, mine, other, neighbour, out):
        low = core[0] == 0
        after = low if reverse else jnp.logical_not(low)
        for side, value in enumerate((jnp.where(low, mine[...], other[...]), jnp.where(low, other[...], mine[...]))):
            lanes = slice(side * half, (side + 1) * half)
            passed = neighbour[STATE : STATE + 1, lanes] * value + neighbour[0:STATE, lanes]
            out[:, lanes] = jnp.where(after, passed, value)

    return small_call(kernel, (STATE, 2 * half), [], core, mine, other, neighbour)


def early_cot_kernel(
    gate_low, values_low, more_v, shared_low, more_s, dt_low, gating, values, control, timestep, tokens, before, scale, before_scale, gain,
    low, row_sum, gain_sum,
):
    extra = more_v.shape[0]
    main = dot(gate_low[...], gating[...]) + dot(dt_low[...], timestep[...])
    total = dot(jnp.concatenate([values_low[...], more_v[...]], axis=0), values[...])
    total = total + dot(jnp.concatenate([shared_low[...], more_s[...]], axis=0), control[...])
    total = total + jnp.concatenate([main, jnp.zeros((extra, main.shape[1]), jnp.float32)], axis=0)
    low[0] = total.astype(jnp.bfloat16)
    units = [tokens[...].astype(jnp.float32) * scale[...], before[...] * before_scale[...]]
    product = total * jnp.concatenate(units, axis=0)
    gain_sum[...] = fold(product)

    @pl.when(pl.program_id(0) == 0)
    def start():
        row_sum[...] = jnp.zeros_like(row_sum)

    row_sum[...] += jnp.sum(product * gain[...], axis=1, keepdims=True)


def early_cotangent(
    gate_low, values_low, more_v, shared_low, more_s, dt_low, gating, values, control, timestep, tokens, before, scale, before_scale, gain, ranks
):
    length = values_low.shape[0]
    rows = length + more_v.shape[0]
    width = gating.shape[1]
    tile = width // ranks
    fixed = lambda array: pl.BlockSpec(array.shape, lambda c: (0, 0))
    first = lambda array: pl.BlockSpec((length, array.shape[1]), lambda c: (0, 0))
    columns = lambda count: pl.BlockSpec((count, tile), lambda c: (0, c))
    weights = (gating, values, control, timestep)
    return pl.pallas_call(
        early_cot_kernel,
        grid=(width // tile,),
        in_specs=[first(gate_low)] + [fixed(a) for a in (values_low, more_v, shared_low, more_s, dt_low)]
        + [columns(a.shape[0]) for a in weights]
        + [columns(length), columns(before.shape[0]), first(scale), fixed(before_scale), columns(1)],
        out_specs=[pl.BlockSpec((1, rows, tile), lambda c: (c, 0, 0)), pl.BlockSpec((rows, 1), lambda c: (0, 0)), columns(8)],
        out_shape=[
            jax.ShapeDtypeStruct((ranks, rows, tile), jnp.bfloat16),
            jax.ShapeDtypeStruct((rows, 1), jnp.float32),
            jax.ShapeDtypeStruct((8, width), jnp.float32),
        ],
        compiler_params=vmem(),
    )(gate_low, values_low, more_v, shared_low, more_s, dt_low, *weights, tokens, before, scale, before_scale, gain)


def shards(
    tokens,
    prenorm,
    gating,
    values,
    control,
    timestep,
    kernel,
    offset,
    filters,
    baseline,
    timing,
    damping,
    direct,
    postnorm,
    readout,
    doc_starts,
    cotangent,
):
    length, share = tokens.shape
    inner = kernel.shape[1]
    heads = timing.shape[0]
    ranks = lax.axis_size("head")
    features = share * ranks
    channels = inner * ranks
    blocks = length // SPAN
    half = length // 2
    f32, bf16 = jnp.float32, jnp.bfloat16

    starts = doc_starts.reshape(blocks, SPAN).astype(bf16)
    place = jnp.arange(SPAN)
    counted = jnp.dot(starts, (place[:, None] <= place[None, :]).astype(bf16), preferred_element_type=f32)
    seg_row, seg_col = counted.reshape(blocks, 1, SPAN), counted.reshape(length, 1)
    expand = (jnp.arange(heads)[:, None] == jnp.arange(inner)[None, :] // HDIM).astype(bf16)
    skip = jnp.repeat(direct, HDIM)[None]
    offset_row, baseline_row, postnorm_row = offset[None], baseline[None], postnorm[None]
    timing_row, damping_row = timing[None], damping[None]

    gains = Chain(all_chain(prenorm, "head"))
    tokens_in = Chain(gather_chain(tokens, "head"))
    weights_back = phase([tokens_in, gains], lambda *a: tuple(w.T for w in a), gating, values, control, timestep, readout)
    readout_t = weights_back[4]
    finish(tokens_in, gains)
    cot_ready, found, gain_blocks = lax.optimization_barrier((cotangent, tokens_in.result, gains.result))
    upstream = lax.all_gather(cot_ready, "head", axis=1, tiled=True)
    gain = gain_blocks.reshape(1, features).astype(f32)

    def project(*found):
        gathered = place_columns(found, "head")
        wide = gathered.astype(f32)
        scale = lax.rsqrt(jnp.mean(wide * wide, axis=1, keepdims=True) + epsilon)
        normed = (wide * scale * gain).astype(bf16)
        projected = jnp.dot(normed, values, preferred_element_type=f32)
        shared = jnp.dot(normed, control, preferred_element_type=f32)
        timestep_in = jnp.dot(normed, timestep, preferred_element_type=f32)
        return gathered, scale, normed, projected, shared, timestep_in

    gathered, scale, normed, projected, shared, timestep_in = phase([], project, *found)
    edges = Chain(shift_chain(
        jnp.concatenate([projected[length - 8 :], shared[length - 8 :], gathered[length - 8 :].astype(f32)], axis=1), "seq", 1
    ))
    finish(edges)
    edge_v, edge_s = edges.result[:, :inner], edges.result[:, inner : inner + 2 * STATE]
    before = edges.result[:, inner + 2 * STATE :]
    before = jnp.pad(before, ((0, 8), (0, 0)))
    before_scale = lax.rsqrt(jnp.mean(before * before, axis=1, keepdims=True) + epsilon)
    normed_more = jnp.concatenate([normed, (before * before_scale * gain).astype(bf16)], axis=0)
    params = (kernel, offset_row, filters, baseline_row, timing_row, damping_row, skip, expand)
    local, readers, run, entry, states, final = phase(
        [], lambda *a: forward_scan(*a, *params), projected, shared, timestep_in, seg_col, seg_row, edge_v, edge_s
    )
    prefix = Chain(state_chain(final, False))
    phase([prefix])
    gate_in = phase([prefix], lambda n: jnp.dot(n, gating, preferred_element_type=f32), normed)
    finish(prefix)
    incoming = prefix.result
    full, squares = join_incoming(local, readers, run, gate_in, incoming, expand)
    squared = Chain(sum_chain(squares.reshape(length), "head"))
    finish(squared)
    inverse = lax.rsqrt(squared.result / channels + epsilon)[:, None]
    norm_cot, normalized, inner_sum, postnorm_sum = norm_cotangent(
        upstream, readout, full, gate_in, inverse, postnorm_row
    )
    means = Chain(sum_chain(inner_sum.reshape(length), "head"))
    partial_rows = phase(
        [means], lambda n: jnp.dot(n, readout_t, preferred_element_type=f32).astype(bf16), normalized
    )
    branch = lax.psum_scatter(partial_rows, "head", scatter_dimension=1, tiled=True)
    mean = means.result[:, None] / channels
    full_cot, gate_low, pending = gate_cotangent(
        norm_cot, full, gate_in, inverse, mean, postnorm_row, run, readers, expand, final
    )
    suffix = Chain(state_chain(pending, True))
    phase([suffix])
    readout_local, gating_local = phase(
        [suffix],
        lambda u, n, m, g: (
            lax.dot_general(u, n, FIRST, preferred_element_type=f32).astype(bf16),
            lax.dot_general(m, g, FIRST, preferred_element_type=f32).astype(bf16),
        ),
        upstream, normalized, normed, gate_low,
    )
    readout_sum = lax.psum_scatter(readout_local, "seq", scatter_dimension=0, tiled=True)
    gating_sum = lax.psum_scatter(gating_local, "seq", scatter_dimension=0, tiled=True)
    finish(suffix)
    leaving = suffix.result

    def backward(base, size, leaving, after_v, after_s, sums):
        return backward_scan(
            projected, shared, timestep_in, seg_col, seg_row, full_cot, states, entry,
            edge_v, edge_s, *params, incoming, leaving, after_v, after_s, sums, base, size,
        )

    def normed_back(base, *lows):
        return normed_cotangent(gate_low, *lows, *weights_back[:4], gathered, scale, gain, base, ranks)

    zeros_v, zeros_s = jnp.zeros((8, inner), f32), jnp.zeros((8, 2 * STATE), f32)
    taps = kernel.shape[0]
    sums = jnp.zeros((2 * taps + 5, inner), f32)
    late = backward(blocks // 2, blocks // 2, leaving, zeros_v, zeros_s, sums)
    normed_late = normed_back(half, *late[:3])
    total_late = Chain(scatter_chain([normed_late[0]], "head"))
    early = phase(
        [total_late], lambda *a: backward(0, blocks // 2, *a), late[6], late[4], late[5], late[3]
    )
    branch, early = lax.optimization_barrier((branch, early))

    def share_before(head, taps_of):
        following = jnp.concatenate([jnp.zeros_like(head), head], axis=0)
        return sum(taps_of[tap][None] * following[taps - 1 - tap : taps + 7 - tap] for tap in range(taps))

    more_v, more_s = share_before(early[4], kernel), share_before(early[5], filters)

    more_v, more_s = [jnp.pad(more.astype(bf16), ((0, 8), (0, 0))) for more in (more_v, more_s)]
    more_dt = jnp.zeros((16, heads), bf16)

    def last_products(low):
        normed_early = early_cotangent(
            gate_low, low, more_v, early[1], more_s, early[2], *weights_back[:4], gathered, before, scale, before_scale, gain, ranks
        )
        shared_low = jnp.concatenate([early[1], late[1], more_s], axis=0)
        low = jnp.concatenate([low, late[0], more_v], axis=0)
        small = jnp.concatenate([early[2], late[2], more_dt], axis=0)
        low = jnp.concatenate([low, jnp.pad(small, ((0, 0), (0, 128 - heads)))], axis=1)
        return (
            normed_early,
            lax.dot_general(normed_more, shared_low, FIRST, preferred_element_type=f32),
            lax.dot_general(normed_more, low, FIRST, preferred_element_type=f32).astype(bf16),
        )

    normed_early, control_local, values_local = phase([total_late], last_products, early[0])
    values_sum = lax.psum_scatter(values_local, "seq", scatter_dimension=0, tiled=True)
    finish(total_late)
    total_early = Chain(scatter_chain([normed_early[0]], "head", 2))
    prenorm_sum = (normed_early[2] + normed_late[2]).sum(0).reshape(-1, inner)
    flat = jnp.concatenate([early[3], postnorm_sum.sum(0)[None], prenorm_sum], axis=0)
    flat_rows = flat.shape[0]
    flat = jnp.pad(flat, ((0, -flat_rows % 8), (0, 0))).reshape(-1, 2 * STATE)
    row_sum = jnp.concatenate(
        [normed_early[1][:half], normed_late[1], normed_early[1][half : half + 8]], axis=0
    ).reshape(length + 8)
    holder = []
    shared_sum = Chain(shared_chain(control_local, flat, row_sum, holder))

    phase([shared_sum, total_early])
    mixed = phase(
        [shared_sum, total_early], lambda t, s: (t.astype(f32) + s.astype(f32)).astype(bf16), tokens, branch
    )
    phase([shared_sum])
    readout_sum, gating_sum = phase([shared_sum, total_early], lambda *a: a, readout_sum, gating_sum)
    finish(total_early, total_late)
    copies, row_sum = holder
    scattered = total_early.result
    extra = jnp.concatenate([scattered[half : half + 8], jnp.broadcast_to(row_sum[length:, None], (8, share))], axis=0)
    from_next = Chain(shift_chain(extra, "seq", -1))

    def closing(row_sum, early_total, late_total, copies):
        own_total = jnp.concatenate([early_total[:half], late_total], axis=0)
        own_units = tokens.astype(f32) * scale
        tokens_gradient = cotangent.astype(f32) + scale * (
            own_total * prenorm.astype(f32) - own_units * (row_sum[:length, None] / features)
        )
        by_head = copies.reshape(ranks, -1, inner)[:, :flat_rows].transpose(1, 0, 2)
        rows = by_head.reshape(flat_rows, channels)
        alike = by_head[:, 0]
        for rank in range(1, ranks):
            alike = alike + by_head[:, rank]
        return (
            tokens_gradient,
            rows[:taps],
            rows[taps],
            alike[taps + 2 : 2 * taps + 2, : 2 * STATE],
            alike[2 * taps + 2, : 2 * STATE],
            by_head[2 * taps + 3, :, :heads].reshape(-1),
            by_head[2 * taps + 4, :, :heads].reshape(-1),
            rows[taps + 1].reshape(ranks * heads, HDIM).sum(1),
            rows[2 * taps + 5],
            alike[2 * taps + 6 :].reshape(-1),
        )

    (
        tokens_gradient, kernel_gradient, offset_gradient, filters_gradient, baseline_gradient, timing_gradient,
        damping_gradient, direct_gradient, postnorm_gradient, prenorm_gradient,
    ) = phase([shared_sum, from_next], closing, row_sum, scattered, total_late.result, copies)
    finish(shared_sum, from_next)
    more_rows, more_sums = from_next.result[:8], from_next.result[8:, :1] / features
    last = scale[length - 8 :] * (
        more_rows * prenorm.astype(f32) - tokens[length - 8 :].astype(f32) * scale[length - 8 :] * more_sums
    )
    tokens_gradient = tokens_gradient.at[length - 8 :].add(last)
    return (
        mixed,
        tokens_gradient,
        prenorm_gradient,
        gating_sum.astype(f32),
        values_sum[:, :inner].astype(f32),
        shared_sum.result,
        values_sum[:, inner : inner + heads].astype(f32),
        kernel_gradient,
        offset_gradient,
        filters_gradient,
        baseline_gradient,
        timing_gradient,
        damping_gradient,
        direct_gradient,
        postnorm_gradient,
        readout_sum.astype(f32),
    )


def solution(mesh):
    return jax.shard_map(
        shards,
        mesh=mesh,
        in_specs=(
            P("seq", "head"),
            P("head"),
            P(None, "head"),
            P(None, "head"),
            P(),
            P(None, "head"),
            P(None, "head"),
            P("head"),
            P(),
            P(),
            P("head"),
            P("head"),
            P("head"),
            P("head"),
            P(None, "head"),
            P("seq"),
            P("seq", "head"),
        ),
        out_specs=(
            P("seq", "head"),
            P("seq", "head"),
            P(),
            P("seq", "head"),
            P("seq", "head"),
            P(),
            P("seq", "head"),
            P(),
            P(),
            P(),
            P(),
            P(),
            P(),
            P(),
            P(),
            P("seq", "head"),
        ),
        check_vma=False,
    )
```

```python
import functools

import jax
import jax.numpy as jnp
from jax import lax
from jax.experimental import pallas as pl
from jax.experimental.pallas import tpu as pltpu
from jax.sharding import PartitionSpec as P

HDIM = 64
STATE = 128
SPAN = 128
BLOCK = 256


epsilon = 1e-05


def rotation(count, steps):
    return [(source, (source + steps) % count) for source in range(count)]


def flips(count, bit):
    return [(source, source ^ (1 << bit)) for source in range(count)]


def bits_of(count):
    return count.bit_length() - 1


class Chain:
    def __init__(self, gen):
        self.gen = gen
        self.result = None
        self.sends = None
        self.step(None)

    def step(self, moved):
        try:
            self.sends = self.gen.send(moved)
        except StopIteration as stop:
            self.sends, self.result = None, stop.value


def phase(chains, work=None, *inputs):
    chains = [chain for chain in chains if chain.sends is not None]
    values = [[send[0] for send in chain.sends] for chain in chains]
    values, inputs = lax.optimization_barrier((values, inputs))
    moved = [
        [lax.ppermute(value, send[1], send[2]) for value, send in zip(group, chain.sends)]
        for group, chain in zip(values, chains)
    ]
    outs = work(*inputs) if work is not None else ()
    moved, outs = lax.optimization_barrier((moved, outs))
    for chain, group in zip(chains, moved):
        chain.step(group)
    return outs


def finish(*chains):
    while any(chain.sends is not None for chain in chains):
        phase(chains)
    return [chain.result for chain in chains]


def gather_chain(block, axis):
    count = lax.axis_size(axis)
    half = count // 2
    rows = block.shape[0] // 2
    found = [None] * count
    found[0] = block
    left = right = block
    for step in range(1, half):
        left, right = yield [(left, axis, rotation(count, 1)), (right, axis, rotation(count, -1))]
        found[count - step] = left
        found[step] = right
    low, high = yield [(left[:rows], axis, rotation(count, 1)), (right[rows:], axis, rotation(count, -1))]
    found[half] = jnp.concatenate([low, high], axis=0)
    return found


def place_columns(found, axis):
    count = len(found)
    me = lax.axis_index(axis)
    width = found[0].shape[1]
    whole = jnp.zeros((found[0].shape[0], count * width), found[0].dtype)
    for step, piece in enumerate(found):
        whole = lax.dynamic_update_slice_in_dim(whole, piece, (me + step) % count * width, 1)
    return whole


def scatter_chain(wholes, axis, pieces=1):
    count = lax.axis_size(axis)
    me = lax.axis_index(axis)
    half = count // 2
    rows = sum(whole.shape[1] for whole in wholes) // 2

    def part(step):
        found = [lax.dynamic_index_in_dim(whole, (me + step) % count, 0, False) for whole in wholes]
        return found[0] if len(found) == 1 else jnp.concatenate(found, axis=0)

    far = part(half)
    ahead, behind = yield [(far[:rows], axis, rotation(count, 1)), (far[rows:], axis, rotation(count, -1))]
    for step in range(half - 1, 0, -1):
        up = part(step).astype(jnp.float32)
        down = part(count - step).astype(jnp.float32)
        if step == half - 1:
            up = up.at[:rows].add(ahead.astype(jnp.float32))
            down = down.at[rows:].add(behind.astype(jnp.float32))
        else:
            up = up + ahead.astype(jnp.float32)
            down = down + behind.astype(jnp.float32)
        arrived = []
        cuts = [2 * rows * cut // (16 * pieces) * 16 for cut in range(pieces + 1)]
        for begin, end in zip(cuts, cuts[1:]):
            arrived.append(
                (yield [
                    (up[begin:end].astype(jnp.bfloat16), axis, rotation(count, 1)),
                    (down[begin:end].astype(jnp.bfloat16), axis, rotation(count, -1)),
                ])
            )
        ahead, behind = [jnp.concatenate(side, axis=0) if pieces > 1 else side[0] for side in zip(*arrived)]
    return part(0).astype(jnp.float32) + ahead.astype(jnp.float32) + behind.astype(jnp.float32)


def sum_chain(value, axis):
    count = lax.axis_size(axis)
    moved = yield [(value, axis, rotation(count, step)) for step in range(1, count)]
    for other in moved:
        value = value + other
    return value


def split_half(value, axis, bit, position):
    mine = (lax.axis_index(axis) >> bit) & 1
    kept = lax.dynamic_index_in_dim(value, mine, position, False)
    sent = lax.dynamic_index_in_dim(value, 1 - mine, position, False)
    return kept, (sent, axis, flips(lax.axis_size(axis), bit))


def rows_chain(value, axis):
    count = lax.axis_size(axis)
    bits = bits_of(count)
    rows, columns = value.shape
    split = value.reshape((2,) * bits + (rows // count, columns))
    kept, send = split_half(split, axis, 0, bits - 1)
    (moved,) = yield [send]
    split = kept + moved
    parts = [split[..., : columns // 2], split[..., columns // 2 :]]
    orders = [list(range(1, bits)), list(range(bits - 1, 0, -1))]
    left = [list(range(bits - 1, 0, -1)) for _ in parts]
    for turn in range(bits - 1):
        keeps, sends = [], []
        for piece in range(2):
            bit = orders[piece][turn]
            kept, send = split_half(parts[piece], axis, bit, left[piece].index(bit))
            left[piece].remove(bit)
            keeps.append(kept)
            sends.append(send)
        moved = yield sends
        parts = [kept + other for kept, other in zip(keeps, moved)]
    return jnp.concatenate(parts, axis=1).astype(jnp.float32)


def state_chain(total, reverse):
    count = lax.axis_size("seq")
    me = lax.axis_index("seq")
    chips = count // 2
    chip, core = me // 2, me % 2
    (neighbour,) = yield [(total, "seq", flips(count, 0))]
    half = chip_state(total, neighbour, core, reverse)
    parts = yield [
        (half, "seq", [(source, source ^ (2 * step)) for source in range(count)]) for step in range(1, chips)
    ]
    entering = entering_state(chip, chips, reverse, parts)
    (other,) = yield [(entering, "seq", flips(count, 0))]
    return core_state(entering, other, neighbour, core, reverse)


def all_chain(value, axis):
    count = lax.axis_size(axis)
    me = lax.axis_index(axis)
    moved = yield [(value, axis, rotation(count, -step)) for step in range(1, count)]
    whole = jnp.zeros((count,) + value.shape, value.dtype)
    for step, piece in enumerate([value] + list(moved)):
        whole = lax.dynamic_update_index_in_dim(whole, piece, (me + step) % count, 0)
    return whole


def parts_of(value):
    high = lax.reduce_precision(value, 8, 7)
    return high.astype(jnp.bfloat16), (value - high).astype(jnp.bfloat16)


def shared_chain(value, flat, row_sum, holder):
    count = lax.axis_size("seq")
    me = lax.axis_index("seq")
    rows, columns = value.shape
    chips = count // 2
    block = rows // count
    chip, core = me // 2, me % 2
    kept, send = split_half(value.reshape(chips, 2, block, columns), "seq", 0, 1)
    moved, flat_moved = yield [send, (flat, "seq", flips(count, 0))]
    own = kept + moved
    flat = flat + flat_moved
    flat_parts = parts_of(flat)
    depth = flat.shape[0]

    def chip_pairs(step):
        return [(source, source ^ (2 * step)) for source in range(count)]

    steps = range(1, chips)
    outgoing = [
        jnp.concatenate([lax.dynamic_index_in_dim(own, chip ^ step, 0, False).astype(jnp.bfloat16), *flat_parts], axis=0)
        for step in steps
    ]
    moved = yield [(part, "seq", chip_pairs(step)) for part, step in zip(outgoing, steps)]
    own = lax.dynamic_index_in_dim(own, chip, 0, False)
    held = jnp.zeros((chips, 2 * depth, columns), jnp.bfloat16)
    held = lax.dynamic_update_index_in_dim(held, jnp.concatenate(flat_parts, axis=0), chip, 0)
    for step, other in zip(steps, moved):
        own = own + other[:block].astype(jnp.float32)
        held = lax.dynamic_update_index_in_dim(held, other[block:], chip ^ step, 0)
    held = held.astype(jnp.float32)
    flat = jnp.sum(held[:, :depth] + held[:, depth:], axis=0)
    length = row_sum.shape[0]
    few = -(-length // (16 * columns)) * 16
    row_sum = jnp.pad(row_sum, (0, few * columns - length)).reshape(few, columns)
    pieces = yield from all_chain(
        jnp.concatenate([own.astype(jnp.bfloat16), *parts_of(flat), *parts_of(row_sum)], axis=0), "head"
    )
    mine = jnp.sum(pieces[:, :block].astype(jnp.float32), axis=0).astype(jnp.bfloat16)
    rest = pieces[:, block:].astype(jnp.float32)
    holder.append(rest[:, :depth] + rest[:, depth : 2 * depth])
    rest = jnp.sum(rest[:, 2 * depth :], axis=0)
    holder.append((rest[:few] + rest[few:]).reshape(-1)[:length])
    moved = yield [(mine, "seq", chip_pairs(step)) for step in steps]
    found = jnp.zeros((chips,) + mine.shape, mine.dtype)
    for step, piece in zip(range(chips), [mine] + list(moved)):
        found = lax.dynamic_update_index_in_dim(found, piece, chip ^ step, 0)
    (moved,) = yield [(found, "seq", flips(count, 0))]
    low = jnp.where(core == 0, found, moved)
    high = jnp.where(core == 0, moved, found)
    return jnp.stack([low, high], axis=1).astype(jnp.float32).reshape(rows, columns)


def shift_chain(value, axis, steps):
    count = lax.axis_size(axis)
    leading, last = (max(0, -steps), min(count, count - steps))
    (moved,) = yield [(value, axis, [(source, source + steps) for source in range(leading, last)])]
    return moved


def dot(a, b, dims=(((1,), (0,)), ((), ()))):
    return lax.dot_general(a, b, dims, preferred_element_type=jnp.float32)


LAST = (((1,), (1,)), ((), ()))
FIRST = (((0,), (0,)), ((), ()))


def halves(value):
    high = value.astype(jnp.bfloat16)
    return high, (value - high.astype(jnp.float32)).astype(jnp.bfloat16)


def spread_heads(value, expand):
    high, rest = halves(value)
    return dot(high, expand) + dot(rest, expand)


def sum_heads(value, expand):
    high, rest = halves(value)
    return dot(high, expand, LAST) + dot(rest, expand, LAST)


def two_part(state):
    return jnp.concatenate(halves(state), axis=0)


def twice(value):
    value = value.astype(jnp.bfloat16)
    return jnp.concatenate([value, value], axis=1)


def rows_three(state):
    high, rest = halves(state)
    return jnp.concatenate([high, rest, high], axis=0)


def columns_three(value, first):
    high, rest = halves(value)
    return jnp.concatenate([high, high, rest] if first else [high, rest, high], axis=1)


def triangle(size, upper):
    row = lax.broadcasted_iota(jnp.int32, (size, size), 0)
    column = lax.broadcasted_iota(jnp.int32, (size, size), 1)
    keep = column >= row if upper else row >= column
    return jnp.where(keep, 1.0, 0.0).astype(jnp.float32)


def exact_dot(a, b):
    return lax.dot_general(
        a, b, (((1,), (0,)), ((), ())), precision=lax.Precision.HIGHEST, preferred_element_type=jnp.float32
    )


def pair_blocks(value):
    lane = lax.broadcasted_iota(jnp.int32, value.shape, 1)
    zero = jnp.zeros_like(value)
    return jnp.concatenate(
        [jnp.where(lane < HDIM, value, zero), jnp.where(lane >= HDIM, value, zero)], axis=0
    )


def conv_rows(extended, taps, bias, rows):
    count = taps.shape[0]
    total = bias
    for tap in range(count):
        begin = 8 - (count - 1) + tap
        total = total + taps[tap : tap + 1] * extended[begin : begin + rows, :]
    return total


def head_terms(dt, timing, damping, seg_column, seg_row):
    value = dt + timing
    step = jnp.maximum(value, 0.0) + jnp.log1p(jnp.exp(-jnp.abs(value)))
    rate = jnp.exp(damping)
    log_decay = -step * rate
    rows = dt.shape[0]
    running = exact_dot(triangle(rows, False), log_decay)
    last = running[rows - 1 : rows]
    seg_last = seg_row[:, rows - 1 : rows]
    entering = jnp.where(seg_column == 0.0, jnp.exp(running), 0.0)
    toward = jnp.where(seg_column == seg_last, jnp.exp(last - running), 0.0)
    return value, step, rate, log_decay, running, entering, toward


def forward_kernel(
    proj, shared, dt, seg_col, seg_row, edge_v, edge_s, taps, offset, filters, baseline, timing, damping, skip, expand,
    full, readers_out, run_out, entry_out, states_out, final_out,
    ext_v, ext_s, state, carried,
):
    rows = dt.shape[0]
    heads = dt.shape[1]

    @pl.when(pl.program_id(0) == 0)
    def start():
        ext_v[0:8, :] = edge_v[...]
        ext_s[0:8, :] = edge_s[...]
        state[...] = jnp.zeros_like(state)
        carried[...] = jnp.ones_like(carried)

    ext_v[8 : 8 + rows, :] = proj[...]
    ext_s[8 : 8 + rows, :] = shared[...]
    pre = conv_rows(ext_v, taps[...], offset[...], rows)
    signal = pre * jax.nn.sigmoid(pre)
    pre_c = conv_rows(ext_s, filters[...], baseline[...], rows)
    control = pre_c * jax.nn.sigmoid(pre_c)
    ext_v[0:8, :] = ext_v[rows : rows + 8, :]
    ext_s[0:8, :] = ext_s[rows : rows + 8, :]
    writers = control[:, :STATE].astype(jnp.bfloat16)
    readers = control[:, STATE:].astype(jnp.bfloat16)
    readers_out[...] = readers
    seg_c, seg_r = seg_col[...], seg_row[0]
    value, step, rate, log_decay, running, entering, toward = head_terms(dt[...], timing[...], damping[...], seg_c, seg_r)
    across = running.T
    row = lax.broadcasted_iota(jnp.int32, (rows, rows), 0)
    column = lax.broadcasted_iota(jnp.int32, (rows, rows), 1)
    bias = jnp.where((seg_c == seg_r) & (row >= column), 0.0, -1e30)
    scores = dot(readers, writers, LAST)
    bias = jnp.concatenate([bias, bias], axis=1)
    scores = jnp.concatenate([scores, scores], axis=1)
    spread = spread_heads(jnp.concatenate([step, entering, toward, entering * carried[...]], axis=0), expand[...])
    step_e, enter_e, toward_e = spread[:rows], spread[rows : 2 * rows], spread[2 * rows : 3 * rows]
    run_out[...] = entering * carried[...]
    weighted = signal * step_e
    low = weighted.astype(jnp.bfloat16)
    old = state[...]
    states_out[0] = old
    carry = dot(columns_three(control[:, STATE:], True), rows_three(old)) * enter_e + skip[...] * signal
    for pair in range(heads // 2):
        a, b = 2 * pair, 2 * pair + 1
        lanes = slice(pair * 2 * HDIM, (pair + 1) * 2 * HDIM)
        ahead = jnp.concatenate(
            [running[:, a : a + 1] - across[a : a + 1], running[:, b : b + 1] - across[b : b + 1]], axis=1
        )
        mixing = (jnp.exp(ahead + bias) * scores).astype(jnp.bfloat16)
        full[:, lanes] = dot(mixing, pair_blocks(low[:, lanes])) + carry[:, lanes]
    passing = enter_e[rows - 1 : rows]
    push_high, push_rest = halves(weighted * toward_e)
    writers_rest = halves(control[:, :STATE])[1]
    new = passing * old + dot(writers, push_high, FIRST)
    new = new + dot(writers, push_rest, FIRST) + dot(writers_rest, push_high, FIRST)
    state[...] = new
    entry_out[0] = carried[...]
    through = carried[...] * entering[rows - 1 : rows]
    carried[...] = through

    @pl.when(pl.program_id(0) == pl.num_programs(0) - 1)
    def last():
        final_out[0:STATE, :] = new
        final_out[STATE : STATE + 8, :] = spread_heads(jnp.broadcast_to(through, (8, heads)), expand[...])


def vmem(limit=56):
    return pltpu.CompilerParams(vmem_limit_bytes=limit * 1024 * 1024, dimension_semantics=("arbitrary",))


def whole_spec(array):
    return pl.BlockSpec(array.shape, lambda *index: (0,) * array.ndim)


def forward_scan(proj, shared, dt, seg_col, seg_row, edge_v, edge_s, taps, offset, filters, baseline, timing, damping, skip, expand):
    length, inner = proj.shape
    heads = dt.shape[1]
    blocks = length // SPAN
    rows2 = lambda width: pl.BlockSpec((SPAN, width), lambda c: (c, 0))
    fixed = (edge_v, edge_s, taps, offset, filters, baseline, timing, damping, skip, expand)
    return pl.pallas_call(
        forward_kernel,
        grid=(blocks,),
        in_specs=[rows2(inner), rows2(2 * STATE), rows2(heads), rows2(1), pl.BlockSpec((1, 1, SPAN), lambda c: (c, 0, 0))]
        + [whole_spec(a) for a in fixed],
        out_specs=[
            rows2(inner), rows2(STATE), rows2(heads),
            pl.BlockSpec((1, 1, heads), lambda c: (c, 0, 0)),
            pl.BlockSpec((1, STATE, inner), lambda c: (c, 0, 0)),
            pl.BlockSpec((STATE + 8, inner), lambda c: (0, 0)),
        ],
        out_shape=[
            jax.ShapeDtypeStruct((length, inner), jnp.float32),
            jax.ShapeDtypeStruct((length, STATE), jnp.bfloat16),
            jax.ShapeDtypeStruct((length, heads), jnp.float32),
            jax.ShapeDtypeStruct((blocks, 1, heads), jnp.float32),
            jax.ShapeDtypeStruct((blocks, STATE, inner), jnp.float32),
            jax.ShapeDtypeStruct((STATE + 8, inner), jnp.float32),
        ],
        scratch_shapes=[
            pltpu.VMEM((SPAN + 8, inner), jnp.float32),
            pltpu.VMEM((SPAN + 8, 2 * STATE), jnp.float32),
            pltpu.VMEM((STATE, inner), jnp.float32),
            pltpu.VMEM((1, heads), jnp.float32),
        ],
        compiler_params=vmem(),
    )(proj, shared, dt, seg_col, seg_row, *fixed)


def join_kernel(local, readers, run, gate_in, incoming, expand, full, squares):
    run_e = spread_heads(run[...], expand[...])
    value = local[...] + run_e * dot(twice(readers[...]), two_part(incoming[...]))
    full[...] = value
    gate = gate_in[...]
    gated = value * gate * jax.nn.sigmoid(gate)
    squares[...] = jnp.sum(gated * gated, axis=1, keepdims=True)


def join_incoming(local, readers, run, gate_in, incoming, expand):
    length, inner = local.shape
    heads = run.shape[1]
    rows2 = lambda width: pl.BlockSpec((BLOCK, width), lambda c: (c, 0))
    return pl.pallas_call(
        join_kernel,
        grid=(length // BLOCK,),
        in_specs=[rows2(inner), rows2(STATE), rows2(heads), rows2(inner), whole_spec(incoming), whole_spec(expand)],
        out_specs=[rows2(inner), rows2(1)],
        out_shape=[jax.ShapeDtypeStruct((length, inner), jnp.float32), jax.ShapeDtypeStruct((length, 1), jnp.float32)],
        compiler_params=vmem(),
    )(local, readers, run, gate_in, incoming, expand)


def norm_cot_kernel(upstream, readout, full, gate_in, inverse, postnorm, norm_cot, normalized, inner_sum, gain_sum):
    @pl.when(pl.program_id(0) == 0)
    def start():
        gain_sum[...] = jnp.zeros_like(gain_sum)

    cot = dot(upstream[...], readout[...])
    norm_cot[...] = cot
    gate = gate_in[...]
    unit = full[...] * gate * jax.nn.sigmoid(gate) * inverse[...]
    normalized[...] = (unit * postnorm[...]).astype(jnp.bfloat16)
    product = cot * unit
    gain_sum[...] += jnp.sum(product.reshape(-1, 8, product.shape[1]), axis=0)
    inner_sum[...] = jnp.sum(product * postnorm[...], axis=1, keepdims=True)


def norm_cotangent(upstream, readout, full, gate_in, inverse, postnorm):
    length, inner = full.shape
    rows2 = lambda width: pl.BlockSpec((BLOCK, width), lambda c: (c, 0))
    return pl.pallas_call(
        norm_cot_kernel,
        grid=(length // BLOCK,),
        in_specs=[rows2(upstream.shape[1]), whole_spec(readout), rows2(inner), rows2(inner), rows2(1), whole_spec(postnorm)],
        out_specs=[rows2(inner), rows2(inner), rows2(1), pl.BlockSpec((8, inner), lambda c: (0, 0))],
        out_shape=[
            jax.ShapeDtypeStruct((length, inner), jnp.float32),
            jax.ShapeDtypeStruct((length, inner), jnp.bfloat16),
            jax.ShapeDtypeStruct((length, 1), jnp.float32),
            jax.ShapeDtypeStruct((8, inner), jnp.float32),
        ],
        compiler_params=vmem(),
    )(upstream, readout, full, gate_in, inverse, postnorm)


def gate_kernel(norm_cot, full_in, gate_in, inverse, mean, postnorm, run, readers, expand, final, full_cot, gate_low, pending):
    @pl.when(pl.program_id(0) == 0)
    def start():
        pending[0:STATE, :] = jnp.zeros((STATE, pending.shape[1]), jnp.float32)
        pending[STATE : STATE + 8, :] = final[STATE : STATE + 8, :]

    gate, full = gate_in[...], full_in[...]
    sigmoid = jax.nn.sigmoid(gate)
    active = gate * sigmoid
    scaled = inverse[...]
    unit = full * active * scaled
    gated_cot = scaled * (norm_cot[...] * postnorm[...] - unit * mean[...])
    cot = gated_cot * active
    full_cot[...] = cot
    gate_low[...] = (gated_cot * full * sigmoid * (1.0 + gate * (1.0 - sigmoid))).astype(jnp.bfloat16)
    run_e = spread_heads(run[...], expand[...])
    high, rest = halves(cot * run_e)
    pending[0:STATE, :] += dot(readers[...], high, FIRST) + dot(readers[...], rest, FIRST)


def gate_cotangent(norm_cot, full, gate_in, inverse, mean, postnorm, run, readers, expand, final):
    length, inner = full.shape
    heads = run.shape[1]
    rows2 = lambda width: pl.BlockSpec((BLOCK, width), lambda c: (c, 0))
    return pl.pallas_call(
        gate_kernel,
        grid=(length // BLOCK,),
        in_specs=[rows2(inner), rows2(inner), rows2(inner), rows2(1), rows2(1), whole_spec(postnorm), rows2(heads), rows2(STATE), whole_spec(expand), whole_spec(final)],
        out_specs=[rows2(inner), rows2(inner), pl.BlockSpec((STATE + 8, inner), lambda c: (0, 0))],
        out_shape=[
            jax.ShapeDtypeStruct((length, inner), jnp.float32),
            jax.ShapeDtypeStruct((length, inner), jnp.bfloat16),
            jax.ShapeDtypeStruct((STATE + 8, inner), jnp.float32),
        ],
        compiler_params=vmem(),
    )(norm_cot, full, gate_in, inverse, mean, postnorm, run, readers, expand, final)


def silu_slope(pre, sigmoid):
    return sigmoid * (1.0 + pre * (1.0 - sigmoid))


def fold(value):
    return jnp.sum(value.reshape(-1, 8, value.shape[1]), axis=0)


def taps_back(pre_cot, taps, following, rows):
    count = taps.shape[0]
    total = taps[count - 1 : count] * pre_cot
    for tap in range(count - 1):
        later = count - 1 - tap
        total = total + taps[tap : tap + 1] * following[later : later + rows, :]
    return total


def backward_kernel(
    opening,
    proj, shared, before_v, before_s, dt, seg_col, seg_row, full_cot, states, entry,
    edge_v, edge_s, taps, offset, filters, baseline, timing, damping, skip, expand, incoming, leaving, after_v, after_s, sums_in,
    values_low, shared_low, dt_low, sums_out, head_v, head_s, lam_out,
    ext_v, ext_s, later_v, later_s, lam, tap_sum, offset_sum, filter_sum, base_sum, timing_sum, damping_sum, direct_sum,
):
    rows, heads = dt.shape
    step_index = pl.program_id(0)
    blocks = pl.num_programs(0)

    @pl.when(step_index == 0)
    def start():
        lam[...] = leaving[...]
        later_v[rows : rows + 8, :] = after_v[...]
        later_s[rows : rows + 8, :] = after_s[...]
        for item in (tap_sum, offset_sum, filter_sum, base_sum, timing_sum, damping_sum, direct_sum):
            item[...] = jnp.zeros_like(item)

    ext_v[0:8, :] = before_v[...]
    ext_s[0:8, :] = before_s[...]
    if opening:

        @pl.when(step_index == blocks - 1)
        def first_block():
            ext_v[0:8, :] = edge_v[...]
            ext_s[0:8, :] = edge_s[...]

    ext_v[8 : 8 + rows, :] = proj[...]
    ext_s[8 : 8 + rows, :] = shared[...]
    pre = conv_rows(ext_v, taps[...], offset[...], rows)
    sigmoid = jax.nn.sigmoid(pre)
    signal = pre * sigmoid
    pre_c = conv_rows(ext_s, filters[...], baseline[...], rows)
    sigmoid_c = jax.nn.sigmoid(pre_c)
    control = pre_c * sigmoid_c
    writers = control[:, :STATE].astype(jnp.bfloat16)
    readers = control[:, STATE:].astype(jnp.bfloat16)
    seg_c, seg_r = seg_col[...], seg_row[0]
    value, step, rate, log_decay, running, entering, toward = head_terms(dt[...], timing[...], damping[...], seg_c, seg_r)
    across = running.T
    row = lax.broadcasted_iota(jnp.int32, (rows, rows), 0)
    column = lax.broadcasted_iota(jnp.int32, (rows, rows), 1)
    bias = jnp.where((seg_c == seg_r) & (column >= row), 0.0, -1e30)
    scores = dot(writers, readers, LAST)
    bias = jnp.concatenate([bias, bias], axis=1)
    scores = jnp.concatenate([scores, scores], axis=1)
    one_hot = expand[...]
    spread = spread_heads(jnp.concatenate([step, entering, toward], axis=0), one_hot)
    step_e, enter_e, toward_e = spread[:rows], spread[rows : 2 * rows], spread[2 * rows : 3 * rows]
    cot = full_cot[...]
    cot_low = cot.astype(jnp.bfloat16)
    weighted = signal * step_e
    low = weighted.astype(jnp.bfloat16)
    after = lam[...]
    from_state = dot(columns_three(control[:, :STATE], True), rows_three(after)) * toward_e
    entry_e = spread_heads(jnp.broadcast_to(entry[0], (8, heads)), one_hot)
    old = states[0] + entry_e[0:1] * incoming[...]
    cot_entering = cot * enter_e
    cot_entering_low, cot_entering_rest = halves(cot_entering)
    score_cot = jnp.zeros((rows, rows), jnp.float32)
    row_sums = jnp.zeros((rows, heads), jnp.float32)
    column_sums = []
    head_place = lax.broadcasted_iota(jnp.int32, (rows, heads), 1)
    direct_part = []
    step_part = []
    for pair in range(heads // 2):
        a, b = 2 * pair, 2 * pair + 1
        lanes = slice(pair * 2 * HDIM, (pair + 1) * 2 * HDIM)
        ahead = jnp.concatenate(
            [across[a : a + 1] - running[:, a : a + 1], across[b : b + 1] - running[:, b : b + 1]], axis=1
        )
        decays = jnp.exp(ahead + bias)
        mixing = decays * scores
        blocked = pair_blocks(cot_low[:, lanes])
        weighted_cot = dot(mixing.astype(jnp.bfloat16), blocked) + from_state[:, lanes]
        step_part.append(weighted_cot * signal[:, lanes])
        later_v[0:rows, lanes] = weighted_cot * step_e[:, lanes] + skip[:, lanes] * cot[:, lanes]
        inner = dot(low[:, lanes], blocked, LAST)
        linked = inner * decays
        score_cot = score_cot + linked[:, :rows] + linked[:, rows:]
        energy = inner * mixing
        for head, side in ((a, energy[:, :rows]), (b, energy[:, rows:])):
            row_sums = jnp.where(head_place == head, jnp.sum(side, axis=1, keepdims=True), row_sums)
            column_sums.append(jnp.sum(side, axis=0, keepdims=True))
    sums_across = jnp.concatenate(column_sums, axis=0)
    state_term = weighted * from_state
    enter_term = cot_entering * dot(columns_three(control[:, STATE:], True), rows_three(old))
    passing = enter_e[rows - 1 : rows]
    last_term = fold(state_term) + fold(after * old * passing)
    by_head = sum_heads(
        jnp.concatenate([jnp.concatenate(step_part, axis=1), enter_term - state_term, last_term], axis=0), one_hot
    )
    step_cot = by_head[:rows]
    running_cot = sums_across.T - row_sums + by_head[rows : 2 * rows]
    last_cot = jnp.sum(by_head[2 * rows :], axis=0, keepdims=True)
    decay_cot = exact_dot(triangle(rows, True), running_cot) + last_cot
    step_cot = step_cot - decay_cot * rate
    dt_cot = step_cot * jax.nn.sigmoid(value)
    dt_low[...] = dt_cot.astype(jnp.bfloat16)
    timing_sum[...] += fold(dt_cot)
    damping_sum[...] += fold(decay_cot * log_decay)
    direct_sum[...] += fold(cot * signal)
    score_low = score_cot.astype(jnp.bfloat16)
    reader_cot = dot(score_low, writers, FIRST) + dot(
        columns_three(cot_entering, True), columns_three(old, False), LAST
    )
    writer_cot = dot(score_low, readers) + dot(
        columns_three(weighted * toward_e, True), columns_three(after, False), LAST
    )
    readers_rest = halves(control[:, STATE:])[1]
    gained = dot(readers, cot_entering_low, FIRST) + dot(readers, cot_entering_rest, FIRST)
    lam[...] = passing * after + gained + dot(readers_rest, cot_entering_low, FIRST)

    pre_cot = later_v[0:rows, :] * silu_slope(pre, sigmoid)
    later_v[0:rows, :] = pre_cot
    pre_cot_c = jnp.concatenate([writer_cot, reader_cot], axis=1) * silu_slope(pre_c, sigmoid_c)
    later_s[0:rows, :] = pre_cot_c
    values_cot = taps_back(pre_cot, taps[...], later_v, rows)
    shared_cot = taps_back(pre_cot_c, filters[...], later_s, rows)
    values_low[...] = values_cot.astype(jnp.bfloat16)
    shared_low[...] = shared_cot.astype(jnp.bfloat16)
    count = taps.shape[0]
    for tap in range(count):
        begin = 8 - (count - 1) + tap
        tap_sum[tap] += fold(pre_cot * ext_v[begin : begin + rows, :])
        filter_sum[tap] += fold(pre_cot_c * ext_s[begin : begin + rows, :])
    offset_sum[...] += fold(pre_cot)
    base_sum[...] += fold(pre_cot_c)
    later_v[rows : rows + 8, :] = later_v[0:8, :]
    later_s[rows : rows + 8, :] = later_s[0:8, :]

    @pl.when(step_index == blocks - 1)
    def head():
        head_v[...] = pre_cot[0:8, :]
        head_s[...] = pre_cot_c[0:8, :]
        lam_out[...] = lam[...]
        sums_out[...] = sums_in[...]
        total = lambda value: jnp.sum(value, axis=0, keepdims=True)
        for tap in range(count):
            sums_out[tap : tap + 1, :] += total(tap_sum[tap])
            sums_out[count + 2 + tap : count + 3 + tap, : 2 * STATE] += total(filter_sum[tap])
        sums_out[count : count + 1, :] += total(offset_sum[...])
        sums_out[count + 1 : count + 2, :] += total(direct_sum[...])
        sums_out[2 * count + 2 : 2 * count + 3, : 2 * STATE] += total(base_sum[...])
        sums_out[2 * count + 3 : 2 * count + 4, :heads] += total(timing_sum[...])
        sums_out[2 * count + 4 : 2 * count + 5, :heads] += total(damping_sum[...])


def backward_scan(
    proj, shared, dt, seg_col, seg_row, full_cot, states, entry,
    edge_v, edge_s, taps, offset, filters, baseline, timing, damping, skip, expand, incoming, leaving, after_v, after_s, sums, base, blocks,
):
    inner = proj.shape[1]
    length = blocks * SPAN
    heads = dt.shape[1]
    count = taps.shape[0]
    back = lambda c: base + blocks - 1 - c
    own = lambda width: pl.BlockSpec((SPAN, width), lambda c: (blocks - 1 - c, 0))
    rows2 = lambda width: pl.BlockSpec((SPAN, width), lambda c: (back(c), 0))
    before = lambda width: pl.BlockSpec((8, width), lambda c: (jnp.maximum(back(c) * (SPAN // 8) - 1, 0), 0))
    lead = lambda *shape: pl.BlockSpec((1,) + shape, lambda c: (back(c), 0, 0))
    fixed = (edge_v, edge_s, taps, offset, filters, baseline, timing, damping, skip, expand, incoming, leaving, after_v, after_s, sums)
    f32 = lambda *shape: jax.ShapeDtypeStruct(shape, jnp.float32)
    carried = [f32(*sums.shape), f32(8, inner), f32(8, 2 * STATE), f32(STATE, inner)]
    low = lambda width: jax.ShapeDtypeStruct((length, width), jnp.bfloat16)
    return pl.pallas_call(
        functools.partial(backward_kernel, base == 0),
        grid=(blocks,),
        in_specs=[rows2(inner), rows2(2 * STATE), before(inner), before(2 * STATE), rows2(heads), rows2(1), lead(1, SPAN), rows2(inner), lead(STATE, inner), lead(1, heads)]
        + [whole_spec(a) for a in fixed],
        out_specs=[own(inner), own(2 * STATE), own(heads)] + [whole_spec(a) for a in carried],
        out_shape=[low(inner), low(2 * STATE), low(heads)] + carried,
        scratch_shapes=[
            pltpu.VMEM((SPAN + 8, inner), jnp.float32),
            pltpu.VMEM((SPAN + 8, 2 * STATE), jnp.float32),
            pltpu.VMEM((SPAN + 8, inner), jnp.float32),
            pltpu.VMEM((SPAN + 8, 2 * STATE), jnp.float32),
            pltpu.VMEM((STATE, inner), jnp.float32),
            pltpu.VMEM((count, 8, inner), jnp.float32),
            pltpu.VMEM((8, inner), jnp.float32),
            pltpu.VMEM((count, 8, 2 * STATE), jnp.float32),
            pltpu.VMEM((8, 2 * STATE), jnp.float32),
            pltpu.VMEM((8, heads), jnp.float32),
            pltpu.VMEM((8, heads), jnp.float32),
            pltpu.VMEM((8, inner), jnp.float32),
        ],
        compiler_params=vmem(),
    )(proj, shared, proj, shared, dt, seg_col, seg_row, full_cot, states, entry, *fixed)


def normed_cot_kernel(gate_low, values_low, shared_low, dt_low, gating, values, control, timestep, tokens, scale, gain, low, row_sum, gain_sum):
    total = dot(gate_low[...], gating[...]) + dot(values_low[...], values[...])
    total = total + dot(shared_low[...], control[...]) + dot(dt_low[...], timestep[...])
    low[0] = total.astype(jnp.bfloat16)
    product = total * (tokens[...].astype(jnp.float32) * scale[...])
    gain_sum[...] = fold(product)

    @pl.when(pl.program_id(0) == 0)
    def start():
        row_sum[...] = jnp.zeros_like(row_sum)

    row_sum[...] += jnp.sum(product * gain[...], axis=1, keepdims=True)


def normed_cotangent(gate_low, values_low, shared_low, dt_low, gating, values, control, timestep, tokens, scale, gain, base, ranks):
    length = values_low.shape[0]
    width = gating.shape[1]
    tile = width // ranks
    here = base // length
    fixed = lambda array: pl.BlockSpec((length, array.shape[1]), lambda c: (0, 0))
    late = lambda size: pl.BlockSpec((length, size), lambda c: (here, 0))
    columns = lambda rows: pl.BlockSpec((rows, tile), lambda c: (0, c))
    parts = (gate_low, values_low, shared_low, dt_low)
    weights = (gating, values, control, timestep)
    return pl.pallas_call(
        normed_cot_kernel,
        grid=(width // tile,),
        in_specs=[late(gate_low.shape[1])] + [fixed(a) for a in parts[1:]] + [columns(a.shape[0]) for a in weights]
        + [pl.BlockSpec((length, tile), lambda c: (here, c)), late(1), columns(1)],
        out_specs=[pl.BlockSpec((1, length, tile), lambda c: (c, 0, 0)), pl.BlockSpec((length, 1), lambda c: (0, 0)), columns(8)],
        out_shape=[
            jax.ShapeDtypeStruct((ranks, length, tile), jnp.bfloat16),
            jax.ShapeDtypeStruct((length, 1), jnp.float32),
            jax.ShapeDtypeStruct((8, width), jnp.float32),
        ],
        compiler_params=vmem(),
    )(*parts, *weights, tokens, scale, gain)


def small_call(kernel, shape, scratch, place, *arrays):
    return pl.pallas_call(
        kernel,
        in_specs=[pl.BlockSpec(memory_space=pltpu.SMEM)] + [pl.BlockSpec(memory_space=pltpu.VMEM)] * len(arrays),
        out_specs=pl.BlockSpec(memory_space=pltpu.VMEM),
        out_shape=jax.ShapeDtypeStruct(shape, jnp.float32),
        scratch_shapes=scratch,
        compiler_params=pltpu.CompilerParams(vmem_limit_bytes=32 * 1024 * 1024),
    )(place.reshape(1), *arrays)


def chip_state(mine, other, core, reverse):
    half = mine.shape[1] // 2

    def kernel(core, mine, other, out):
        index = core[0]
        first = (index == 1) if reverse else (index == 0)
        lanes = pl.ds(pl.multiple_of(index * half, 128), half)
        a, b = mine[:, lanes], other[:, lanes]
        early, late = jnp.where(first, a, b), jnp.where(first, b, a)
        out[0:STATE, :] = late[STATE : STATE + 1] * early[0:STATE] + late[0:STATE]
        out[STATE : STATE + 8, :] = late[STATE : STATE + 8] * early[STATE : STATE + 8]

    return small_call(kernel, (STATE + 8, half), [], core, mine, other)


def entering_state(chip, chips, reverse, parts):
    shape = parts[0].shape

    def kernel(chip, *refs):
        ins, out, held = refs[: len(parts)], refs[len(parts)], refs[len(parts) + 1]
        for step, ref in enumerate(ins):
            held[step + 1] = ref[...]
        here = chip[0]
        out[...] = jnp.zeros_like(out)

        def add(turn, carry):
            source = chips - 1 - turn if reverse else turn
            step = source ^ here
            out[...] = held[step, STATE : STATE + 1, :] * out[...] + held[step, 0:STATE, :]
            return carry

        lax.fori_loop(0, chips - 1 - here if reverse else here, add, 0)

    return small_call(kernel, (STATE, shape[1]), [pltpu.VMEM((chips,) + shape, jnp.float32)], chip, *parts)


def core_state(mine, other, neighbour, core, reverse):
    half = mine.shape[1]

    def kernel(core, mine, other, neighbour, out):
        low = core[0] == 0
        after = low if reverse else jnp.logical_not(low)
        for side, value in enumerate((jnp.where(low, mine[...], other[...]), jnp.where(low, other[...], mine[...]))):
            lanes = slice(side * half, (side + 1) * half)
            passed = neighbour[STATE : STATE + 1, lanes] * value + neighbour[0:STATE, lanes]
            out[:, lanes] = jnp.where(after, passed, value)

    return small_call(kernel, (STATE, 2 * half), [], core, mine, other, neighbour)


def early_cot_kernel(
    gate_low, values_low, more_v, shared_low, more_s, dt_low, gating, values, control, timestep, tokens, before, scale, before_scale, gain,
    low, row_sum, gain_sum,
):
    extra = more_v.shape[0]
    main = dot(gate_low[...], gating[...]) + dot(dt_low[...], timestep[...])
    total = dot(jnp.concatenate([values_low[...], more_v[...]], axis=0), values[...])
    total = total + dot(jnp.concatenate([shared_low[...], more_s[...]], axis=0), control[...])
    total = total + jnp.concatenate([main, jnp.zeros((extra, main.shape[1]), jnp.float32)], axis=0)
    low[0] = total.astype(jnp.bfloat16)
    units = [tokens[...].astype(jnp.float32) * scale[...], before[...] * before_scale[...]]
    product = total * jnp.concatenate(units, axis=0)
    gain_sum[...] = fold(product)

    @pl.when(pl.program_id(0) == 0)
    def start():
        row_sum[...] = jnp.zeros_like(row_sum)

    row_sum[...] += jnp.sum(product * gain[...], axis=1, keepdims=True)


def early_cotangent(
    gate_low, values_low, more_v, shared_low, more_s, dt_low, gating, values, control, timestep, tokens, before, scale, before_scale, gain, ranks
):
    length = values_low.shape[0]
    rows = length + more_v.shape[0]
    width = gating.shape[1]
    tile = width // ranks
    fixed = lambda array: pl.BlockSpec(array.shape, lambda c: (0, 0))
    first = lambda array: pl.BlockSpec((length, array.shape[1]), lambda c: (0, 0))
    columns = lambda count: pl.BlockSpec((count, tile), lambda c: (0, c))
    weights = (gating, values, control, timestep)
    return pl.pallas_call(
        early_cot_kernel,
        grid=(width // tile,),
        in_specs=[first(gate_low)] + [fixed(a) for a in (values_low, more_v, shared_low, more_s, dt_low)]
        + [columns(a.shape[0]) for a in weights]
        + [columns(length), columns(before.shape[0]), first(scale), fixed(before_scale), columns(1)],
        out_specs=[pl.BlockSpec((1, rows, tile), lambda c: (c, 0, 0)), pl.BlockSpec((rows, 1), lambda c: (0, 0)), columns(8)],
        out_shape=[
            jax.ShapeDtypeStruct((ranks, rows, tile), jnp.bfloat16),
            jax.ShapeDtypeStruct((rows, 1), jnp.float32),
            jax.ShapeDtypeStruct((8, width), jnp.float32),
        ],
        compiler_params=vmem(),
    )(gate_low, values_low, more_v, shared_low, more_s, dt_low, *weights, tokens, before, scale, before_scale, gain)


def two_products_kernel(first, second, by_first, by_second, out):
    out[0] = dot(first[...], by_first[...], FIRST).astype(jnp.bfloat16)
    out[1] = dot(second[...], by_second[...], FIRST).astype(jnp.bfloat16)


def two_products(first, by_first, second, by_second):
    length, width = first.shape
    inner = by_first.shape[1]
    tile = 512
    columns = pl.BlockSpec((length, tile), lambda c: (0, c))
    return pl.pallas_call(
        two_products_kernel,
        grid=(width // tile,),
        in_specs=[columns, columns, whole_spec(by_first), whole_spec(by_second)],
        out_specs=pl.BlockSpec((2, tile, inner), lambda c: (0, c, 0)),
        out_shape=jax.ShapeDtypeStruct((2, width, inner), jnp.bfloat16),
        compiler_params=vmem(),
    )(first, second, by_first, by_second)


def shards(
    tokens,
    prenorm,
    gating,
    values,
    control,
    timestep,
    kernel,
    offset,
    filters,
    baseline,
    timing,
    damping,
    direct,
    postnorm,
    readout,
    doc_starts,
    cotangent,
):
    length, share = tokens.shape
    inner = kernel.shape[1]
    heads = timing.shape[0]
    ranks = lax.axis_size("head")
    features = share * ranks
    channels = inner * ranks
    blocks = length // SPAN
    half = length // 2
    f32, bf16 = jnp.float32, jnp.bfloat16

    starts = doc_starts.reshape(blocks, SPAN).astype(bf16)
    place = jnp.arange(SPAN)
    counted = jnp.dot(starts, (place[:, None] <= place[None, :]).astype(bf16), preferred_element_type=f32)
    seg_row, seg_col = counted.reshape(blocks, 1, SPAN), counted.reshape(length, 1)
    expand = (jnp.arange(heads)[:, None] == jnp.arange(inner)[None, :] // HDIM).astype(bf16)
    skip = jnp.repeat(direct, HDIM)[None]
    offset_row, baseline_row, postnorm_row = offset[None], baseline[None], postnorm[None]
    timing_row, damping_row = timing[None], damping[None]

    gains = Chain(all_chain(prenorm, "head"))
    tokens_in = Chain(gather_chain(tokens, "head"))
    weights_back = phase([tokens_in, gains], lambda *a: tuple(w.T for w in a), gating, values, control, timestep, readout)
    readout_t = weights_back[4]
    finish(tokens_in, gains)
    cot_ready, found, gain_blocks = lax.optimization_barrier((cotangent, tokens_in.result, gains.result))
    upstream = lax.all_gather(cot_ready, "head", axis=1, tiled=True)
    gain = gain_blocks.reshape(1, features).astype(f32)

    def project(*found):
        gathered = place_columns(found, "head")
        wide = gathered.astype(f32)
        scale = lax.rsqrt(jnp.mean(wide * wide, axis=1, keepdims=True) + epsilon)
        normed = (wide * scale * gain).astype(bf16)
        projected = jnp.dot(normed, values, preferred_element_type=f32)
        shared = jnp.dot(normed, control, preferred_element_type=f32)
        timestep_in = jnp.dot(normed, timestep, preferred_element_type=f32)
        return gathered, scale, normed, projected, shared, timestep_in

    gathered, scale, normed, projected, shared, timestep_in = phase([], project, *found)
    edges = Chain(shift_chain(
        jnp.concatenate([projected[length - 8 :], shared[length - 8 :], gathered[length - 8 :].astype(f32)], axis=1), "seq", 1
    ))
    finish(edges)
    edge_v, edge_s = edges.result[:, :inner], edges.result[:, inner : inner + 2 * STATE]
    before = edges.result[:, inner + 2 * STATE :]
    before = jnp.pad(before, ((0, 8), (0, 0)))
    before_scale = lax.rsqrt(jnp.mean(before * before, axis=1, keepdims=True) + epsilon)
    normed_more = jnp.concatenate([normed, (before * before_scale * gain).astype(bf16)], axis=0)
    params = (kernel, offset_row, filters, baseline_row, timing_row, damping_row, skip, expand)
    local, readers, run, entry, states, final = phase(
        [], lambda *a: forward_scan(*a, *params), projected, shared, timestep_in, seg_col, seg_row, edge_v, edge_s
    )
    prefix = Chain(state_chain(final, False))
    phase([prefix])
    gate_in = phase([prefix], lambda n: jnp.dot(n, gating, preferred_element_type=f32), normed)
    finish(prefix)
    incoming = prefix.result
    full, squares = join_incoming(local, readers, run, gate_in, incoming, expand)
    squared = Chain(sum_chain(squares.reshape(length), "head"))
    finish(squared)
    inverse = lax.rsqrt(squared.result / channels + epsilon)[:, None]
    norm_cot, normalized, inner_sum, postnorm_sum = norm_cotangent(
        upstream, readout, full, gate_in, inverse, postnorm_row
    )
    means = Chain(sum_chain(inner_sum.reshape(length), "head"))
    partial_rows = phase(
        [means], lambda n: jnp.dot(n, readout_t, preferred_element_type=f32).astype(bf16), normalized
    )
    branch = lax.psum_scatter(partial_rows, "head", scatter_dimension=1, tiled=True)
    mean = means.result[:, None] / channels
    full_cot, gate_low, pending = gate_cotangent(
        norm_cot, full, gate_in, inverse, mean, postnorm_row, run, readers, expand, final
    )
    suffix = Chain(state_chain(pending, True))
    phase([suffix])
    weights_local = phase(
        [suffix],
        two_products,
        upstream, normalized, normed, gate_low,
    )
    weights_sum = lax.psum_scatter(weights_local, "seq", scatter_dimension=1, tiled=True)
    finish(suffix)
    leaving = suffix.result

    def backward(base, size, leaving, after_v, after_s, sums):
        return backward_scan(
            projected, shared, timestep_in, seg_col, seg_row, full_cot, states, entry,
            edge_v, edge_s, *params, incoming, leaving, after_v, after_s, sums, base, size,
        )

    def normed_back(base, *lows):
        return normed_cotangent(gate_low, *lows, *weights_back[:4], gathered, scale, gain, base, ranks)

    zeros_v, zeros_s = jnp.zeros((8, inner), f32), jnp.zeros((8, 2 * STATE), f32)
    taps = kernel.shape[0]
    sums = jnp.zeros((2 * taps + 5, inner), f32)
    late = backward(blocks // 2, blocks // 2, leaving, zeros_v, zeros_s, sums)
    normed_late = normed_back(half, *late[:3])
    total_late = Chain(scatter_chain([normed_late[0]], "head"))
    early = phase(
        [total_late], lambda *a: backward(0, blocks // 2, *a), late[6], late[4], late[5], late[3]
    )
    branch, early = lax.optimization_barrier((branch, early))

    def share_before(head, taps_of):
        following = jnp.concatenate([jnp.zeros_like(head), head], axis=0)
        return sum(taps_of[tap][None] * following[taps - 1 - tap : taps + 7 - tap] for tap in range(taps))

    more_v, more_s = share_before(early[4], kernel), share_before(early[5], filters)

    more_v, more_s = [jnp.pad(more.astype(bf16), ((0, 8), (0, 0))) for more in (more_v, more_s)]
    more_dt = jnp.zeros((16, heads), bf16)

    def last_products(low):
        normed_early = early_cotangent(
            gate_low, low, more_v, early[1], more_s, early[2], *weights_back[:4], gathered, before, scale, before_scale, gain, ranks
        )
        shared_low = jnp.concatenate([early[1], late[1], more_s], axis=0)
        low = jnp.concatenate([low, late[0], more_v], axis=0)
        small = jnp.concatenate([early[2], late[2], more_dt], axis=0)
        low = jnp.concatenate([low, jnp.pad(small, ((0, 0), (0, 128 - heads)))], axis=1)
        return (
            normed_early,
            lax.dot_general(normed_more, shared_low, FIRST, preferred_element_type=f32),
            lax.dot_general(normed_more, low, FIRST, preferred_element_type=f32).astype(bf16),
        )

    normed_early, control_local, values_local = phase([total_late], last_products, early[0])
    values_sum = lax.psum_scatter(values_local, "seq", scatter_dimension=0, tiled=True)
    finish(total_late)
    total_early = Chain(scatter_chain([normed_early[0]], "head", 2))
    prenorm_sum = (normed_early[2] + normed_late[2]).sum(0).reshape(-1, inner)
    flat = jnp.concatenate([early[3], postnorm_sum.sum(0)[None], prenorm_sum], axis=0)
    flat_rows = flat.shape[0]
    flat = jnp.pad(flat, ((0, -flat_rows % 8), (0, 0))).reshape(-1, 2 * STATE)
    row_sum = jnp.concatenate(
        [normed_early[1][:half], normed_late[1], normed_early[1][half : half + 8]], axis=0
    ).reshape(length + 8)
    holder = []
    shared_sum = Chain(shared_chain(control_local, flat, row_sum, holder))

    phase([shared_sum, total_early])
    mixed = phase(
        [shared_sum, total_early], lambda t, s: (t.astype(f32) + s.astype(f32)).astype(bf16), tokens, branch
    )
    phase([shared_sum])
    weights_sum = phase([shared_sum, total_early], lambda a: a, weights_sum)
    finish(total_early, total_late)
    copies, row_sum = holder
    scattered = total_early.result
    extra = jnp.concatenate([scattered[half : half + 8], jnp.broadcast_to(row_sum[length:, None], (8, share))], axis=0)
    from_next = Chain(shift_chain(extra, "seq", -1))

    def closing(row_sum, early_total, late_total, copies):
        own_total = jnp.concatenate([early_total[:half], late_total], axis=0)
        own_units = tokens.astype(f32) * scale
        tokens_gradient = cotangent.astype(f32) + scale * (
            own_total * prenorm.astype(f32) - own_units * (row_sum[:length, None] / features)
        )
        by_head = copies.reshape(ranks, -1, inner)[:, :flat_rows].transpose(1, 0, 2)
        rows = by_head.reshape(flat_rows, channels)
        alike = by_head[:, 0]
        for rank in range(1, ranks):
            alike = alike + by_head[:, rank]
        return (
            tokens_gradient,
            rows[:taps],
            rows[taps],
            alike[taps + 2 : 2 * taps + 2, : 2 * STATE],
            alike[2 * taps + 2, : 2 * STATE],
            by_head[2 * taps + 3, :, :heads].reshape(-1),
            by_head[2 * taps + 4, :, :heads].reshape(-1),
            rows[taps + 1].reshape(ranks * heads, HDIM).sum(1),
            rows[2 * taps + 5],
            alike[2 * taps + 6 :].reshape(-1),
        )

    (
        tokens_gradient, kernel_gradient, offset_gradient, filters_gradient, baseline_gradient, timing_gradient,
        damping_gradient, direct_gradient, postnorm_gradient, prenorm_gradient,
    ) = phase([shared_sum, from_next], closing, row_sum, scattered, total_late.result, copies)
    finish(shared_sum, from_next)
    more_rows, more_sums = from_next.result[:8], from_next.result[8:, :1] / features
    last = scale[length - 8 :] * (
        more_rows * prenorm.astype(f32) - tokens[length - 8 :].astype(f32) * scale[length - 8 :] * more_sums
    )
    tokens_gradient = tokens_gradient.at[length - 8 :].add(last)
    return (
        mixed,
        tokens_gradient,
        prenorm_gradient,
        weights_sum[1].astype(f32),
        values_sum[:, :inner].astype(f32),
        shared_sum.result,
        values_sum[:, inner : inner + heads].astype(f32),
        kernel_gradient,
        offset_gradient,
        filters_gradient,
        baseline_gradient,
        timing_gradient,
        damping_gradient,
        direct_gradient,
        postnorm_gradient,
        weights_sum[0].astype(f32),
    )


def solution(mesh):
    return jax.shard_map(
        shards,
        mesh=mesh,
        in_specs=(
            P("seq", "head"),
            P("head"),
            P(None, "head"),
            P(None, "head"),
            P(),
            P(None, "head"),
            P(None, "head"),
            P("head"),
            P(),
            P(),
            P("head"),
            P("head"),
            P("head"),
            P("head"),
            P(None, "head"),
            P("seq"),
            P("seq", "head"),
        ),
        out_specs=(
            P("seq", "head"),
            P("seq", "head"),
            P(),
            P("seq", "head"),
            P("seq", "head"),
            P(),
            P("seq", "head"),
            P(),
            P(),
            P(),
            P(),
            P(),
            P(),
            P(),
            P(),
            P("seq", "head"),
        ),
        check_vma=False,
    )
```
